128 devices in a mesh: section: 2 (over core), shard: 8 (over z_lo, x), replica: 8 (over y, z_hi).
Axes of the slice: x: 4, y: 4, z: 4 (z_hi: 2, z_lo: 2; z = z_hi * 2 + z_lo), core: 2. Of those that a mesh axis runs over, the one named last changes fastest.
Arguments:
- inputs: bfloat16 [2, 8, 1024, 1088], P(None, 'replica', 'shard'), may hold values from -6 to 6
- cotangent: bfloat16 [2, 8, 1024, 1088], P(None, 'replica', 'shard'), may hold values from -6 to 6
- w_qkv: bfloat16 [2, 1088, 3264], P('section', 'shard'), may hold values from -0.1875 to 0.1875
- qv_bias: bfloat16 [2, 2176], P('section', 'shard'), may hold values from -3 to 3
- w_out: bfloat16 [2, 1088, 1088], P('section', 'shard'), may hold values from -2 to 2
- out_bias: bfloat16 [2, 1088], P('section', 'shard'), may hold values from -3 to 3
- gain_one: bfloat16 [2, 1088], P('section', 'shard'), may hold values from 0.5 to 1.5
- bias_one: bfloat16 [2, 1088], P('section', 'shard'), may hold values from -3 to 3
- gain_two: bfloat16 [2, 1088], P('section', 'shard'), may hold values from 0.5 to 1.5
- bias_two: bfloat16 [2, 1088], P('section', 'shard'), may hold values from -3 to 3
- w_up: bfloat16 [2, 1088, 4352], P('section', 'shard'), may hold values from -0.1875 to 0.1875
- up_bias: bfloat16 [2, 4352], P('section', 'shard'), may hold values from -3 to 3
- w_down: bfloat16 [2, 4352, 1088], P('section', 'shard'), may hold values from -0.09375 to 0.09375
- down_bias: bfloat16 [2, 1088], P('section', 'shard'), may hold values from -3 to 3
Outputs:
- section_out: float32 [2, 2, 8, 1024, 1088], P('section', None, 'replica', 'shard')
- input_grad: float32 [2, 2, 8, 1024, 1088], P('section', None, 'replica', 'shard')
- grad_w_qkv: float32 [2, 1088, 3264], P('section', 'shard')
- grad_qv_bias: float32 [2, 2176], P('section', 'shard')
- grad_w_out: float32 [2, 1088, 1088], P('section', 'shard')
- grad_out_bias: float32 [2, 1088], P('section', 'shard')
- grad_gain_one: float32 [2, 1088], P('section', 'shard')
- grad_bias_one: float32 [2, 1088], P('section', 'shard')
- grad_gain_two: float32 [2, 1088], P('section', 'shard')
- grad_bias_two: float32 [2, 1088], P('section', 'shard')
- grad_w_up: float32 [2, 1088, 4352], P('section', 'shard')
- grad_up_bias: float32 [2, 4352], P('section', 'shard')
- grad_w_down: float32 [2, 4352, 1088], P('section', 'shard')
- grad_down_bias: float32 [2, 1088], P('section', 'shard')
The draws below stay inside these ranges and needn't reach their ends.
All inputs are finite; a program needn't handle non-finite values.
Results may differ from the reference program's by a relative error of at most 0.02.
Values may be sent and summed in bfloat16 or wider, within the bound.
A program may use at most 256 MiB of HBM per device.

```python
import jax
import jax.numpy as jnp
from jax import lax

D = 1088
HEADS = 17
HEAD_DIM = 64
FF = 4352
SEQLEN = 1024
MICRO = 2
SEQS = 8
N_SECTION = 2


def block_scale(rng, dims, shards, least, largest):
    gain, own = 1.0, jax.random.fold_in(rng, 6)
    for dim, shards_of in shards:
        steps = jnp.exp(jax.random.uniform(jax.random.fold_in(own, dim), (shards_of,), jnp.float32, least / len(shards), largest / len(shards)))
        gain = gain * jnp.repeat(steps, dims[dim] // shards_of).reshape([-1 if axis == dim else 1 for axis in range(len(dims))])
    return gain


def noise(key, shape, width, reach, cuts=(), dtype=jnp.bfloat16):
    array = width * jax.random.normal(key, shape, jnp.float32)
    if cuts:
        array = array * block_scale(key, shape, cuts, -0.22, 0.18)
    return jnp.clip(array, -reach, reach).astype(dtype)


def setup_inputs(seed: int = 0) -> dict:
    streams_of = jax.random.split(jax.random.key(seed), 15)
    inputs = noise(streams_of[0], (MICRO, SEQS, SEQLEN, D), 1.0, 6.0, ((1, 8), (2, 8)))
    cotangent = noise(streams_of[1], (MICRO, SEQS, SEQLEN, D), 1.0, 6.0, ((1, 8), (2, 8)))
    w_qkv = noise(streams_of[2], (N_SECTION, D, 3 * D), D ** -0.5, 0.1875, ((0, 2), (1, 8)))
    qv_bias = noise(streams_of[3], (N_SECTION, 2 * D), 0.5, 3.0, ((0, 2), (1, 8)))
    w_out = noise(streams_of[4], (N_SECTION, D, D), (max(D // 128, 2)) ** -0.5, 2.0, ((0, 2), (1, 8)))
    out_bias = noise(streams_of[5], (N_SECTION, D), 0.5, 3.0, ((0, 2), (1, 8)))
    gain_one = jnp.clip(0.5 + 1.0 * jax.random.uniform(streams_of[6], (N_SECTION, D), jnp.float32) ** block_scale(streams_of[6], (N_SECTION, D), ((0, 2), (1, 8)), -0.2, 0.2), 0.5, 1.5).astype(jnp.bfloat16)
    bias_one = noise(streams_of[7], (N_SECTION, D), 0.5, 3.0, ((0, 2), (1, 8)))
    gain_two = jnp.clip(0.5 + 1.0 * jax.random.uniform(streams_of[8], (N_SECTION, D), jnp.float32) ** block_scale(streams_of[8], (N_SECTION, D), ((0, 2), (1, 8)), -0.2, 0.2), 0.5, 1.5).astype(jnp.bfloat16)
    bias_two = noise(streams_of[9], (N_SECTION, D), 0.5, 3.0, ((0, 2), (1, 8)))
    w_up = noise(streams_of[10], (N_SECTION, D, FF), D ** -0.5, 0.1875, ((0, 2), (1, 8)))
    up_bias = noise(streams_of[11], (N_SECTION, FF), 0.5, 3.0, ((0, 2), (1, 8)))
    w_down = noise(streams_of[12], (N_SECTION, FF, D), FF ** -0.5, 0.09375, ((0, 2), (1, 8)))
    down_bias = noise(streams_of[13], (N_SECTION, D), 0.5, 3.0, ((0, 2), (1, 8)))
    return dict(inputs=inputs, cotangent=cotangent, w_qkv=w_qkv, qv_bias=qv_bias, w_out=w_out, out_bias=out_bias, gain_one=gain_one, bias_one=bias_one, gain_two=gain_two, bias_two=bias_two, w_up=w_up, up_bias=up_bias, w_down=w_down, down_bias=down_bias)


@jax.custom_vjp
def low(v):
    return lax.optimization_barrier(v.astype(jnp.bfloat16)).astype(jnp.float32)

@jax.custom_vjp
def low_back(v):
    return v

def low_keep(v):
    return (low(v), None)

def low_pass(kept, grad):
    return (grad,)

def back_keep(v):
    return (v, None)

def back_low(kept, grad):
    return (low(grad),)
low.defvjp(low_keep, low_pass)
low_back.defvjp(back_keep, back_low)
EPSILON = 1e-05
GELU_C = 0.7978845608028654
NEG_FILL = -1e+30

def matmul(left_side, right_side):
    return jnp.dot(left_side, right_side, precision=lax.Precision.HIGHEST)

def layer_norm(hidden, gain_vec, offset):
    center = hidden - lax.optimization_barrier(jnp.mean(hidden, axis=-1, keepdims=True))
    spread = lax.optimization_barrier(jnp.mean(center * center, axis=-1, keepdims=True))
    return center * lax.rsqrt(spread + EPSILON) * gain_vec + offset

def gelu_tanh(values):
    return 0.5 * values * (1.0 + jnp.tanh(GELU_C * (values + 0.044715 * values * values * values)))

def attend_one(operand):
    query_rows, key_rows, value_rows = operand
    raw_scores = jnp.einsum('qhe,khe->hqk', query_rows, key_rows, precision=lax.Precision.HIGHEST)
    scores = low_back(raw_scores * HEAD_DIM ** (-0.5))
    query_pos = lax.broadcasted_iota(jnp.int32, (1, SEQLEN, SEQLEN), 1)
    key_pos = lax.broadcasted_iota(jnp.int32, (1, SEQLEN, SEQLEN), 2)
    masked = jnp.where(key_pos <= query_pos, scores, NEG_FILL)
    row_max = lax.optimization_barrier(jnp.max(masked, axis=-1, keepdims=True))
    shifted = jnp.exp(masked - row_max)
    softmax_rows = low(shifted / lax.optimization_barrier(jnp.sum(shifted, axis=-1, keepdims=True)))
    return jnp.einsum('hqk,khe->qhe', softmax_rows, value_rows, precision=lax.Precision.HIGHEST)

def layer(hidden, params):
    w_qkv, qv_bias, w_out, out_bias, gain_one, bias_one, gain_two, bias_two, w_up, up_bias, w_down, down_bias = params
    seq_count = hidden.shape[0]
    flat_rows = hidden.reshape(seq_count * SEQLEN, D)
    normed = low(layer_norm(flat_rows, gain_one, bias_one))
    bias_full = jnp.concatenate([qv_bias[:D], jnp.zeros_like(qv_bias[:D]), qv_bias[D:]])
    projected = low_back(low(matmul(normed, w_qkv) + bias_full))
    split_heads = projected.reshape(seq_count, SEQLEN, 3, HEADS, HEAD_DIM)
    mixed_heads = lax.map(jax.checkpoint(attend_one), (split_heads[:, :, 0], split_heads[:, :, 1], split_heads[:, :, 2]))
    attended = low_back(low(mixed_heads.reshape(seq_count * SEQLEN, D)))
    middle = flat_rows + low_back(matmul(attended, w_out) + out_bias)
    second = low(layer_norm(middle, gain_two, bias_two))
    upper_pre = low_back(matmul(second, w_up) + up_bias)
    activated = low(gelu_tanh(upper_pre))
    result = middle + low_back(matmul(activated, w_down) + down_bias)
    return result.reshape(seq_count, SEQLEN, D)

def forward(start_rows, extra_zero, first_params, second_params):
    out_first = layer(start_rows, first_params)
    passed = low_back(low(out_first)) + extra_zero
    out_second = layer(passed, second_params)
    return (out_first, out_second)

def reference(inputs, cotangent, w_qkv, qv_bias, w_out, out_bias, gain_one, bias_one, gain_two, bias_two, w_up, up_bias, w_down, down_bias):
    seq_count = MICRO * SEQS
    start_rows = inputs.astype(jnp.float32).reshape(seq_count, SEQLEN, D)
    stacks = (w_qkv, qv_bias, w_out, out_bias, gain_one, bias_one, gain_two, bias_two, w_up, up_bias, w_down, down_bias)
    first_params = tuple((stacked[0].astype(jnp.float32) for stacked in stacks))
    second_params = tuple((stacked[1].astype(jnp.float32) for stacked in stacks))
    extra_zero = jnp.zeros_like(start_rows)
    outputs_pair, pullback = jax.vjp(forward, start_rows, extra_zero, first_params, second_params)
    seed_grad = cotangent.astype(jnp.float32).reshape(seq_count, SEQLEN, D)
    grad_start, grad_extra, grad_first, grad_second = pullback((jnp.zeros_like(outputs_pair[0]), seed_grad))
    full_shape = (MICRO, SEQS, SEQLEN, D)
    section_out = jnp.stack([outputs_pair[0].reshape(full_shape), outputs_pair[1].reshape(full_shape)])
    input_grad = jnp.stack([grad_start.reshape(full_shape), grad_extra.reshape(full_shape)])
    weight_grads = tuple((jnp.stack([grad_first[slot_index], grad_second[slot_index]]) for slot_index in range(12)))
    return (section_out, input_grad, weight_grads[0], weight_grads[1], weight_grads[2], weight_grads[3], weight_grads[4], weight_grads[5], weight_grads[6], weight_grads[7], weight_grads[8], weight_grads[9], weight_grads[10], weight_grads[11])
```

```python
import functools

import jax
import jax.numpy as jnp
from jax import lax
from jax.experimental import pallas as pl
from jax.experimental.pallas import tpu as pltpu
from jax.sharding import PartitionSpec as P

D = 1088
FF = 4352
HEAD_DIM = 64
EPSILON = 1e-05
GELU_C = 0.7978845608028654
NEG_FILL = -1e30
BF = jnp.bfloat16
F32 = jnp.float32
MESH = pl.DeviceIdType.MESH
VMEM = pl.BlockSpec(memory_space=pltpu.VMEM)
LIMIT = 56 * 1024 * 1024


def place():
    c = lax.axis_index("section")
    j = lax.axis_index("shard")
    return c, j // 4, j % 4


def at(c, z, x):
    return {"section": c, "shard": z * 4 + x}


def greet(devices):
    barrier = pltpu.get_barrier_semaphore()
    for device in devices:
        pl.semaphore_signal(barrier, inc=1, device_id=device, device_id_type=MESH)
    pl.semaphore_wait(barrier, len(devices))


def sender(send_sems, recv_sems):
    def make(src, dst, index, device):
        copy = pltpu.make_async_remote_copy(
            src_ref=src,
            dst_ref=dst,
            send_sem=send_sems.at[index],
            recv_sem=recv_sems.at[index],
            device_id=device,
            device_id_type=MESH,
        )
        copy.start()
        return copy

    return make


def gather_kernel(half, own, out, send_sems, recv_sems, local_sem):
    c, z, x = place()
    ahead, behind, far = (x + 1) % 4, (x + 3) % 4, (x + 2) % 4
    partner, up, down = at(1 - c, z, x), at(c, z, ahead), at(c, z, behind)
    rows = own.shape[0]
    first, second = pl.ds(0, half), pl.ds(half, rows - half)
    me = c * 4 + x
    local = pltpu.make_async_copy(own, out.at[me], local_sem)
    local.start()
    greet((partner, up, down))
    send = sender(send_sems, recv_sems)
    to_up = send(own, out.at[me], 0, up)
    to_down = send(own, out.at[me], 1, down)
    to_partner = send(own, out.at[me], 2, partner)
    from_down, from_up, from_far = c * 4 + behind, c * 4 + ahead, c * 4 + far
    to_up.wait_recv()
    pass_up = send(out.at[from_down, first], out.at[from_down, first], 3, up)
    share_down = send(out.at[from_down], out.at[from_down], 4, partner)
    to_down.wait_recv()
    pass_down = send(out.at[from_up, second], out.at[from_up, second], 5, down)
    share_up = send(out.at[from_up], out.at[from_up], 6, partner)
    pass_up.wait_recv()
    share_first = send(out.at[from_far, first], out.at[from_far, first], 7, partner)
    pass_down.wait_recv()
    share_second = send(out.at[from_far, second], out.at[from_far, second], 8, partner)
    for copy in (to_partner, share_down, share_up, share_first, share_second):
        copy.wait_recv()
    for copy in (
        to_up,
        to_down,
        to_partner,
        pass_up,
        share_down,
        pass_down,
        share_up,
        share_first,
        share_second,
    ):
        copy.wait_send()
    local.wait()


def team_gather(own):
    rows, columns = own.shape
    return pl.pallas_call(
        functools.partial(gather_kernel, rows // 2),
        out_shape=jax.ShapeDtypeStruct((8, rows, columns), BF),
        in_specs=[VMEM],
        out_specs=VMEM,
        scratch_shapes=[
            pltpu.SemaphoreType.DMA((9,)),
            pltpu.SemaphoreType.DMA((9,)),
            pltpu.SemaphoreType.DMA,
        ],
        compiler_params=pltpu.CompilerParams(
            collective_id=0, has_side_effects=True, vmem_limit_bytes=LIMIT
        ),
    )(own)


def scatter_kernel(
    half,
    parts,
    out,
    from_partner,
    far_sum,
    up_sum,
    down_sum,
    far_first,
    far_second,
    got_down,
    got_up,
    send_sems,
    recv_sems,
):
    c, z, x = place()
    ahead, behind, far = (x + 1) % 4, (x + 3) % 4, (x + 2) % 4
    partner, up, down = at(1 - c, z, x), at(c, z, ahead), at(c, z, behind)
    rows = parts.shape[1]
    first, second = pl.ds(0, half), pl.ds(half, rows - half)
    greet((partner, up, down))
    send = sender(send_sems, recv_sems)
    other = (1 - c) * 4
    mine = c * 4
    swap_far = send(parts.at[other + far], from_partner.at[far], 0, partner)
    swap_up = send(parts.at[other + ahead], from_partner.at[ahead], 1, partner)
    swap_down = send(parts.at[other + behind], from_partner.at[behind], 2, partner)
    swap_own = send(parts.at[other + x], from_partner.at[x], 3, partner)

    def both(place_x, part):
        return parts[mine + place_x, part, :].astype(F32) + from_partner[
            place_x, part, :
        ].astype(F32)

    swap_far.wait_recv()
    far_sum[first, :] = both(far, first).astype(BF)
    far_up = send(far_sum.at[first], far_first, 4, up)
    far_sum[second, :] = both(far, second).astype(BF)
    far_down = send(far_sum.at[second], far_second, 5, down)
    swap_up.wait_recv()
    up_sum[second, :] = both(ahead, second).astype(BF)
    up_second = send(up_sum.at[second], got_down.at[second], 6, up)
    swap_down.wait_recv()
    down_sum[first, :] = both(behind, first).astype(BF)
    down_first = send(down_sum.at[first], got_up.at[first], 7, down)
    far_up.wait_recv()
    up_sum[first, :] = (both(ahead, first) + far_first[...].astype(F32)).astype(BF)
    up_first = send(up_sum.at[first], got_down.at[first], 8, up)
    far_down.wait_recv()
    down_sum[second, :] = (both(behind, second) + far_second[...].astype(F32)).astype(BF)
    down_second = send(down_sum.at[second], got_up.at[second], 9, down)
    swap_own.wait_recv()
    out[...] = parts[mine + x].astype(F32) + from_partner[x].astype(F32)
    up_second.wait_recv()
    up_first.wait_recv()
    down_first.wait_recv()
    down_second.wait_recv()
    out[...] = out[...] + got_down[...].astype(F32) + got_up[...].astype(F32)
    for copy in (
        swap_far,
        swap_up,
        swap_down,
        swap_own,
        far_up,
        far_down,
        up_second,
        down_first,
        up_first,
        down_second,
    ):
        copy.wait_send()


def team_scatter(parts, collective_id):
    count, rows, columns = parts.shape
    half = rows // 32 * 16
    block = pltpu.VMEM((rows, columns), BF)
    return pl.pallas_call(
        functools.partial(scatter_kernel, half),
        out_shape=jax.ShapeDtypeStruct((rows, columns), F32),
        in_specs=[VMEM],
        out_specs=VMEM,
        scratch_shapes=[
            pltpu.VMEM((4, rows, columns), BF),
            block,
            block,
            block,
            pltpu.VMEM((half, columns), BF),
            pltpu.VMEM((rows - half, columns), BF),
            block,
            block,
            pltpu.SemaphoreType.DMA((10,)),
            pltpu.SemaphoreType.DMA((10,)),
        ],
        compiler_params=pltpu.CompilerParams(
            collective_id=collective_id, has_side_effects=True, vmem_limit_bytes=LIMIT
        ),
    )(parts)


TEAM_STEPS = tuple((dc, dx) for dc in range(2) for dx in range(4) if dc or dx)


def heads_to_rows_kernel(heads, extra, out, send_sems, recv_sems, local_sems):
    c, z, x = place()
    me = c * 4 + x
    spots = [((c + dc) % 2, (x + dx) % 4) for dc, dx in TEAM_STEPS]
    own_columns = pl.ds(pl.multiple_of(me * 128, 128), 128)
    local = pltpu.make_async_copy(heads.at[me], out.at[:, own_columns], local_sems.at[0])
    local.start()
    last = pltpu.make_async_copy(extra, out.at[:, pl.ds(1024, 128)], local_sems.at[1])
    last.start()
    greet([at(tc, z, tx) for tc, tx in spots])
    send = sender(send_sems, recv_sems)
    copies = [
        send(heads.at[tc * 4 + tx], out.at[:, own_columns], index, at(tc, z, tx))
        for index, (tc, tx) in enumerate(spots)
    ]
    for copy in copies:
        copy.wait_recv()
    for copy in copies:
        copy.wait_send()
    local.wait()
    last.wait()


def heads_to_rows(heads, extra):
    return pl.pallas_call(
        heads_to_rows_kernel,
        out_shape=jax.ShapeDtypeStruct((128, 1152), BF),
        in_specs=[VMEM, VMEM],
        out_specs=VMEM,
        scratch_shapes=[
            pltpu.SemaphoreType.DMA((7,)),
            pltpu.SemaphoreType.DMA((7,)),
            pltpu.SemaphoreType.DMA((2,)),
        ],
        compiler_params=pltpu.CompilerParams(
            collective_id=1, has_side_effects=True, vmem_limit_bytes=LIMIT
        ),
    )(heads, extra)


def rows_to_heads_kernel(rows, out, send_sems, recv_sems, local_sem):
    c, z, x = place()
    me = c * 4 + x
    spots = [((c + dc) % 2, (x + dx) % 4) for dc, dx in TEAM_STEPS]

    def columns(q):
        return rows.at[:, pl.ds(pl.multiple_of(q * 128, 128), 128)]

    local = pltpu.make_async_copy(columns(me), out.at[me], local_sem)
    local.start()
    greet([at(tc, z, tx) for tc, tx in spots])
    send = sender(send_sems, recv_sems)
    copies = [
        send(columns(tc * 4 + tx), out.at[me], index, at(tc, z, tx))
        for index, (tc, tx) in enumerate(spots)
    ]
    for copy in copies:
        copy.wait_recv()
    for copy in copies:
        copy.wait_send()
    local.wait()


def rows_to_heads(rows):
    return pl.pallas_call(
        rows_to_heads_kernel,
        out_shape=jax.ShapeDtypeStruct((8, 128, 128), BF),
        in_specs=[VMEM],
        out_specs=VMEM,
        scratch_shapes=[
            pltpu.SemaphoreType.DMA((7,)),
            pltpu.SemaphoreType.DMA((7,)),
            pltpu.SemaphoreType.DMA,
        ],
        compiler_params=pltpu.CompilerParams(
            collective_id=2, has_side_effects=True, vmem_limit_bytes=LIMIT
        ),
    )(rows)


GROUP_STEPS = tuple(
    (dc, dz, dx) for dx in (2, 1, 3, 0) for dz in range(2) for dc in range(2) if dc or dz or dx
)


def weights_kernel(blocks, common, out, out_common, send_sems, recv_sems, local_sems):
    c, z, x = place()
    slot = (c, z * 4 + x)
    spots = [((c + dc) % 2, (z + dz) % 2, (x + dx) % 4) for dc, dz, dx in GROUP_STEPS]
    locals_ = [
        pltpu.make_async_copy(blocks.at[c * 4 + x], out.at[slot], local_sems.at[0]),
        pltpu.make_async_copy(common, out_common.at[slot], local_sems.at[1]),
    ]
    for copy in locals_:
        copy.start()
    greet([at(*spot) for spot in spots])
    send = sender(send_sems, recv_sems)
    copies = []
    for index, (tc, tz, tx) in enumerate(spots):
        device = at(tc, tz, tx)
        copies.append(send(blocks.at[tc * 4 + tx], out.at[slot], 2 * index, device))
        copies.append(send(common, out_common.at[slot], 2 * index + 1, device))
    for copy in copies:
        copy.wait_recv()
    for copy in copies:
        copy.wait_send()
    for copy in locals_:
        copy.wait()


def spread_weights(blocks, common):
    return pl.pallas_call(
        weights_kernel,
        out_shape=(
            jax.ShapeDtypeStruct((2,) + blocks.shape, BF),
            jax.ShapeDtypeStruct((2, 8) + common.shape, BF),
        ),
        in_specs=[VMEM, VMEM],
        out_specs=(VMEM, VMEM),
        scratch_shapes=[
            pltpu.SemaphoreType.DMA((30,)),
            pltpu.SemaphoreType.DMA((30,)),
            pltpu.SemaphoreType.DMA((2,)),
        ],
        compiler_params=pltpu.CompilerParams(
            collective_id=3, has_side_effects=True, vmem_limit_bytes=LIMIT
        ),
    )(blocks, common)


def grads_kernel(blocks, out, got, send_sems, recv_sems, local_sem):
    c, z, x = place()
    spots = [((c + dc) % 2, (z + dz) % 2, (x + dx) % 4) for dc, dz, dx in GROUP_STEPS]
    slot = (z, c * 4 + x)
    local = pltpu.make_async_copy(blocks.at[c, z * 4 + x], got.at[slot], local_sem)
    local.start()
    greet([at(*spot) for spot in spots])
    send = sender(send_sems, recv_sems)
    copies = [
        send(blocks.at[tc, tz * 4 + tx], got.at[slot], index, at(tc, tz, tx))
        for index, (tc, tz, tx) in enumerate(spots)
    ]
    for copy in copies:
        copy.wait_recv()
    local.wait()
    for q in range(8):
        out[q] = (got[0, q].astype(F32) + got[1, q].astype(F32)).astype(BF)
    for copy in copies:
        copy.wait_send()


def collect_grads(blocks):
    shape = blocks.shape[1:]
    return pl.pallas_call(
        grads_kernel,
        out_shape=jax.ShapeDtypeStruct(shape, BF),
        in_specs=[VMEM],
        out_specs=VMEM,
        scratch_shapes=[
            pltpu.VMEM((2,) + shape, BF),
            pltpu.SemaphoreType.DMA((15,)),
            pltpu.SemaphoreType.DMA((15,)),
            pltpu.SemaphoreType.DMA,
        ],
        compiler_params=pltpu.CompilerParams(
            collective_id=4, has_side_effects=True, vmem_limit_bytes=LIMIT
        ),
    )(blocks)


def dot_nt(left, right):
    return lax.dot_general(left, right, (((1,), (1,)), ((), ())), preferred_element_type=F32)


def dot_tn(left, right):
    return lax.dot_general(left, right, (((0,), (0,)), ((), ())), preferred_element_type=F32)


def dot(left, right):
    return jnp.dot(left, right, preferred_element_type=F32)


def lane_half(block, which):
    lane = lax.broadcasted_iota(jnp.int32, block.shape, 1)
    keep = lane < 64 if which == 0 else lane >= 64
    return jnp.where(keep, block, jnp.zeros_like(block))


def softmax_rows(scores, start):
    row = lax.broadcasted_iota(jnp.int32, scores.shape, 0) + start
    key = lax.broadcasted_iota(jnp.int32, scores.shape, 1)
    masked = jnp.where(key <= row, scores, NEG_FILL)
    shifted = jnp.exp(masked - jnp.max(masked, axis=1, keepdims=True))
    return shifted * (1.0 / jnp.sum(shifted, axis=1, keepdims=True))


STEP = 256


def attend_kernel(projected, last_query, attended, attended_last):
    c, z, x = place()
    for start in range(0, 1024, STEP):
        size = start + STEP
        query = projected[start:size, 0:128] * 0.125
        total = jnp.zeros((STEP, 128), F32)
        for head in range(2):
            keys = lane_half(projected[0:size, 128:256], head)
            values = lane_half(projected[0:size, 256:384], head)
            soft = softmax_rows(dot_nt(query, keys), start).astype(BF)
            total = total + dot(soft, values)
        attended[start:size, :] = total.astype(BF)
    both = projected[:, 384:512]
    soft = softmax_rows(dot_nt(last_query[...] * 0.125, both), (c * 4 + x) * 128).astype(BF)
    attended_last[...] = dot(soft, lane_half(both, 1)).astype(BF)


def attend(projected, last_query):
    return pl.pallas_call(
        attend_kernel,
        out_shape=(
            jax.ShapeDtypeStruct((1024, 128), BF),
            jax.ShapeDtypeStruct((128, 128), BF),
        ),
        in_specs=[VMEM, VMEM],
        out_specs=(VMEM, VMEM),
        compiler_params=pltpu.CompilerParams(vmem_limit_bytes=LIMIT),
    )(projected, last_query)


def attend_back_kernel(
    projected, last_query, grad, last_grad, out, out_last, key_total, value_total
):
    c, z, x = place()
    key_total[...] = jnp.zeros_like(key_total)
    value_total[...] = jnp.zeros_like(value_total)
    for start in range(0, 1024, STEP):
        size = start + STEP
        query = projected[start:size, 0:128] * 0.125
        grad_rows = grad[start:size, :]
        total = jnp.zeros((STEP, 128), F32)
        for head in range(2):
            keys = lane_half(projected[0:size, 128:256], head)
            values = lane_half(projected[0:size, 256:384], head)
            soft = softmax_rows(dot_nt(query, keys), start)
            grad_soft = dot_nt(grad_rows, values)
            inner = jnp.sum(soft * grad_soft, axis=1, keepdims=True)
            grad_scores = (soft * (grad_soft - inner)).astype(BF)
            total = total + dot(grad_scores, keys)
            key_total[0:size, :] += dot_tn(grad_scores, lane_half(query, head))
            value_total[0:size, :] += dot_tn(soft.astype(BF), lane_half(grad_rows, head))
        out[start:size, 0:128] = (total * 0.125).astype(BF)
    out[:, 128:256] = key_total[...].astype(BF)
    out[:, 256:384] = value_total[...].astype(BF)
    both = projected[:, 384:512]
    query = last_query[...] * 0.125
    soft = softmax_rows(dot_nt(query, both), (c * 4 + x) * 128)
    grad_soft = dot_nt(last_grad[...], both)
    inner = jnp.sum(soft * grad_soft, axis=1, keepdims=True)
    grad_scores = (soft * (grad_soft - inner)).astype(BF)
    out_last[...] = (dot(grad_scores, lane_half(both, 0)) * 0.125).astype(BF)
    out[:, 384:512] = (dot_tn(grad_scores, query) + dot_tn(soft.astype(BF), last_grad[...])).astype(
        BF
    )


def attend_back(projected, last_query, grad, last_grad):
    return pl.pallas_call(
        attend_back_kernel,
        out_shape=(
            jax.ShapeDtypeStruct((1024, 512), BF),
            jax.ShapeDtypeStruct((128, 128), BF),
        ),
        in_specs=[VMEM] * 4,
        out_specs=(VMEM, VMEM),
        scratch_shapes=[pltpu.VMEM((1024, 128), F32), pltpu.VMEM((1024, 128), F32)],
        compiler_params=pltpu.CompilerParams(vmem_limit_bytes=LIMIT),
    )(projected, last_query, grad, last_grad)


def norm_forward(hidden, gain, offset):
    center = hidden - jnp.mean(hidden, axis=-1, keepdims=True)
    inverse = lax.rsqrt(jnp.mean(center * center, axis=-1, keepdims=True) + EPSILON)
    unit = center * inverse
    return unit * gain + offset, unit, inverse


def norm_backward(grad_rows, unit, inverse, gain):
    grad_unit = grad_rows * gain
    grad_in = inverse * (
        grad_unit
        - jnp.mean(grad_unit, axis=-1, keepdims=True)
        - unit * jnp.mean(grad_unit * unit, axis=-1, keepdims=True)
    )
    return grad_in, jnp.sum(grad_rows * unit, axis=0), jnp.sum(grad_rows, axis=0)


def gelu_pair(values):
    tangent = jnp.tanh(GELU_C * (values + 0.044715 * values * values * values))
    output = 0.5 * values * (1.0 + tangent)
    slope = 0.5 * (1.0 + tangent) + 0.5 * values * (1.0 - tangent * tangent) * GELU_C * (
        1.0 + 3.0 * 0.044715 * values * values
    )
    return output, slope


def layer_forward(hidden, w):
    normed, unit_one, inverse_one = norm_forward(hidden, w["gain_one"], w["bias_one"])
    normed = normed.astype(BF)
    normed_all = team_gather(normed).reshape(1024, D)
    projected = (dot(normed_all, w["qkv"]) + w["qkv_bias"]).astype(BF)
    last_query = (dot(normed, w["last_query"]) + w["last_bias"]).astype(BF)
    heads, last = attend(projected, last_query)
    attended = heads_to_rows(heads.reshape(8, 128, 128), last)
    middle = hidden + dot(attended, w["out"]) + w["out_bias"]
    second, unit_two, inverse_two = norm_forward(middle, w["gain_two"], w["bias_two"])
    second_all = team_gather(second.astype(BF)).reshape(1024, D)
    upper = dot(second_all, w["up"]) + w["up_bias"]
    activated = gelu_pair(upper)[0].astype(BF)
    parts = dot(activated, w["down"]).astype(BF).reshape(8, 128, D)
    output = middle + team_scatter(parts, 5) + w["down_bias"]
    saved = dict(
        normed=normed,
        normed_all=normed_all,
        unit_one=unit_one,
        inverse_one=inverse_one,
        projected=projected,
        last_query=last_query,
        attended=attended,
        unit_two=unit_two,
        inverse_two=inverse_two,
        second_all=second_all,
        upper=upper,
        activated=activated,
    )
    return output, saved


def layer_backward(grad_out, w, kept, q):
    grad_low = grad_out.astype(BF)
    grad_low_all = team_gather(grad_low).reshape(1024, D)
    slope = gelu_pair(kept["upper"])[1]
    up_grad = (dot_nt(grad_low_all, w["down"]) * slope).astype(BF)
    parts = dot_nt(up_grad, w["up"]).astype(BF).reshape(8, 128, D)
    grad_second = team_scatter(parts, 5)
    grad_in, gain_two, bias_two = norm_backward(
        grad_second, kept["unit_two"], kept["inverse_two"], w["gain_two"]
    )
    grad_middle = grad_out + grad_in
    middle_low = grad_middle.astype(BF)
    attended_grad = dot_nt(middle_low, w["out"]).astype(BF)
    heads_grad = rows_to_heads(attended_grad).reshape(1024, 128)
    qkv_grad, last_grad = attend_back(
        kept["projected"], kept["last_query"], heads_grad, attended_grad[:, 1024:]
    )
    parts = dot_nt(qkv_grad, w["qkv"]).astype(BF).reshape(8, 128, D)
    grad_normed = team_scatter(parts, 5) + dot_nt(last_grad, w["last_query"])
    grad_in, gain_one, bias_one = norm_backward(
        grad_normed, kept["unit_one"], kept["inverse_one"], w["gain_one"]
    )
    grad_input = grad_middle + grad_in

    grad_qkv = dot_tn(kept["normed_all"], qkv_grad)
    grad_last_query = dot_tn(kept["normed"], last_grad)
    grad_up = dot_tn(kept["second_all"], up_grad)
    grad_down = dot_tn(kept["activated"], grad_low_all)
    grad_out_w = dot_tn(kept["attended"], middle_low)
    split = jnp.concatenate([grad_qkv[:, :384], grad_up], axis=1).astype(BF).reshape(8, 136, 928)
    out_rows = jnp.concatenate([grad_out_w[:1024], grad_out_w[1088:]], axis=0)
    shared = jnp.concatenate(
        [out_rows, grad_qkv[:, 384:512], grad_last_query[:, :64]], axis=1
    ).reshape(8, 136, 1280)

    qkv_sums = jnp.sum(qkv_grad, axis=0, dtype=F32)
    last_sums = jnp.sum(last_grad, axis=0, dtype=F32)
    zeros = jnp.zeros((1024,), F32)
    qv = jnp.concatenate(
        [
            lax.dynamic_update_slice(zeros, qkv_sums[:128], (q * 128,)),
            last_sums[:64],
            lax.dynamic_update_slice(zeros, qkv_sums[256:384], (q * 128,)),
            qkv_sums[448:512],
        ]
    )
    up_sums = lax.dynamic_update_slice(
        jnp.zeros((FF,), F32), jnp.sum(up_grad, axis=0, dtype=F32), (q * 544,)
    )
    vectors = jnp.concatenate(
        [
            qv.reshape(8, 272),
            jnp.sum(middle_low, axis=0, dtype=F32).reshape(8, 136),
            gain_one.reshape(8, 136),
            bias_one.reshape(8, 136),
            gain_two.reshape(8, 136),
            bias_two.reshape(8, 136),
            up_sums.reshape(8, 544),
            jnp.sum(grad_low, axis=0, dtype=F32).reshape(8, 136),
        ],
        axis=1,
    )
    vectors = jnp.pad(vectors, ((0, 0), (0, 8 * 1280 - 1632))).reshape(8, 8, 1280)
    shared = jnp.concatenate([shared, vectors], axis=1).astype(BF)
    shared = team_scatter(shared, 6).astype(BF)
    return grad_input, (split, grad_down.astype(BF), shared)


BOTH = ("section", "shard")


def pairs(route):
    out = []
    for c in range(2):
        for z in range(2):
            for x in range(4):
                tc, tz = route(c, z)
                out.append((c * 8 + z * 4 + x, tc * 8 + tz * 4 + x))
    return out


def local(
    inputs,
    cotangent,
    w_qkv,
    qv_bias,
    w_out,
    out_bias,
    gain_one,
    bias_one,
    gain_two,
    bias_two,
    w_up,
    up_bias,
    w_down,
    down_bias,
):
    c, z, x = place()
    q = c * 4 + x
    swap = pairs(lambda a, b: (b, a))
    cross = pairs(lambda a, b: (1 - b, a))
    cross_back = pairs(lambda a, b: (b, 1 - a))

    def mine(array):
        return lax.ppermute(jnp.where(c == z, array[z], array[1 - z])[0], BOTH, swap)

    def by_z(own, other):
        return jnp.where(z == 0, jnp.stack([own, other]), jnp.stack([other, own]))

    small = jnp.concatenate(
        [
            qv_bias[0],
            out_bias[0],
            gain_one[0],
            bias_one[0],
            gain_two[0],
            bias_two[0],
            up_bias[0],
            down_bias[0],
        ]
    )
    own_qkv = w_qkv[0]
    last_cols = [own_qkv[:, part * D + 1024 : (part + 1) * D] for part in range(3)]
    common = jnp.concatenate(
        [
            jnp.concatenate(
                [last_cols[1], last_cols[2], last_cols[0], jnp.zeros((136, 64), BF)], axis=1
            ),
            jnp.pad(small, (0, 2048 - 1632)).reshape(8, 256),
        ]
    )
    blocks = jnp.concatenate(
        [own_qkv[:, part * D : part * D + 1024].reshape(136, 8, 128) for part in range(3)]
        + [w_up[0].reshape(136, 8, 544)],
        axis=2,
    ).transpose(1, 0, 2)
    all_blocks, all_common = spread_weights(blocks, common)
    all_out = lax.all_gather(w_out[0], BOTH, axis=0, tiled=True).reshape(2, D, D)
    down_own = lax.ppermute(w_down[0], BOTH, swap)
    down_other = lax.ppermute(w_down[0], BOTH, cross_back)
    all_down = by_z(down_own, down_other)

    def layer_weights(layer):
        cut = all_blocks[layer].reshape(D, 928)
        shared = all_common[layer, :, :136].reshape(D, 256)
        vec = all_common[layer, :, 136:].reshape(8, 2048)[:, :1632].astype(F32)

        def piece(start, size):
            return vec[:, start : start + size].reshape(-1)

        qv = piece(0, 272)
        none = jnp.zeros((128,), F32)
        qkv_bias = jnp.concatenate(
            [
                lax.dynamic_slice(qv, (q * 128,), (128,)),
                none,
                lax.dynamic_slice(qv, (D + q * 128,), (128,)),
                none[:64],
                qv[2 * D - 64 :],
            ]
        )
        out = all_out[layer]
        return dict(
            qkv=jnp.concatenate([cut[:, :384], shared[:, :128]], axis=1),
            last_query=shared[:, 128:],
            qkv_bias=qkv_bias,
            last_bias=jnp.concatenate([qv[1024:D], none[:64]]),
            out=jnp.concatenate([out[:1024], jnp.zeros((64, D), BF), out[1024:]]),
            out_bias=piece(272, 136),
            gain_one=piece(408, 136),
            bias_one=piece(544, 136),
            gain_two=piece(680, 136),
            bias_two=piece(816, 136),
            up=cut[:, 384:],
            up_bias=lax.dynamic_slice(piece(952, 544), (q * 544,), (544,)),
            down=all_down[layer],
            down_bias=piece(1496, 136),
        )

    weights = [layer_weights(0), layer_weights(1)]
    hidden = mine(inputs).astype(F32)
    top_grad = mine(cotangent).astype(F32)
    out_first, kept_first = layer_forward(hidden, weights[0])
    out_second, kept_second = layer_forward(out_first.astype(BF).astype(F32), weights[1])
    grad_second, parts_second = layer_backward(top_grad, weights[1], kept_second, q)
    grad_first, parts_first = layer_backward(
        grad_second.astype(BF).astype(F32), weights[0], kept_first, q
    )

    def home(first, second):
        own = lax.ppermute(jnp.where(z == 0, first, second), BOTH, swap)
        other = lax.ppermute(jnp.where(z == 0, second, first), BOTH, cross)
        return own, other

    def rows_home(first, second):
        own, other = home(first.astype(BF), second.astype(BF))
        stacked = jnp.where(c == 0, jnp.stack([own, other]), jnp.stack([other, own]))
        return stacked.astype(F32)[None, :, None]

    section_out = rows_home(out_first, out_second)
    input_grad = rows_home(grad_first, grad_second)

    def sum_home(first, second):
        own, other = home(first, second)
        return (own.astype(F32) + other.astype(F32)).astype(BF)

    down_grad = sum_home(parts_first[1], parts_second[1])
    shared_grad = sum_home(parts_first[2], parts_second[2])
    split_grad = collect_grads(jnp.stack([parts_first[0], parts_second[0]]))
    split_grad, down_grad, shared_grad = lax.psum((split_grad, down_grad, shared_grad), "replica")
    split_grad, down_grad, shared_grad = (
        array.astype(F32) for array in (split_grad, down_grad, shared_grad)
    )
    split_rows = split_grad.transpose(1, 0, 2)
    head_rows = split_rows[:, :, :384].reshape(136, 8, 3, 128)
    last = shared_grad[:136, D:]
    grad_qkv = jnp.concatenate(
        [
            head_rows[:, :, 0].reshape(136, 1024),
            last[:, 128:],
            head_rows[:, :, 1].reshape(136, 1024),
            last[:, :64],
            head_rows[:, :, 2].reshape(136, 1024),
            last[:, 64:128],
        ],
        axis=1,
    )
    grad_up = split_rows[:, :, 384:].reshape(136, FF)
    vec = shared_grad[136:].reshape(-1)
    grads = (
        grad_qkv,
        vec[:272],
        shared_grad[:136, :D],
        vec[272:408],
        vec[408:544],
        vec[544:680],
        vec[680:816],
        vec[816:952],
        grad_up,
        vec[952:1496],
        down_grad,
        vec[1496:1632],
    )
    return (section_out, input_grad) + tuple(grad[None] for grad in grads)


def solution(mesh):
    return jax.shard_map(
        local,
        mesh=mesh,
        in_specs=(
            P(None, "replica", "shard", None),
            P(None, "replica", "shard", None),
            P("section", "shard", None),
            P("section", "shard"),
            P("section", "shard", None),
            P("section", "shard"),
            P("section", "shard"),
            P("section", "shard"),
            P("section", "shard"),
            P("section", "shard"),
            P("section", "shard", None),
            P("section", "shard"),
            P("section", "shard", None),
            P("section", "shard"),
        ),
        out_specs=(
            P("section", None, "replica", "shard", None),
            P("section", None, "replica", "shard", None),
            P("section", "shard", None),
            P("section", "shard"),
            P("section", "shard", None),
            P("section", "shard"),
            P("section", "shard"),
            P("section", "shard"),
            P("section", "shard"),
            P("section", "shard"),
            P("section", "shard", None),
            P("section", "shard"),
            P("section", "shard", None),
            P("section", "shard"),
        ),
        check_vma=False,
    )
```

```python
import functools

import jax
import jax.numpy as jnp
from jax import lax
from jax.experimental import pallas as pl
from jax.experimental.pallas import tpu as pltpu
from jax.sharding import PartitionSpec as P

D = 1088
FF = 4352
HEAD_DIM = 64
EPSILON = 1e-05
GELU_C = 0.7978845608028654
NEG_FILL = -1e30
BF = jnp.bfloat16
F32 = jnp.float32
MESH = pl.DeviceIdType.MESH
VMEM = pl.BlockSpec(memory_space=pltpu.VMEM)
LIMIT = 56 * 1024 * 1024


def place():
    c = lax.axis_index("section")
    j = lax.axis_index("shard")
    return c, j // 4, j % 4


def at(c, z, x):
    return {"section": c, "shard": z * 4 + x}


def greet(devices):
    barrier = pltpu.get_barrier_semaphore()
    for device in devices:
        pl.semaphore_signal(barrier, inc=1, device_id=device, device_id_type=MESH)
    pl.semaphore_wait(barrier, len(devices))


def sender(send_sems, recv_sems):
    def make(src, dst, index, device):
        copy = pltpu.make_async_remote_copy(
            src_ref=src,
            dst_ref=dst,
            send_sem=send_sems.at[index],
            recv_sem=recv_sems.at[index],
            device_id=device,
            device_id_type=MESH,
        )
        copy.start()
        return copy

    return make


def gather_core(own, out, send_sems, recv_sems, local_sem, use):
    c, z, x = place()
    ahead, behind, far = (x + 1) % 4, (x + 3) % 4, (x + 2) % 4
    partner, up, down = at(1 - c, z, x), at(c, z, ahead), at(c, z, behind)
    rows = own.shape[0]
    first, second = pl.ds(0, rows // 2), pl.ds(rows // 2, rows // 2)
    me, other = c * 4 + x, (1 - c) * 4
    local = pltpu.make_async_copy(own, out.at[me], local_sem)
    local.start()
    greet((partner, up, down))
    send = sender(send_sems, recv_sems)
    to_up = send(own.at[first], out.at[me, first], 0, up)
    to_down = send(own.at[second], out.at[me, second], 1, down)
    to_partner = send(own, out.at[me], 2, partner)
    up_rest = send(own.at[second], out.at[me, second], 3, up)
    down_rest = send(own.at[first], out.at[me, first], 4, down)
    from_down, from_up, from_far = c * 4 + behind, c * 4 + ahead, c * 4 + far
    local.wait()
    use(me)
    to_up.wait_recv()
    pass_up = send(out.at[from_down, first], out.at[from_down, first], 5, up)
    to_down.wait_recv()
    pass_down = send(out.at[from_up, second], out.at[from_up, second], 6, down)
    to_partner.wait_recv()
    use(other + x)
    up_rest.wait_recv()
    share_down = send(out.at[from_down], out.at[from_down], 7, partner)
    down_rest.wait_recv()
    share_up = send(out.at[from_up], out.at[from_up], 8, partner)
    use(from_down)
    use(from_up)
    pass_up.wait_recv()
    share_first = send(out.at[from_far, first], out.at[from_far, first], 9, partner)
    pass_down.wait_recv()
    share_second = send(out.at[from_far, second], out.at[from_far, second], 10, partner)
    use(from_far)
    share_down.wait_recv()
    use(other + behind)
    share_up.wait_recv()
    use(other + ahead)
    share_first.wait_recv()
    share_second.wait_recv()
    use(other + far)
    for copy in (
        to_up,
        to_down,
        to_partner,
        up_rest,
        down_rest,
        pass_up,
        pass_down,
        share_down,
        share_up,
        share_first,
        share_second,
    ):
        copy.wait_send()


def row_block(q):
    return pl.ds(pl.multiple_of(q * 128, 128), 128)


def gather_qkv_kernel(own, weight, bias, out, projected, send_sems, recv_sems, local_sem):
    def use(q):
        projected[row_block(q), :] = (dot(out[q], weight[...]) + bias[...]).astype(BF)

    gather_core(own, out, send_sems, recv_sems, local_sem, use)


def gather_up_kernel(own, weight, bias, out, upper, activated, send_sems, recv_sems, local_sem):
    def use(q):
        values = dot(out[q], weight[...]) + bias[...]
        upper[row_block(q), :] = values
        activated[row_block(q), :] = gelu_pair(values)[0].astype(BF)

    gather_core(own, out, send_sems, recv_sems, local_sem, use)


def gather_back_kernel(own, weight, upper, out, up_grad, send_sems, recv_sems, local_sem):
    def use(q):
        slope = gelu_pair(upper[row_block(q), :])[1]
        up_grad[row_block(q), :] = (dot_nt(out[q], weight[...]) * slope).astype(BF)

    gather_core(own, out, send_sems, recv_sems, local_sem, use)


def team_gather(kernel, collective_id, own, weight, third, results):
    rows, columns = own.shape
    return pl.pallas_call(
        kernel,
        out_shape=(jax.ShapeDtypeStruct((8, rows, columns), BF),) + results,
        in_specs=[VMEM] * 3,
        out_specs=(VMEM,) * (1 + len(results)),
        scratch_shapes=[
            pltpu.SemaphoreType.DMA((11,)),
            pltpu.SemaphoreType.DMA((11,)),
            pltpu.SemaphoreType.DMA,
        ],
        compiler_params=pltpu.CompilerParams(
            collective_id=collective_id, has_side_effects=True, vmem_limit_bytes=LIMIT
        ),
    )(own, weight, third)


def scatter_core(
    half,
    other_part,
    mine_part,
    prepare,
    beside,
    out,
    from_partner,
    far_sum,
    up_sum,
    down_sum,
    far_first,
    far_second,
    got_down,
    got_up,
    send_sems,
    recv_sems,
):
    c, z, x = place()
    ahead, behind, far = (x + 1) % 4, (x + 3) % 4, (x + 2) % 4
    partner, up, down = at(1 - c, z, x), at(c, z, ahead), at(c, z, behind)
    rows = out.shape[0]
    first, second = pl.ds(0, half), pl.ds(half, rows - half)
    send = sender(send_sems, recv_sems)
    greet([partner, up, down] + beside[0])
    swaps = []
    for index, where in enumerate((far, ahead, behind, x)):
        swaps.append(send(other_part(where), from_partner.at[where], index, partner))
    beside[1]()
    for where in (far, ahead, behind, x):
        prepare(where)
    swap_far, swap_up, swap_down, swap_own = swaps

    def both(where, part):
        return mine_part(where, part) + from_partner[where, part, :].astype(F32)

    swap_far.wait_recv()
    far_sum[first, :] = both(far, first).astype(BF)
    far_up = send(far_sum.at[first], far_first, 4, up)
    far_sum[second, :] = both(far, second).astype(BF)
    far_down = send(far_sum.at[second], far_second, 5, down)
    swap_up.wait_recv()
    up_sum[second, :] = both(ahead, second).astype(BF)
    up_second = send(up_sum.at[second], got_down.at[second], 6, up)
    swap_down.wait_recv()
    down_sum[first, :] = both(behind, first).astype(BF)
    down_first = send(down_sum.at[first], got_up.at[first], 7, down)
    far_up.wait_recv()
    up_sum[first, :] = (both(ahead, first) + far_first[...].astype(F32)).astype(BF)
    up_first = send(up_sum.at[first], got_down.at[first], 8, up)
    far_down.wait_recv()
    down_sum[second, :] = (both(behind, second) + far_second[...].astype(F32)).astype(BF)
    down_second = send(down_sum.at[second], got_up.at[second], 9, down)
    swap_own.wait_recv()
    out[first, :] = both(x, first)
    out[second, :] = both(x, second)
    beside[2]()
    up_second.wait_recv()
    up_first.wait_recv()
    down_first.wait_recv()
    down_second.wait_recv()
    out[...] = out[...] + got_down[...].astype(F32) + got_up[...].astype(F32)
    for copy in (
        swap_far,
        swap_up,
        swap_down,
        swap_own,
        far_up,
        far_down,
        up_second,
        down_first,
        up_first,
        down_second,
    ):
        copy.wait_send()
    beside[3]()


def nothing():
    pass


ALONE = ([], nothing, nothing, nothing)


def product_scatter_kernel(product, left, right, out, other, mine, *rest):
    c, z, x = place()

    def other_part(where):
        rows = left[row_block((1 - c) * 4 + where), :]
        other[where] = product(rows, right[...]).astype(BF)
        return other.at[where]

    def prepare(where):
        mine[where] = product(left[row_block(c * 4 + where), :], right[...])

    scatter_core(
        64, other_part, lambda where, part: mine[where, part, :], prepare, ALONE, out, *rest
    )


def scatter_scratch(rows, columns, half):
    block = pltpu.VMEM((rows, columns), BF)
    return [
        pltpu.VMEM((4, rows, columns), BF),
        block,
        block,
        block,
        pltpu.VMEM((half, columns), BF),
        pltpu.VMEM((rows - half, columns), BF),
        block,
        block,
        pltpu.SemaphoreType.DMA((10,)),
        pltpu.SemaphoreType.DMA((10,)),
    ]


def product_scatter(product, collective_id, left, right):
    return pl.pallas_call(
        functools.partial(product_scatter_kernel, product),
        out_shape=jax.ShapeDtypeStruct((128, D), F32),
        in_specs=[VMEM, VMEM],
        out_specs=VMEM,
        scratch_shapes=[pltpu.VMEM((4, 128, D), BF), pltpu.VMEM((4, 128, D), F32)]
        + scatter_scratch(128, D, 64),
        compiler_params=pltpu.CompilerParams(
            collective_id=collective_id, has_side_effects=True, vmem_limit_bytes=LIMIT
        ),
    )(left, right)


TEAM_STEPS = tuple((dc, dx) for dc in range(2) for dx in range(4) if dc or dx)


def heads_to_rows_kernel(heads, extra, out, send_sems, recv_sems, local_sems):
    c, z, x = place()
    me = c * 4 + x
    spots = [((c + dc) % 2, (x + dx) % 4) for dc, dx in TEAM_STEPS]
    own_columns = pl.ds(pl.multiple_of(me * 128, 128), 128)
    local = pltpu.make_async_copy(heads.at[me], out.at[:, own_columns], local_sems.at[0])
    local.start()
    last = pltpu.make_async_copy(extra, out.at[:, pl.ds(1024, 128)], local_sems.at[1])
    last.start()
    greet([at(tc, z, tx) for tc, tx in spots])
    send = sender(send_sems, recv_sems)
    copies = [
        send(heads.at[tc * 4 + tx], out.at[:, own_columns], index, at(tc, z, tx))
        for index, (tc, tx) in enumerate(spots)
    ]
    for copy in copies:
        copy.wait_recv()
    for copy in copies:
        copy.wait_send()
    local.wait()
    last.wait()


def heads_to_rows(heads, extra):
    return pl.pallas_call(
        heads_to_rows_kernel,
        out_shape=jax.ShapeDtypeStruct((128, 1152), BF),
        in_specs=[VMEM, VMEM],
        out_specs=VMEM,
        scratch_shapes=[
            pltpu.SemaphoreType.DMA((7,)),
            pltpu.SemaphoreType.DMA((7,)),
            pltpu.SemaphoreType.DMA((2,)),
        ],
        compiler_params=pltpu.CompilerParams(
            collective_id=1, has_side_effects=True, vmem_limit_bytes=LIMIT
        ),
    )(heads, extra)


def rows_to_heads_kernel(rows, out, send_sems, recv_sems, local_sem):
    c, z, x = place()
    me = c * 4 + x
    spots = [((c + dc) % 2, (x + dx) % 4) for dc, dx in TEAM_STEPS]

    def columns(q):
        return rows.at[:, pl.ds(pl.multiple_of(q * 128, 128), 128)]

    local = pltpu.make_async_copy(columns(me), out.at[me], local_sem)
    local.start()
    greet([at(tc, z, tx) for tc, tx in spots])
    send = sender(send_sems, recv_sems)
    copies = [
        send(columns(tc * 4 + tx), out.at[me], index, at(tc, z, tx))
        for index, (tc, tx) in enumerate(spots)
    ]
    for copy in copies:
        copy.wait_recv()
    for copy in copies:
        copy.wait_send()
    local.wait()


def rows_to_heads(rows):
    return pl.pallas_call(
        rows_to_heads_kernel,
        out_shape=jax.ShapeDtypeStruct((8, 128, 128), BF),
        in_specs=[VMEM],
        out_specs=VMEM,
        scratch_shapes=[
            pltpu.SemaphoreType.DMA((7,)),
            pltpu.SemaphoreType.DMA((7,)),
            pltpu.SemaphoreType.DMA,
        ],
        compiler_params=pltpu.CompilerParams(
            collective_id=2, has_side_effects=True, vmem_limit_bytes=LIMIT
        ),
    )(rows)


def ring_spread(send, base, source, block, me, up, down, first, second):
    before, after = (me + 3) % 4, (me + 1) % 4
    copies = [
        send(source(first), block(me, first), base, up),
        send(source(second), block(me, second), base + 1, down),
        send(source(second), block(me, second), base + 2, up),
        send(source(first), block(me, first), base + 3, down),
    ]

    def middle():
        copies[0].wait_recv()
        copies.append(send(block(before, first), block(before, first), base + 4, up))
        copies[1].wait_recv()
        copies.append(send(block(after, second), block(after, second), base + 5, down))

    def last():
        for copy in copies[2:]:
            copy.wait_recv()

    return copies, middle, last


def weights_kernel(
    late,
    common,
    rows,
    other_rows,
    first,
    second,
    out_common,
    out_rows,
    out_other,
    send_sems,
    recv_sems,
    common_send,
    common_recv,
    share_send,
    share_recv,
    ring_send,
    ring_recv,
    swap_send,
    swap_recv,
    local_sems,
):
    c, z, x = place()
    r = lax.axis_index("replica")
    y, zh = r // 2, r % 2
    zf = zh * 2 + z
    slot = z * 4 + x

    def device(ty, tz):
        return {"section": c, "shard": (tz % 2) * 4 + x, "replica": ty * 2 + tz // 2}

    y_up, y_down = device((y + 1) % 4, zf), device((y + 3) % 4, zf)
    z_up, z_down = device(y, (zf + 1) % 4), device(y, (zf + 3) % 4)
    z_other = device(y, (zf + 3 + 2 * z) % 4)
    partner, diagonal, z_pair = at(1 - c, z, x), at(1 - c, 1 - z, x), at(c, 1 - z, x)
    team = [((c + dc) % 2, (x + dx) % 4) for dc, dx in TEAM_STEPS]
    core_steps = [(dz, dx) for dx in (1, 3, 2, 0) for dz in range(2) if dz or dx]
    core = [((z + dz) % 2, (x + dx) % 4) for dz, dx in core_steps]
    source_of = [core_steps.index((dz, (4 - dx) % 4)) for dz, dx in core_steps]
    greet(
        [at(tc, z, tx) for tc, tx in team]
        + [at(c, 1 - z, (x + dx) % 4) for dx in range(4)]
        + [diagonal, y_up, y_down, z_other]
    )

    def remote(src, dst, sends, recvs, index, target):
        return pltpu.make_async_remote_copy(
            src_ref=src,
            dst_ref=dst,
            send_sem=sends.at[index],
            recv_sem=recvs.at[index],
            device_id=target,
            device_id_type=MESH,
        )

    def to_team(index, layer):
        tc, tx = team[index]
        place_at = first.at[y, zf, x] if layer == 0 else second.at[slot]
        return remote(late.at[tc * 4 + tx], place_at, send_sems, recv_sems, index, at(tc, z, tx))

    def swapped(index):
        src, dst = ((rows, out_rows), (other_rows, out_other))[index]
        return remote(src.at[c], dst, swap_send, swap_recv, index, diagonal)

    def kept(index):
        src, dst = ((rows, out_rows), (other_rows, out_other))[index]
        return pltpu.make_async_copy(src.at[c], dst, local_sems.at[2 + index])

    def common_to(index):
        tz, tx = core[index]
        return remote(
            common, out_common.at[c, slot], common_send, common_recv, index, at(c, tz, tx)
        )

    def shared(index):
        if index == 7:
            source = out_common.at[c, slot]
        else:
            tz, tx = core[index]
            source = out_common.at[c, tz * 4 + tx]
        return remote(source, source, share_send, share_recv, index, partner)

    keep = pltpu.make_async_copy(common, out_common.at[c, slot], local_sems.at[0])
    keep.start()

    @pl.when(c == 0)
    def _():
        for index in range(7):
            to_team(index, 0).start()
        pltpu.make_async_copy(late.at[c * 4 + x], first.at[y, zf, x], local_sems.at[1]).start()

    @pl.when(c == 1)
    def _():
        for index in range(7):
            to_team(index, 1).start()
        pltpu.make_async_copy(late.at[c * 4 + x], second.at[slot], local_sems.at[1]).start()

    for index in range(7):
        common_to(index).start()

    @pl.when(c == z)
    def _():
        kept(0).start()
        kept(1).start()

    @pl.when(c != z)
    def _():
        swapped(0).start()
        swapped(1).start()

    for index, (dc, dx) in enumerate(TEAM_STEPS):

        @pl.when((c + dc) % 2 == 0)
        def _():
            to_team(index, 0).wait_recv()

        @pl.when((c + dc) % 2 == 1)
        def _():
            to_team(index, 1).wait_recv()

    @pl.when(c == 0)
    def _():
        pltpu.make_async_copy(late.at[c * 4 + x], first.at[y, zf, x], local_sems.at[1]).wait()

    @pl.when(c == 1)
    def _():
        pltpu.make_async_copy(late.at[c * 4 + x], second.at[slot], local_sems.at[1]).wait()

    def send(src, dst, index, target):
        copy = remote(src, dst, ring_send, ring_recv, index, target)
        copy.start()
        return copy

    one, two = pl.ds(0, 1), pl.ds(1, 1)
    three, four = pl.ds(2, 1), pl.ds(3, 1)
    left, right = pl.ds(0, 2), pl.ds(2, 2)
    y_copies, y_middle, y_last = ring_spread(
        send,
        0,
        lambda part: first.at[y, zf, part],
        lambda i, part: first.at[i, zf, part],
        y,
        y_up,
        y_down,
        one,
        two,
    )
    z_copies, z_middle, z_last = ring_spread(
        send,
        6,
        lambda part: first.at[y, zf, part],
        lambda i, part: first.at[y, i, part],
        zf,
        z_up,
        z_down,
        three,
        four,
    )
    pair_copy = send(second.at[pl.ds(z * 4, 4)], second.at[pl.ds(z * 4, 4)], 24, z_pair)
    keep.wait()
    shared(7).start()
    for index in range(7):
        common_to(source_of[index]).wait_recv()
        shared(index).start()
    y_middle()
    z_middle()
    y_last()
    more_z, z_middle_too, z_last_too = ring_spread(
        send,
        12,
        lambda part: first.at[part, zf, pl.ds(0, 2)],
        lambda i, part: first.at[part, i, pl.ds(0, 2)],
        zf,
        z_up,
        z_down,
        left,
        right,
    )
    z_last()
    more_y, y_middle_too, y_last_too = ring_spread(
        send,
        18,
        lambda part: first.at[y, part, pl.ds(2, 2)],
        lambda i, part: first.at[i, part, pl.ds(2, 2)],
        y,
        y_up,
        y_down,
        left,
        right,
    )
    z_middle_too()
    y_middle_too()
    pair_copy.wait_recv()
    for index in range(8):
        shared(index).wait_recv()
    z_last_too()
    y_last_too()

    @pl.when(c == z)
    def _():
        kept(0).wait()
        kept(1).wait()

    @pl.when(c != z)
    def _():
        for index in range(2):
            swapped(index).wait_recv()
            swapped(index).wait_send()

    @pl.when(c == 0)
    def _():
        for index in range(7):
            to_team(index, 0).wait_send()

    @pl.when(c == 1)
    def _():
        for index in range(7):
            to_team(index, 1).wait_send()

    for index in range(7):
        common_to(index).wait_send()
    for index in range(8):
        shared(index).wait_send()
    for copy in y_copies + z_copies + more_z + more_y + [pair_copy]:
        copy.wait_send()


def spread_weights(late, common, rows, other_rows):
    dma = pltpu.SemaphoreType.DMA
    return pl.pallas_call(
        weights_kernel,
        out_shape=(
            jax.ShapeDtypeStruct((4, 4, 4, 144, 128), BF),
            jax.ShapeDtypeStruct(late.shape, BF),
            jax.ShapeDtypeStruct((2, 8) + common.shape, BF),
            jax.ShapeDtypeStruct(rows.shape[1:], BF),
            jax.ShapeDtypeStruct(rows.shape[1:], BF),
        ),
        in_specs=[VMEM] * 4,
        out_specs=(VMEM,) * 5,
        scratch_shapes=[
            dma((7,)),
            dma((7,)),
            dma((7,)),
            dma((7,)),
            dma((8,)),
            dma((8,)),
            dma((25,)),
            dma((25,)),
            dma((2,)),
            dma((2,)),
            dma((4,)),
        ],
        compiler_params=pltpu.CompilerParams(
            collective_id=3, has_side_effects=True, vmem_limit_bytes=LIMIT
        ),
    )(late, common, rows, other_rows)


SPLIT_ROWS = 4 * 144
DOWN_ROWS = 320
SHARED_ROWS = 96
ROWS = SPLIT_ROWS + DOWN_ROWS + SHARED_ROWS
OWN_ROWS = DOWN_ROWS + SHARED_ROWS
GOT_ROWS = 8 * 144 + 2 * OWN_ROWS


def widen(block):
    return block.astype(F32)


def ring_reduce(send, base, block, me, up, down, first, second, far, relay, got, result):
    after, before, opposite = (me + 1) % 4, (me + 3) % 4, (me + 2) % 4
    copies = [
        send(block(opposite, first), far[0], base, up),
        send(block(opposite, second), far[1], base + 1, down),
        send(block(after, second), got[0].at[second], base + 2, up),
        send(block(before, first), got[1].at[first], base + 3, down),
    ]

    def middle():
        copies[0].wait_recv()
        relay[0][...] = (widen(block(after, first)[...]) + widen(far[0][...])).astype(BF)
        copies.append(send(relay[0], got[0].at[first], base + 4, up))
        copies[1].wait_recv()
        relay[1][...] = (widen(block(before, second)[...]) + widen(far[1][...])).astype(BF)
        copies.append(send(relay[1], got[1].at[second], base + 5, down))

    def last():
        for copy in copies[2:]:
            copy.wait_recv()
        for part in (first, second):
            value = (
                widen(block(me, part)[...])
                + widen(got[0].at[part][...])
                + widen(got[1].at[part][...])
            )
            result.at[part][...] = value.astype(BF)
        for copy in copies:
            copy.wait_send()

    return middle, last


TOP = ROWS // 2
CUT = TOP // 32 * 16


def rings_scratch():
    dma = pltpu.SemaphoreType.DMA
    return [
        pltpu.VMEM((2, 4, TOP, 128), BF),
        pltpu.VMEM((2, 2, 2, TOP, 128), BF),
        pltpu.VMEM((2, 2, 2, TOP, 128), BF),
        pltpu.VMEM((2, 2, 4, TOP, 128), BF),
        pltpu.VMEM((2, 2, TOP - CUT, 128), BF),
        pltpu.VMEM((2, 2, TOP - CUT, 128), BF),
        pltpu.VMEM((2, 2, TOP, 128), BF),
        dma((24,)),
        dma((24,)),
    ]


def grid_place():
    c, z, x = place()
    r = lax.axis_index("replica")
    y, zh = r // 2, r % 2
    zf = zh * 2 + z

    def device(ty, tz):
        return {"section": c, "shard": (tz % 2) * 4 + x, "replica": ty * 2 + tz // 2}

    return (
        y,
        zf,
        (
            device((y + 1) % 4, zf),
            device((y + 3) % 4, zf),
            device(y, (zf + 1) % 4),
            device(y, (zf + 3) % 4),
        ),
    )


def layer_rings(pieces, out, wide_sum, far, relay, got, far_s, relay_s, got_s, sends, recvs):
    y, zf, (y_up, y_down, z_up, z_down) = grid_place()

    def send(src, dst, index, target):
        copy = pltpu.make_async_remote_copy(
            src_ref=src,
            dst_ref=dst,
            send_sem=sends.at[index],
            recv_sem=recvs.at[index],
            device_id=target,
            device_id_type=MESH,
        )
        copy.start()
        return copy

    low, high = pl.ds(0, 2), pl.ds(2, 2)
    top, bottom = pl.ds(0, TOP), pl.ds(TOP, TOP)
    first, second = pl.ds(0, CUT), pl.ds(CUT, TOP - CUT)

    def wide(k):
        return (
            [far.at[k, 0], far.at[k, 1]],
            [relay.at[k, 0], relay.at[k, 1]],
            [got.at[k, 0], got.at[k, 1]],
            wide_sum.at[k],
        )

    def small(k, result):
        parts = pl.ds(0, CUT), pl.ds(0, TOP - CUT)
        return (
            [far_s.at[k, 0, parts[0]], far_s.at[k, 1, parts[1]]],
            [relay_s.at[k, 0, parts[0]], relay_s.at[k, 1, parts[1]]],
            [got_s.at[k, 0], got_s.at[k, 1]],
            result,
        )

    y_mid, y_last = ring_reduce(
        send,
        0,
        lambda i, part: pieces.at[i, part, top],
        y,
        y_up,
        y_down,
        low,
        high,
        *wide(0),
    )
    z_mid, z_last = ring_reduce(
        send,
        6,
        lambda i, part: pieces.at[part, i, bottom],
        zf,
        z_up,
        z_down,
        low,
        high,
        *wide(1),
    )
    later = []

    def turn():
        y_last()
        later.append(
            ring_reduce(
                send,
                12,
                lambda i, part: wide_sum.at[0, i, part],
                zf,
                z_up,
                z_down,
                first,
                second,
                *small(0, out.at[top]),
            )
        )
        z_last()
        later.append(
            ring_reduce(
                send,
                18,
                lambda i, part: wide_sum.at[1, i, part],
                y,
                y_up,
                y_down,
                first,
                second,
                *small(1, out.at[bottom]),
            )
        )

    def middle():
        y_mid()
        z_mid()

    def finish():
        for mid, _ in later:
            mid()
        for _, last in later:
            last()

    return middle, turn, finish


def reduce_kernel(
    pieces,
    second_layer,
    out,
    summed,
    own,
    home_send,
    home_recv,
    local_sems,
    spread_send,
    spread_recv,
    *scratch,
):
    c, z, x = place()
    r = lax.axis_index("replica")
    y, zh = r // 2, r % 2
    zf, (y_up, y_down, z_up, z_down) = grid_place()[1:]
    across = {"section": c, "shard": z * 4 + x, "replica": y * 2 + 1 - zh}
    team = [at((c + dc) % 2, z, (x + dx) % 4) for dc, dx in TEAM_STEPS]
    greet([y_up, y_down, z_up, z_down, across, at(1 - c, 1 - z, x)] + team)

    def remote(src, dst, sends, recvs, index, target):
        copy = pltpu.make_async_remote_copy(
            src_ref=src,
            dst_ref=dst,
            send_sem=sends.at[index],
            recv_sem=recvs.at[index],
            device_id=target,
            device_id_type=MESH,
        )
        copy.start()
        return copy

    middle, turn, finish = layer_rings(pieces, summed.at[0], *scratch)
    summed[1] = second_layer[...]
    middle()
    turn()
    finish()

    me = c * 4 + x
    mine = pl.ds(pl.multiple_of(me * 144, 16), 144)
    own_part = pl.ds(SPLIT_ROWS, OWN_ROWS)

    def home_part(t):
        return own.at[pl.ds(pl.multiple_of(8 * 144 + t * OWN_ROWS, 16), OWN_ROWS)]

    def split_part(tc, tx):
        return summed.at[tc, pl.ds(pl.multiple_of(tx * 144, 16), 144)]

    keep = pltpu.make_async_copy(split_part(c, x), own.at[mine], local_sems.at[0])
    keep.start()
    copies = []
    for index, (dc, dx) in enumerate(TEAM_STEPS):
        tc, tx = (c + dc) % 2, (x + dx) % 4
        copies.append(
            remote(split_part(tc, tx), own.at[mine], home_send, home_recv, index, at(tc, z, tx))
        )

    def same_layer():
        return pltpu.make_async_remote_copy(
            src_ref=summed.at[c, own_part],
            dst_ref=home_part(z),
            send_sem=home_send.at[7],
            recv_sem=home_recv.at[7],
            device_id=at(c, 1 - z, x),
            device_id_type=MESH,
        )

    def same_here():
        return pltpu.make_async_copy(summed.at[c, own_part], home_part(z), local_sems.at[1])

    def other_layer(t):
        return pltpu.make_async_remote_copy(
            src_ref=summed.at[1 - c, own_part],
            dst_ref=home_part(z),
            send_sem=home_send.at[8],
            recv_sem=home_recv.at[8 + t],
            device_id=at(1 - c, c, x),
            device_id_type=MESH,
        )

    @pl.when(z == c)
    def _():
        same_here().start()

    @pl.when(z != c)
    def _():
        same_layer().start()

    other_layer(z).start()
    for copy in copies:
        copy.wait_recv()

    @pl.when(z == c)
    def _():
        same_here().wait()
        same_layer().wait_recv()

    @pl.when(z != c)
    def _():
        other_layer(0).wait_recv()
        other_layer(1).wait_recv()
        same_layer().wait_send()

    other_layer(z).wait_send()
    for copy in copies:
        copy.wait_send()
    keep.wait()

    here = y * 2 + zh
    front, back = pl.ds(0, GOT_ROWS // 2), pl.ds(GOT_ROWS // 2, GOT_ROWS // 2)
    local = pltpu.make_async_copy(own, out.at[here], local_sems.at[2])
    local.start()

    def send(src, dst, index, target):
        return remote(src, dst, spread_send, spread_recv, index, target)

    over = send(own, out.at[here], 0, across)

    def spread(base, source, block):
        return [
            send(source.at[front], out.at[block, front], base, y_up),
            send(source.at[back], out.at[block, back], base + 1, y_down),
            send(source.at[back], out.at[block, back], base + 2, y_up),
            send(source.at[front], out.at[block, front], base + 3, y_down),
        ]

    def forward(base, which, sent):
        below, above = ((y + 3) % 4) * 2 + which, ((y + 1) % 4) * 2 + which
        sent[0].wait_recv()
        sent.append(send(out.at[below, front], out.at[below, front], base + 4, y_up))
        sent[1].wait_recv()
        sent.append(send(out.at[above, back], out.at[above, back], base + 5, y_down))

    sent = spread(1, own, here)
    forward(1, zh, sent)
    over.wait_recv()
    there = y * 2 + 1 - zh
    more = spread(7, out.at[there], there)
    forward(7, 1 - zh, more)
    for copy in sent[2:] + more[2:]:
        copy.wait_recv()
    for copy in [over] + sent + more:
        copy.wait_send()
    local.wait()


def reduce_grads(pieces, second_layer):
    dma = pltpu.SemaphoreType.DMA
    return pl.pallas_call(
        reduce_kernel,
        out_shape=jax.ShapeDtypeStruct((8, GOT_ROWS, 128), BF),
        in_specs=[VMEM, VMEM],
        out_specs=VMEM,
        scratch_shapes=[
            pltpu.VMEM((2, ROWS, 128), BF),
            pltpu.VMEM((GOT_ROWS, 128), BF),
            dma((9,)),
            dma((10,)),
            dma((3,)),
            dma((13,)),
            dma((13,)),
        ]
        + rings_scratch(),
        compiler_params=pltpu.CompilerParams(
            collective_id=4, has_side_effects=True, vmem_limit_bytes=LIMIT
        ),
    )(pieces, second_layer)


def shared_kernel(rings, *refs):
    if rings:
        pieces, *refs = refs
    attended, middle_low, normed_all, qkv_grad, normed, last_grad, vectors, rows = refs[:8]
    refs = refs[8:]
    if rings:
        out, out_rows, out_pieces, *refs = refs
    else:
        out, out_rows, *refs = refs
    products, last_keys, last_queries, parts, home_send, home_recv, home_local, *refs = refs
    scatter_refs, ring_refs = refs[:10], refs[10:]
    c, z, x = place()
    products[...] = dot_tn(attended[...], middle_low[...])
    last_keys[...] = dot_tn(normed_all[...], qkv_grad[:, 384:512])
    last_queries[...] = dot_tn(normed[...], last_grad[...])
    for j in range(8):
        block = pl.ds(136 * j, 136)

        def stack(value, lanes):
            tail = vectors[j, :, lanes]
            return jnp.concatenate([value, tail], axis=0).astype(BF)

        if j < 7:
            product = products[block, :]
        else:
            product = jnp.concatenate(
                [products[952:1024, :], products[1088:1152, :]], axis=0
            )
        parts[j, :, 0:128] = stack(last_keys[block, :], pl.ds(0, 128))
        parts[j, :, 128:1152] = stack(product[:, 0:1024], pl.ds(128, 1024))
        parts[j, :, 1152:1280] = stack(
            product[:, 1024:1152] + last_queries[block, :], pl.ds(1152, 128)
        )

    def same_layer():
        return pltpu.make_async_remote_copy(
            src_ref=rows.at[c],
            dst_ref=out_rows.at[z],
            send_sem=home_send.at[0],
            recv_sem=home_recv.at[0],
            device_id=at(c, 1 - z, x),
            device_id_type=MESH,
        )

    def same_here():
        return pltpu.make_async_copy(rows.at[c], out_rows.at[z], home_local)

    def other_layer(t):
        return pltpu.make_async_remote_copy(
            src_ref=rows.at[1 - c],
            dst_ref=out_rows.at[z],
            send_sem=home_send.at[1],
            recv_sem=home_recv.at[1 + t],
            device_id=at(1 - c, c, x),
            device_id_type=MESH,
        )

    stages = []

    def begin():
        if rings:
            stages.extend(layer_rings(pieces, out_pieces, *ring_refs))

        @pl.when(z == c)
        def _():
            same_here().start()

        @pl.when(z != c)
        def _():
            same_layer().start()

        other_layer(z).start()

    def during():
        if rings:
            stages[0]()
            stages[1]()

    def end():
        if rings:
            stages[2]()

        @pl.when(z == c)
        def _():
            same_here().wait()
            same_layer().wait_recv()

        @pl.when(z != c)
        def _():
            other_layer(0).wait_recv()
            other_layer(1).wait_recv()
            same_layer().wait_send()

        other_layer(z).wait_send()

    friends = [at(c, 1 - z, x), at(1 - c, 1 - z, x)]
    if rings:
        y, zf, (y_up, y_down, z_up, z_down) = grid_place()
        z_other = {
            "section": c,
            "shard": (1 - z) * 4 + x,
            "replica": y * 2 + ((zf + 3 + 2 * z) % 4) // 2,
        }
        friends += [y_up, y_down, z_other]

    def mine_part(where, part):
        return parts[c * 4 + where, part, :].astype(F32)

    scatter_core(
        64,
        lambda where: parts.at[(1 - c) * 4 + where],
        mine_part,
        lambda where: None,
        (friends, begin, during, end),
        out,
        *scatter_refs,
    )


def shared_scatter(operands, pieces):
    rings = pieces is not None
    dma = pltpu.SemaphoreType.DMA
    out_shape = (
        jax.ShapeDtypeStruct((144, 1280), F32),
        jax.ShapeDtypeStruct((2, 128, D), BF),
    )
    if rings:
        operands = (pieces,) + operands
        out_shape += (jax.ShapeDtypeStruct((ROWS, 128), BF),)
    return pl.pallas_call(
        functools.partial(shared_kernel, rings),
        out_shape=out_shape,
        in_specs=[VMEM] * len(operands),
        out_specs=(VMEM,) * len(out_shape),
        scratch_shapes=[
            pltpu.VMEM((1152, 1152), F32),
            pltpu.VMEM((D, 128), F32),
            pltpu.VMEM((D, 128), F32),
            pltpu.VMEM((8, 144, 1280), BF),
            dma((2,)),
            dma((3,)),
            dma,
        ]
        + scatter_scratch(144, 1280, 64)
        + (rings_scratch() if rings else []),
        compiler_params=pltpu.CompilerParams(
            collective_id=11 if rings else 6, has_side_effects=True, vmem_limit_bytes=LIMIT
        ),
    )(*operands)


def segments(start, size, piece_rows):
    done = 0
    while done < size:
        piece, row = divmod(start + done, piece_rows)
        count = min(piece_rows - row, size - done)
        yield piece, row, done, count
        done += count


def pieces_kernel(
    normed_all, qkv_grad, second_all, up_grad, activated, low_all, shared, out, wide, tall
):
    wide[:, 896:1024] = jnp.zeros((D, 128), F32)
    wide[:, 0:384] = dot_tn(normed_all[...], qkv_grad[:, 0:384])
    wide[:, 384:928] = dot_tn(second_all[...], up_grad[...])
    blank = jnp.zeros((8, 128), F32)
    for chunk in range(8):
        for j in range(8):
            block = wide[136 * j : 136 * j + 136, 128 * chunk : 128 * chunk + 128]
            place_at = pl.ds((j % 4) * 144, 144)
            out[chunk // 2, (chunk % 2) * 2 + j // 4, place_at, :] = jnp.concatenate(
                [block, blank], axis=0
            ).astype(BF)
    tall[:, 1024:1152] = jnp.zeros((544, 128), F32)
    tall[:, 0:D] = dot_tn(activated[...], low_all[...])

    def put(base, piece_rows, start, value):
        for piece, row, at_row, count in segments(start, value.shape[0], piece_rows):
            out[piece // 4, piece % 4, base + row : base + row + count, :] = value[
                at_row : at_row + count
            ].astype(BF)

    for k in range(9):
        put(SPLIT_ROWS, DOWN_ROWS, 544 * k, tall[:, 128 * k : 128 * k + 128])
    put(SPLIT_ROWS, DOWN_ROWS, 9 * 544, jnp.zeros((16 * DOWN_ROWS - 9 * 544, 128), F32))
    base = SPLIT_ROWS + DOWN_ROWS
    for k in range(10):
        put(base, SHARED_ROWS, 144 * k, shared[:, 128 * k : 128 * k + 128])
    put(base, SHARED_ROWS, 1440, jnp.zeros((16 * SHARED_ROWS - 1440, 128), F32))


def grad_pieces(*operands):
    return pl.pallas_call(
        pieces_kernel,
        out_shape=jax.ShapeDtypeStruct((4, 4, ROWS, 128), BF),
        in_specs=[VMEM] * 7,
        out_specs=VMEM,
        scratch_shapes=[pltpu.VMEM((D, 1024), F32), pltpu.VMEM((544, 1152), F32)],
        compiler_params=pltpu.CompilerParams(vmem_limit_bytes=LIMIT),
    )(*operands)


def assemble_kernel(got, qkv, out_w, up, down, vectors, shared):
    for q in range(8):
        for chunk in range(8):
            block = got[chunk, 144 * q : 144 * q + 144, :].astype(F32)[:136]
            if chunk < 3:
                start = chunk * D + 128 * q
                qkv[:, start : start + 128] = block
            elif chunk < 7:
                start = 544 * q + 128 * (chunk - 3)
                up[:, start : start + 128] = block
            else:
                up[:, 544 * q + 512 : 544 * q + 544] = block[:, :32]
    for k in range(9):
        width = 128 if k < 8 else 64
        for piece, row, at_row, count in segments(544 * k, 544, DOWN_ROWS):
            start = 8 * 144 + (piece % 2) * OWN_ROWS + row
            block = got[piece // 2, start : start + count, :].astype(F32)
            down[at_row : at_row + count, 128 * k : 128 * k + width] = block[:, :width]
    for k in range(10):
        for piece, row, at_row, count in segments(144 * k, 144, SHARED_ROWS):
            start = 8 * 144 + (piece % 2) * OWN_ROWS + DOWN_ROWS + row
            block = got[piece // 2, start : start + count, :].astype(F32)
            shared[k, at_row : at_row + count, :] = block
        vectors[:, 128 * k : 128 * k + 128] = shared[k, 136:144, :]
        if 1 <= k < 9:
            out_w[:, 128 * (k - 1) : 128 * k] = shared[k, 0:136, :]
    out_w[:, 1024:D] = shared[9, 0:136, 0:64]
    qkv[:, 1024:D] = shared[9, 0:136, 64:128]
    qkv[:, D + 1024 : 2 * D] = shared[0, 0:136, 0:64]
    qkv[:, 2 * D + 1024 : 3 * D] = shared[0, 0:136, 64:128]


def assemble(got):
    shapes = ((136, 3 * D), (136, D), (136, FF), (544, D), (8, 1280))
    return pl.pallas_call(
        assemble_kernel,
        out_shape=tuple(jax.ShapeDtypeStruct(shape, F32) for shape in shapes),
        in_specs=[VMEM],
        out_specs=(VMEM,) * 5,
        scratch_shapes=[pltpu.VMEM((10, 144, 128), F32)],
        compiler_params=pltpu.CompilerParams(vmem_limit_bytes=LIMIT),
    )(got)


def dot_nt(left, right):
    return lax.dot_general(left, right, (((1,), (1,)), ((), ())), preferred_element_type=F32)


def dot_tn(left, right):
    return lax.dot_general(left, right, (((0,), (0,)), ((), ())), preferred_element_type=F32)


def dot(left, right):
    return jnp.dot(left, right, preferred_element_type=F32)


def lane_half(block, which):
    lane = lax.broadcasted_iota(jnp.int32, block.shape, 1)
    keep = lane < 64 if which == 0 else lane >= 64
    return jnp.where(keep, block, jnp.zeros_like(block))


def softmax_rows(scores, start):
    row = lax.broadcasted_iota(jnp.int32, scores.shape, 0) + start
    key = lax.broadcasted_iota(jnp.int32, scores.shape, 1)
    masked = jnp.where(key <= row, scores, NEG_FILL)
    shifted = jnp.exp(masked - jnp.max(masked, axis=1, keepdims=True))
    return shifted * (1.0 / jnp.sum(shifted, axis=1, keepdims=True))


STEP = 256


def attend_kernel(projected, last_query, attended, attended_last):
    c, z, x = place()
    for start in range(0, 1024, STEP):
        size = start + STEP
        query = projected[start:size, 0:128] * 0.125
        total = jnp.zeros((STEP, 128), F32)
        for head in range(2):
            keys = lane_half(projected[0:size, 128:256], head)
            values = lane_half(projected[0:size, 256:384], head)
            soft = softmax_rows(dot_nt(query, keys), start).astype(BF)
            total = total + dot(soft, values)
        attended[start:size, :] = total.astype(BF)
    both = projected[:, 384:512]
    soft = softmax_rows(dot_nt(last_query[...] * 0.125, both), (c * 4 + x) * 128).astype(BF)
    attended_last[...] = dot(soft, lane_half(both, 1)).astype(BF)


def attend(projected, last_query):
    return pl.pallas_call(
        attend_kernel,
        out_shape=(
            jax.ShapeDtypeStruct((1024, 128), BF),
            jax.ShapeDtypeStruct((128, 128), BF),
        ),
        in_specs=[VMEM, VMEM],
        out_specs=(VMEM, VMEM),
        compiler_params=pltpu.CompilerParams(vmem_limit_bytes=LIMIT),
    )(projected, last_query)


def attend_back_kernel(
    projected, last_query, grad, last_grad, out, out_last, key_total, value_total
):
    c, z, x = place()
    key_total[...] = jnp.zeros_like(key_total)
    value_total[...] = jnp.zeros_like(value_total)
    for start in range(0, 1024, STEP):
        size = start + STEP
        query = projected[start:size, 0:128] * 0.125
        grad_rows = grad[start:size, :]
        total = jnp.zeros((STEP, 128), F32)
        for head in range(2):
            keys = lane_half(projected[0:size, 128:256], head)
            values = lane_half(projected[0:size, 256:384], head)
            soft = softmax_rows(dot_nt(query, keys), start)
            grad_soft = dot_nt(grad_rows, values)
            inner = jnp.sum(soft * grad_soft, axis=1, keepdims=True)
            grad_scores = (soft * (grad_soft - inner)).astype(BF)
            total = total + dot(grad_scores, keys)
            key_total[0:size, :] += dot_tn(grad_scores, lane_half(query, head))
            value_total[0:size, :] += dot_tn(soft.astype(BF), lane_half(grad_rows, head))
        out[start:size, 0:128] = (total * 0.125).astype(BF)
    out[:, 128:256] = key_total[...].astype(BF)
    out[:, 256:384] = value_total[...].astype(BF)
    both = projected[:, 384:512]
    query = last_query[...] * 0.125
    soft = softmax_rows(dot_nt(query, both), (c * 4 + x) * 128)
    grad_soft = dot_nt(last_grad[...], both)
    inner = jnp.sum(soft * grad_soft, axis=1, keepdims=True)
    grad_scores = (soft * (grad_soft - inner)).astype(BF)
    out_last[...] = (dot(grad_scores, lane_half(both, 0)) * 0.125).astype(BF)
    out[:, 384:512] = (dot_tn(grad_scores, query) + dot_tn(soft.astype(BF), last_grad[...])).astype(
        BF
    )


def attend_back(projected, last_query, grad, last_grad):
    return pl.pallas_call(
        attend_back_kernel,
        out_shape=(
            jax.ShapeDtypeStruct((1024, 512), BF),
            jax.ShapeDtypeStruct((128, 128), BF),
        ),
        in_specs=[VMEM] * 4,
        out_specs=(VMEM, VMEM),
        scratch_shapes=[pltpu.VMEM((1024, 128), F32), pltpu.VMEM((1024, 128), F32)],
        compiler_params=pltpu.CompilerParams(vmem_limit_bytes=LIMIT),
    )(projected, last_query, grad, last_grad)


def norm_forward(hidden, gain, offset):
    center = hidden - jnp.mean(hidden, axis=-1, keepdims=True)
    inverse = lax.rsqrt(jnp.mean(center * center, axis=-1, keepdims=True) + EPSILON)
    unit = center * inverse
    return unit * gain + offset, unit, inverse


def norm_backward(grad_rows, unit, inverse, gain):
    grad_unit = grad_rows * gain
    grad_in = inverse * (
        grad_unit
        - jnp.mean(grad_unit, axis=-1, keepdims=True)
        - unit * jnp.mean(grad_unit * unit, axis=-1, keepdims=True)
    )
    return grad_in, jnp.sum(grad_rows * unit, axis=0), jnp.sum(grad_rows, axis=0)


def gelu_pair(values):
    tangent = jnp.tanh(GELU_C * (values + 0.044715 * values * values * values))
    output = 0.5 * values * (1.0 + tangent)
    slope = 0.5 * (1.0 + tangent) + 0.5 * values * (1.0 - tangent * tangent) * GELU_C * (
        1.0 + 3.0 * 0.044715 * values * values
    )
    return output, slope


def layer_forward(hidden, w):
    normed, unit_one, inverse_one = norm_forward(hidden, w["gain_one"], w["bias_one"])
    normed = normed.astype(BF)
    normed_all, projected = team_gather(
        gather_qkv_kernel,
        0,
        normed,
        w["qkv"],
        w["qkv_bias"].reshape(1, 512),
        (jax.ShapeDtypeStruct((1024, 512), BF),),
    )
    normed_all = normed_all.reshape(1024, D)
    last_query = (dot(normed, w["last_query"]) + w["last_bias"]).astype(BF)
    heads, last = attend(projected, last_query)
    attended = heads_to_rows(heads.reshape(8, 128, 128), last)
    middle = hidden + dot(attended, w["out"]) + w["out_bias"]
    second, unit_two, inverse_two = norm_forward(middle, w["gain_two"], w["bias_two"])
    second_all, upper, activated = team_gather(
        gather_up_kernel,
        7,
        second.astype(BF),
        w["up"],
        w["up_bias"].reshape(1, 544),
        (jax.ShapeDtypeStruct((1024, 544), F32), jax.ShapeDtypeStruct((1024, 544), BF)),
    )
    second_all = second_all.reshape(1024, D)
    output = middle + product_scatter(dot, 5, activated, w["down"]) + w["down_bias"]
    saved = dict(
        normed=normed,
        normed_all=normed_all,
        unit_one=unit_one,
        inverse_one=inverse_one,
        projected=projected,
        last_query=last_query,
        attended=attended,
        unit_two=unit_two,
        inverse_two=inverse_two,
        second_all=second_all,
        upper=upper,
        activated=activated,
    )
    return output, saved


def layer_backward(grad_out, grad_low_all, w, kept, q):
    grad_low = grad_out.astype(BF)
    if grad_low_all is None:
        grad_low_all, up_grad = team_gather(
            gather_back_kernel,
            8,
            grad_low,
            w["down"],
            kept["upper"],
            (jax.ShapeDtypeStruct((1024, 544), BF),),
        )
        grad_low_all = grad_low_all.reshape(1024, D)
    else:
        slope = gelu_pair(kept["upper"])[1]
        up_grad = (dot_nt(grad_low_all, w["down"]) * slope).astype(BF)
    grad_second = product_scatter(dot_nt, 9, up_grad, w["up"])
    grad_in, gain_two, bias_two = norm_backward(
        grad_second, kept["unit_two"], kept["inverse_two"], w["gain_two"]
    )
    grad_middle = grad_out + grad_in
    middle_low = grad_middle.astype(BF)
    attended_grad = dot_nt(middle_low, w["out"]).astype(BF)
    heads_grad = rows_to_heads(attended_grad).reshape(1024, 128)
    qkv_grad, last_grad = attend_back(
        kept["projected"], kept["last_query"], heads_grad, attended_grad[:, 1024:]
    )
    grad_normed = product_scatter(dot_nt, 10, qkv_grad, w["qkv"])
    grad_normed = grad_normed + dot_nt(last_grad, w["last_query"])
    grad_in, gain_one, bias_one = norm_backward(
        grad_normed, kept["unit_one"], kept["inverse_one"], w["gain_one"]
    )
    grad_input = grad_middle + grad_in

    qkv_sums = jnp.sum(qkv_grad, axis=0, dtype=F32)
    last_sums = jnp.sum(last_grad, axis=0, dtype=F32)
    zeros = jnp.zeros((1024,), F32)
    qv = jnp.concatenate(
        [
            lax.dynamic_update_slice(zeros, qkv_sums[:128], (q * 128,)),
            last_sums[:64],
            lax.dynamic_update_slice(zeros, qkv_sums[256:384], (q * 128,)),
            qkv_sums[448:512],
        ]
    )
    up_sums = lax.dynamic_update_slice(
        jnp.zeros((FF,), F32), jnp.sum(up_grad, axis=0, dtype=F32), (q * 544,)
    )
    vectors = jnp.concatenate(
        [
            qv.reshape(8, 272),
            jnp.sum(middle_low, axis=0, dtype=F32).reshape(8, 136),
            gain_one.reshape(8, 136),
            bias_one.reshape(8, 136),
            gain_two.reshape(8, 136),
            bias_two.reshape(8, 136),
            up_sums.reshape(8, 544),
            jnp.sum(grad_low, axis=0, dtype=F32).reshape(8, 136),
        ],
        axis=1,
    )
    vectors = jnp.pad(vectors, ((0, 0), (0, 8 * 1280 - 1632))).reshape(8, 8, 1280)
    swapped_grad = jnp.concatenate([jnp.zeros((128, 64), BF), last_grad[:, :64]], axis=1)
    operands = (
        kept["attended"],
        jnp.pad(middle_low, ((0, 0), (0, 64))),
        kept["normed_all"],
        qkv_grad,
        kept["normed"],
        swapped_grad,
        vectors,
    )
    split = (
        kept["normed_all"],
        qkv_grad,
        kept["second_all"],
        up_grad,
        kept["activated"],
        grad_low_all,
    )
    return grad_input, operands, split


BOTH = ("section", "shard")


def pairs(route):
    out = []
    for c in range(2):
        for z in range(2):
            for x in range(4):
                tc, tz = route(c, z)
                out.append((c * 8 + z * 4 + x, tc * 8 + tz * 4 + x))
    return out


def local(
    inputs,
    cotangent,
    w_qkv,
    qv_bias,
    w_out,
    out_bias,
    gain_one,
    bias_one,
    gain_two,
    bias_two,
    w_up,
    up_bias,
    w_down,
    down_bias,
):
    c, z, x = place()
    q = c * 4 + x
    swap = [pair for pair in pairs(lambda a, b: (b, a)) if pair[0] != pair[1]]
    cross_back = pairs(lambda a, b: (b, 1 - a))

    def swapped(array):
        return jnp.where(c == z, array, lax.ppermute(array, BOTH, swap))

    def by_z(own, other):
        return jnp.where(z == 0, jnp.stack([own, other]), jnp.stack([other, own]))

    small = jnp.concatenate(
        [
            qv_bias[0],
            up_bias[0],
            out_bias[0],
            gain_one[0],
            bias_one[0],
            gain_two[0],
            bias_two[0],
            down_bias[0],
        ]
    )
    own_qkv = w_qkv[0]
    last_cols = [own_qkv[:, part * D + 1024 : (part + 1) * D] for part in range(3)]
    common = jnp.concatenate(
        [
            jnp.concatenate(
                [last_cols[1], last_cols[2], last_cols[0], jnp.zeros((136, 64), BF)], axis=1
            ),
            jnp.pad(small, (0, 2048 - 1632)).reshape(8, 256),
        ]
    )
    blocks = jnp.concatenate(
        [own_qkv[:, part * D : part * D + 1024].reshape(136, 8, 128) for part in range(3)]
        + [w_up[0].reshape(136, 8, 544)],
        axis=2,
    ).transpose(1, 0, 2)
    blocks = jnp.pad(blocks, ((0, 0), (0, 8), (0, 0)))
    replica = lax.axis_index("replica")
    late = lax.dynamic_slice(
        jnp.pad(blocks, ((0, 0), (0, 0), (0, 96))), (0, 0, replica * 128), (8, 144, 128)
    )
    first_blocks, late, all_common, hidden, top_grad = spread_weights(
        late, common, inputs[:, 0], cotangent[:, 0]
    )
    teams = [[a * 8 + b * 4 + d for a in range(2) for d in range(4)] for b in range(2)]
    top_grad_all = lax.all_gather(top_grad, BOTH, axis_index_groups=teams, axis=0, tiled=True)
    second_blocks = lax.all_gather(late, "replica", axis=0)
    own_out = lax.all_gather(w_out[0], "shard", axis=0, tiled=True)
    partner_out = lax.ppermute(own_out, "section", [(0, 1), (1, 0)])
    all_out = jnp.where(
        c == 0, jnp.stack([own_out, partner_out]), jnp.stack([partner_out, own_out])
    )
    cuts = (
        first_blocks.reshape(4, 2, 2, 4, 144, 128)
        .transpose(2, 3, 4, 0, 1, 5)[:, :, :136]
        .reshape(D, 1024)[:, :928],
        second_blocks.transpose(1, 2, 0, 3)[:, :136].reshape(D, 1024)[:, :928],
    )
    down_own = swapped(w_down[0])
    down_other = lax.ppermute(w_down[0], BOTH, cross_back)
    all_down = by_z(down_own, down_other)

    def layer_weights(layer):
        cut = cuts[layer]
        shared = all_common[layer, :, :136].reshape(D, 256)
        vec = all_common[layer, :, 136:].reshape(8, 2048)[:, :1632].astype(F32)

        def piece(start, size):
            return vec[:, start : start + size].reshape(-1)

        qv = piece(0, 272)
        six = vec[:, 816:].reshape(8, 6, 136).transpose(1, 0, 2).reshape(6, D)
        six = lax.optimization_barrier(six)
        none = jnp.zeros((128,), F32)
        qkv_bias = jnp.concatenate(
            [
                lax.dynamic_slice(qv, (q * 128,), (128,)),
                none,
                lax.dynamic_slice(qv, (D + q * 128,), (128,)),
                none[:64],
                qv[2 * D - 64 :],
            ]
        )
        out = all_out[layer]
        return dict(
            qkv=jnp.concatenate([cut[:, :384], shared[:, :128]], axis=1),
            last_query=shared[:, 128:],
            qkv_bias=qkv_bias,
            last_bias=jnp.concatenate([qv[1024:D], none[:64]]),
            out=jnp.concatenate([out[:1024], jnp.zeros((64, D), BF), out[1024:]]),
            out_bias=six[0:1],
            gain_one=six[1:2],
            bias_one=six[2:3],
            gain_two=six[3:4],
            bias_two=six[4:5],
            up=cut[:, 384:],
            up_bias=lax.dynamic_slice(piece(272, 544), (q * 544,), (544,)),
            down=all_down[layer],
            down_bias=six[5:6],
        )

    weights = [layer_weights(0), layer_weights(1)]
    hidden = hidden.astype(F32)
    top_grad = top_grad.astype(F32)
    out_first, kept_first = layer_forward(hidden, weights[0])
    out_second, kept_second = layer_forward(out_first.astype(BF).astype(F32), weights[1])
    grad_second, operands, split = layer_backward(
        top_grad, top_grad_all, weights[1], kept_second, q
    )
    rows = jnp.stack([out_first.astype(BF), out_second.astype(BF)])
    shared, section_out = shared_scatter(operands + (rows,), None)
    pieces = grad_pieces(*split, shared)
    grad_first, operands, split = layer_backward(
        grad_second.astype(BF).astype(F32), None, weights[0], kept_first, q
    )
    rows = jnp.stack([grad_first.astype(BF), grad_second.astype(BF)])
    shared, input_grad, second_layer = shared_scatter(operands + (rows,), pieces)
    pieces = grad_pieces(*split, shared)
    grad_qkv, grad_out_w, grad_up, grad_down, vectors = assemble(
        reduce_grads(pieces, second_layer)
    )
    section_out = section_out.astype(F32)[None, :, None]
    input_grad = input_grad.astype(F32)[None, :, None]
    vec = vectors.reshape(-1)
    grads = (
        grad_qkv,
        vec[:272],
        grad_out_w,
        vec[272:408],
        vec[408:544],
        vec[544:680],
        vec[680:816],
        vec[816:952],
        grad_up,
        vec[952:1496],
        grad_down,
        vec[1496:1632],
    )
    return (section_out, input_grad) + tuple(grad[None] for grad in grads)


def solution(mesh):
    return jax.shard_map(
        local,
        mesh=mesh,
        in_specs=(
            P(None, "replica", "shard", None),
            P(None, "replica", "shard", None),
            P("section", "shard", None),
            P("section", "shard"),
            P("section", "shard", None),
            P("section", "shard"),
            P("section", "shard"),
            P("section", "shard"),
            P("section", "shard"),
            P("section", "shard"),
            P("section", "shard", None),
            P("section", "shard"),
            P("section", "shard", None),
            P("section", "shard"),
        ),
        out_specs=(
            P("section", None, "replica", "shard", None),
            P("section", None, "replica", "shard", None),
            P("section", "shard", None),
            P("section", "shard"),
            P("section", "shard", None),
            P("section", "shard"),
            P("section", "shard"),
            P("section", "shard"),
            P("section", "shard"),
            P("section", "shard"),
            P("section", "shard", None),
            P("section", "shard"),
            P("section", "shard", None),
            P("section", "shard"),
        ),
        check_vma=False,
    )
```

```python
import functools

import jax
import jax.numpy as jnp
from jax import lax
from jax.experimental import pallas as pl
from jax.experimental.pallas import tpu as pltpu
from jax.sharding import PartitionSpec as P

D = 1088
FF = 4352
HEAD_DIM = 64
EPSILON = 1e-05
GELU_C = 0.7978845608028654
NEG_FILL = -1e30
BF = jnp.bfloat16
F32 = jnp.float32
MESH = pl.DeviceIdType.MESH
VMEM = pl.BlockSpec(memory_space=pltpu.VMEM)
LIMIT = 56 * 1024 * 1024


def place():
    c = lax.axis_index("section")
    j = lax.axis_index("shard")
    return c, j // 4, j % 4


def at(c, z, x):
    return {"section": c, "shard": z * 4 + x}


def arrive(devices):
    barrier = pltpu.get_barrier_semaphore()
    for device in devices:
        pl.semaphore_signal(barrier, inc=1, device_id=device, device_id_type=MESH)


def meet(devices):
    pl.semaphore_wait(pltpu.get_barrier_semaphore(), len(devices))


def greet(devices):
    arrive(devices)
    meet(devices)


def nothing():
    pass


ALONE = ([], nothing, nothing, nothing, nothing)


def sender(send_sems, recv_sems):
    def make(src, dst, index, device):
        copy = pltpu.make_async_remote_copy(
            src_ref=src,
            dst_ref=dst,
            send_sem=send_sems.at[index],
            recv_sem=recv_sems.at[index],
            device_id=device,
            device_id_type=MESH,
        )
        copy.start()
        return copy

    return make


def gather_core(own, out, send_sems, recv_sems, local_sem, use, beside=ALONE):
    c, z, x = place()
    ahead, behind, far = (x + 1) % 4, (x + 3) % 4, (x + 2) % 4
    partner, up, down = at(1 - c, z, x), at(c, z, ahead), at(c, z, behind)
    rows = own.shape[0]
    first, second = pl.ds(0, rows // 2), pl.ds(rows // 2, rows // 2)
    me, other = c * 4 + x, (1 - c) * 4
    local = pltpu.make_async_copy(own, out.at[me], local_sem)
    local.start()
    friends = [partner, up, down] + beside[0]
    arrive(friends)
    local.wait()
    meet(friends)
    send = sender(send_sems, recv_sems)
    to_up = send(own.at[first], out.at[me, first], 0, up)
    to_down = send(own.at[second], out.at[me, second], 1, down)
    to_partner = send(own, out.at[me], 2, partner)
    up_rest = send(own.at[second], out.at[me, second], 3, up)
    down_rest = send(own.at[first], out.at[me, first], 4, down)
    from_down, from_up, from_far = c * 4 + behind, c * 4 + ahead, c * 4 + far
    beside[1]()
    use(me)
    to_up.wait_recv()
    pass_up = send(out.at[from_down, first], out.at[from_down, first], 5, up)
    to_down.wait_recv()
    pass_down = send(out.at[from_up, second], out.at[from_up, second], 6, down)
    to_partner.wait_recv()
    use(other + x)
    up_rest.wait_recv()
    share_down = send(out.at[from_down], out.at[from_down], 7, partner)
    down_rest.wait_recv()
    share_up = send(out.at[from_up], out.at[from_up], 8, partner)
    use(from_down)
    use(from_up)
    beside[2]()
    pass_up.wait_recv()
    share_first = send(out.at[from_far, first], out.at[from_far, first], 9, partner)
    pass_down.wait_recv()
    share_second = send(out.at[from_far, second], out.at[from_far, second], 10, partner)
    use(from_far)
    beside[3]()
    share_down.wait_recv()
    use(other + behind)
    share_up.wait_recv()
    use(other + ahead)
    share_first.wait_recv()
    share_second.wait_recv()
    use(other + far)
    for copy in (
        to_up,
        to_down,
        to_partner,
        up_rest,
        down_rest,
        pass_up,
        pass_down,
        share_down,
        share_up,
        share_first,
        share_second,
    ):
        copy.wait_send()
    beside[4]()


def row_block(q):
    return pl.ds(pl.multiple_of(q * 128, 128), 128)


def gather_qkv_kernel(own, weight, bias, out, projected, send_sems, recv_sems, local_sem):
    def use(q):
        projected[row_block(q), :] = (dot(out[q], weight[...]) + bias[...]).astype(BF)

    gather_core(own, out, send_sems, recv_sems, local_sem, use)


def gather_up_kernel(own, weight, bias, out, upper, activated, send_sems, recv_sems, local_sem):
    def use(q):
        values = dot(out[q], weight[...]) + bias[...]
        upper[row_block(q), :] = values
        activated[row_block(q), :] = gelu_pair(values)[0].astype(BF)

    gather_core(own, out, send_sems, recv_sems, local_sem, use)


def gather_back_kernel(
    own, weight, upper, pieces, out, up_grad, out_pieces, send_sems, recv_sems, local_sem, *rings
):
    def use(q):
        slope = gelu_pair(upper[row_block(q), :])[1]
        up_grad[row_block(q), :] = (dot_nt(out[q], weight[...]) * slope).astype(BF)

    stages = []

    def begin():
        stages.extend(layer_rings(pieces, out_pieces, *rings))

    gather_core(
        own,
        out,
        send_sems,
        recv_sems,
        local_sem,
        use,
        (
            list(grid_place()[2]),
            begin,
            lambda: stages[0](),
            lambda: stages[1](),
            lambda: stages[2](),
        ),
    )


def team_gather(kernel, collective_id, own, weight, rest, results, scratch=()):
    rows, columns = own.shape
    return pl.pallas_call(
        kernel,
        out_shape=(jax.ShapeDtypeStruct((8, rows, columns), BF),) + results,
        in_specs=[VMEM] * (2 + len(rest)),
        out_specs=(VMEM,) * (1 + len(results)),
        scratch_shapes=[
            pltpu.SemaphoreType.DMA((11,)),
            pltpu.SemaphoreType.DMA((11,)),
            pltpu.SemaphoreType.DMA,
        ]
        + list(scratch),
        compiler_params=pltpu.CompilerParams(
            collective_id=collective_id, has_side_effects=True, vmem_limit_bytes=LIMIT
        ),
    )(own, weight, *rest)


def scatter_core(
    half,
    other_part,
    mine_part,
    prepare,
    beside,
    out,
    from_partner,
    far_sum,
    up_sum,
    down_sum,
    far_first,
    far_second,
    got_down,
    got_up,
    send_sems,
    recv_sems,
):
    c, z, x = place()
    ahead, behind, far = (x + 1) % 4, (x + 3) % 4, (x + 2) % 4
    partner, up, down = at(1 - c, z, x), at(c, z, ahead), at(c, z, behind)
    rows = out.shape[0]
    first, second = pl.ds(0, half), pl.ds(half, rows - half)
    send = sender(send_sems, recv_sems)
    friends = [partner, up, down] + beside[0]
    arrive(friends)
    order = (far, ahead, behind, x)
    parts = [other_part(where) for where in order]
    meet(friends)
    swaps = [
        send(part, from_partner.at[where], index, partner)
        for index, (where, part) in enumerate(zip(order, parts))
    ]
    beside[1]()
    for where in (far, ahead, behind, x):
        prepare(where)
    swap_far, swap_up, swap_down, swap_own = swaps

    def both(where, part):
        return mine_part(where, part) + from_partner[where, part, :].astype(F32)

    swap_far.wait_recv()
    far_sum[first, :] = both(far, first).astype(BF)
    far_up = send(far_sum.at[first], far_first, 4, up)
    far_sum[second, :] = both(far, second).astype(BF)
    far_down = send(far_sum.at[second], far_second, 5, down)
    swap_up.wait_recv()
    up_sum[second, :] = both(ahead, second).astype(BF)
    up_second = send(up_sum.at[second], got_down.at[second], 6, up)
    swap_down.wait_recv()
    down_sum[first, :] = both(behind, first).astype(BF)
    down_first = send(down_sum.at[first], got_up.at[first], 7, down)
    beside[2]()
    far_up.wait_recv()
    up_sum[first, :] = (both(ahead, first) + far_first[...].astype(F32)).astype(BF)
    up_first = send(up_sum.at[first], got_down.at[first], 8, up)
    far_down.wait_recv()
    down_sum[second, :] = (both(behind, second) + far_second[...].astype(F32)).astype(BF)
    down_second = send(down_sum.at[second], got_up.at[second], 9, down)
    swap_own.wait_recv()
    out[first, :] = both(x, first)
    out[second, :] = both(x, second)
    beside[3]()
    up_second.wait_recv()
    up_first.wait_recv()
    down_first.wait_recv()
    down_second.wait_recv()
    out[...] = out[...] + got_down[...].astype(F32) + got_up[...].astype(F32)
    for copy in (
        swap_far,
        swap_up,
        swap_down,
        swap_own,
        far_up,
        far_down,
        up_second,
        down_first,
        up_first,
        down_second,
    ):
        copy.wait_send()
    beside[4]()


def product_scatter_kernel(product, spreads, left, right, *refs):
    c, z, x = place()
    beside = ALONE
    if spreads:
        summed, out, got, other, mine, *refs = refs
        refs, spread_refs = refs[:10], refs[10:]
        beside = spread_beside(1, summed, got, spread_refs)
    else:
        out, other, mine, *refs = refs

    def other_part(where):
        rows = left[row_block((1 - c) * 4 + where), :]
        other[where] = product(rows, right[...]).astype(BF)
        return other.at[where]

    def prepare(where):
        mine[where] = product(left[row_block(c * 4 + where), :], right[...])

    scatter_core(
        64, other_part, lambda where, part: mine[where, part, :], prepare, beside, out, *refs
    )


def scatter_scratch(rows, columns, half):
    block = pltpu.VMEM((rows, columns), BF)
    return [
        pltpu.VMEM((4, rows, columns), BF),
        block,
        block,
        block,
        pltpu.VMEM((half, columns), BF),
        pltpu.VMEM((rows - half, columns), BF),
        block,
        block,
        pltpu.SemaphoreType.DMA((10,)),
        pltpu.SemaphoreType.DMA((10,)),
    ]


def product_scatter(product, collective_id, left, right, summed=None):
    spreads = summed is not None
    out_shape = (jax.ShapeDtypeStruct((128, D), F32),)
    operands = (left, right)
    if spreads:
        out_shape += (jax.ShapeDtypeStruct((8, GOT_ROWS, 128), BF),)
        operands += (summed,)
    out = pl.pallas_call(
        functools.partial(product_scatter_kernel, product, spreads),
        out_shape=out_shape,
        in_specs=[VMEM] * len(operands),
        out_specs=(VMEM,) * len(out_shape),
        scratch_shapes=[pltpu.VMEM((4, 128, D), BF), pltpu.VMEM((4, 128, D), F32)]
        + scatter_scratch(128, D, 64)
        + (spread_scratch() if spreads else []),
        compiler_params=pltpu.CompilerParams(
            collective_id=collective_id, has_side_effects=True, vmem_limit_bytes=LIMIT
        ),
    )(*operands)
    return out if spreads else out[0]


TEAM_STEPS = tuple((dc, dx) for dc in range(2) for dx in range(4) if dc or dx)


def ring_spread(send, base, source, block, me, up, down, first, second):
    before, after = (me + 3) % 4, (me + 1) % 4
    copies = [
        send(source(first), block(me, first), base, up),
        send(source(second), block(me, second), base + 1, down),
        send(source(second), block(me, second), base + 2, up),
        send(source(first), block(me, first), base + 3, down),
    ]

    def middle():
        copies[0].wait_recv()
        copies.append(send(block(before, first), block(before, first), base + 4, up))
        copies[1].wait_recv()
        copies.append(send(block(after, second), block(after, second), base + 5, down))

    def last():
        for copy in copies[2:]:
            copy.wait_recv()

    return copies, middle, last


def weights_kernel(
    late,
    common,
    rows,
    other_rows,
    first,
    second,
    out_common,
    out_rows,
    out_other,
    send_sems,
    recv_sems,
    common_send,
    common_recv,
    share_send,
    share_recv,
    ring_send,
    ring_recv,
    swap_send,
    swap_recv,
    local_sems,
):
    c, z, x = place()
    r = lax.axis_index("replica")
    y, zh = r // 2, r % 2
    zf = zh * 2 + z
    slot = z * 4 + x

    def device(ty, tz):
        return {"section": c, "shard": (tz % 2) * 4 + x, "replica": ty * 2 + tz // 2}

    y_up, y_down = device((y + 1) % 4, zf), device((y + 3) % 4, zf)
    z_up, z_down = device(y, (zf + 1) % 4), device(y, (zf + 3) % 4)
    z_other = device(y, (zf + 3 + 2 * z) % 4)
    partner, diagonal, z_pair = at(1 - c, z, x), at(1 - c, 1 - z, x), at(c, 1 - z, x)
    team = [((c + dc) % 2, (x + dx) % 4) for dc, dx in TEAM_STEPS]
    core_steps = [(dz, dx) for dx in (1, 3, 2, 0) for dz in range(2) if dz or dx]
    core = [((z + dz) % 2, (x + dx) % 4) for dz, dx in core_steps]
    source_of = [core_steps.index((dz, (4 - dx) % 4)) for dz, dx in core_steps]
    greet(
        [at(tc, z, tx) for tc, tx in team]
        + [at(c, 1 - z, (x + dx) % 4) for dx in range(4)]
        + [diagonal, y_up, y_down, z_other]
    )

    def remote(src, dst, sends, recvs, index, target):
        return pltpu.make_async_remote_copy(
            src_ref=src,
            dst_ref=dst,
            send_sem=sends.at[index],
            recv_sem=recvs.at[index],
            device_id=target,
            device_id_type=MESH,
        )

    def to_team(index, layer):
        tc, tx = team[index]
        place_at = first.at[y, zf, x] if layer == 0 else second.at[slot]
        return remote(late.at[tc * 4 + tx], place_at, send_sems, recv_sems, index, at(tc, z, tx))

    def swapped(index):
        src, dst = ((rows, out_rows), (other_rows, out_other))[index]
        return remote(src.at[c], dst, swap_send, swap_recv, index, diagonal)

    def kept(index):
        src, dst = ((rows, out_rows), (other_rows, out_other))[index]
        return pltpu.make_async_copy(src.at[c], dst, local_sems.at[2 + index])

    def common_to(index):
        tz, tx = core[index]
        return remote(
            common, out_common.at[c, slot], common_send, common_recv, index, at(c, tz, tx)
        )

    def shared(index):
        if index == 7:
            source = out_common.at[c, slot]
        else:
            tz, tx = core[index]
            source = out_common.at[c, tz * 4 + tx]
        return remote(source, source, share_send, share_recv, index, partner)

    keep = pltpu.make_async_copy(common, out_common.at[c, slot], local_sems.at[0])
    keep.start()

    @pl.when(c == 0)
    def _():
        for index in range(7):
            to_team(index, 0).start()
        pltpu.make_async_copy(late.at[c * 4 + x], first.at[y, zf, x], local_sems.at[1]).start()

    @pl.when(c == 1)
    def _():
        for index in range(7):
            to_team(index, 1).start()
        pltpu.make_async_copy(late.at[c * 4 + x], second.at[slot], local_sems.at[1]).start()

    for index in range(7):
        common_to(index).start()

    @pl.when(c == z)
    def _():
        kept(0).start()
        kept(1).start()

    @pl.when(c != z)
    def _():
        swapped(0).start()
        swapped(1).start()

    for index, (dc, dx) in enumerate(TEAM_STEPS):

        @pl.when((c + dc) % 2 == 0)
        def _():
            to_team(index, 0).wait_recv()

        @pl.when((c + dc) % 2 == 1)
        def _():
            to_team(index, 1).wait_recv()

    @pl.when(c == 0)
    def _():
        pltpu.make_async_copy(late.at[c * 4 + x], first.at[y, zf, x], local_sems.at[1]).wait()

    @pl.when(c == 1)
    def _():
        pltpu.make_async_copy(late.at[c * 4 + x], second.at[slot], local_sems.at[1]).wait()

    def send(src, dst, index, target):
        copy = remote(src, dst, ring_send, ring_recv, index, target)
        copy.start()
        return copy

    one, two = pl.ds(0, 1), pl.ds(1, 1)
    three, four = pl.ds(2, 1), pl.ds(3, 1)
    left, right = pl.ds(0, 2), pl.ds(2, 2)
    y_copies, y_middle, y_last = ring_spread(
        send,
        0,
        lambda part: first.at[y, zf, part],
        lambda i, part: first.at[i, zf, part],
        y,
        y_up,
        y_down,
        one,
        two,
    )
    z_copies, z_middle, z_last = ring_spread(
        send,
        6,
        lambda part: first.at[y, zf, part],
        lambda i, part: first.at[y, i, part],
        zf,
        z_up,
        z_down,
        three,
        four,
    )
    pair_copy = send(second.at[pl.ds(z * 4, 4)], second.at[pl.ds(z * 4, 4)], 24, z_pair)
    keep.wait()
    shared(7).start()
    for index in range(7):
        common_to(source_of[index]).wait_recv()
        shared(index).start()
    y_middle()
    z_middle()
    y_last()
    more_z, z_middle_too, z_last_too = ring_spread(
        send,
        12,
        lambda part: first.at[part, zf, pl.ds(0, 2)],
        lambda i, part: first.at[part, i, pl.ds(0, 2)],
        zf,
        z_up,
        z_down,
        left,
        right,
    )
    z_last()
    more_y, y_middle_too, y_last_too = ring_spread(
        send,
        18,
        lambda part: first.at[y, part, pl.ds(2, 2)],
        lambda i, part: first.at[i, part, pl.ds(2, 2)],
        y,
        y_up,
        y_down,
        left,
        right,
    )
    z_middle_too()
    y_middle_too()
    pair_copy.wait_recv()
    for index in range(8):
        shared(index).wait_recv()
    z_last_too()
    y_last_too()

    @pl.when(c == z)
    def _():
        kept(0).wait()
        kept(1).wait()

    @pl.when(c != z)
    def _():
        for index in range(2):
            swapped(index).wait_recv()
            swapped(index).wait_send()

    @pl.when(c == 0)
    def _():
        for index in range(7):
            to_team(index, 0).wait_send()

    @pl.when(c == 1)
    def _():
        for index in range(7):
            to_team(index, 1).wait_send()

    for index in range(7):
        common_to(index).wait_send()
    for index in range(8):
        shared(index).wait_send()
    for copy in y_copies + z_copies + more_z + more_y + [pair_copy]:
        copy.wait_send()


def spread_weights(late, common, rows, other_rows):
    dma = pltpu.SemaphoreType.DMA
    return pl.pallas_call(
        weights_kernel,
        out_shape=(
            jax.ShapeDtypeStruct((4, 4, 4, 144, 128), BF),
            jax.ShapeDtypeStruct(late.shape, BF),
            jax.ShapeDtypeStruct((2, 8) + common.shape, BF),
            jax.ShapeDtypeStruct(rows.shape[1:], BF),
            jax.ShapeDtypeStruct(rows.shape[1:], BF),
        ),
        in_specs=[VMEM] * 4,
        out_specs=(VMEM,) * 5,
        scratch_shapes=[
            dma((7,)),
            dma((7,)),
            dma((7,)),
            dma((7,)),
            dma((8,)),
            dma((8,)),
            dma((25,)),
            dma((25,)),
            dma((2,)),
            dma((2,)),
            dma((4,)),
        ],
        compiler_params=pltpu.CompilerParams(
            collective_id=3, has_side_effects=True, vmem_limit_bytes=LIMIT
        ),
    )(late, common, rows, other_rows)


SPLIT_ROWS = 4 * 144
DOWN_ROWS = 320
SHARED_ROWS = 96
ROWS = SPLIT_ROWS + DOWN_ROWS + SHARED_ROWS
OWN_ROWS = DOWN_ROWS + SHARED_ROWS
GOT_ROWS = 8 * 144 + 2 * OWN_ROWS


def widen(block):
    return block.astype(F32)


def ring_reduce(send, base, block, me, up, down, first, second, far, relay, got, result):
    after, before, opposite = (me + 1) % 4, (me + 3) % 4, (me + 2) % 4
    copies = [
        send(block(opposite, first), far[0], base, up),
        send(block(opposite, second), far[1], base + 1, down),
        send(block(after, second), got[0].at[second], base + 2, up),
        send(block(before, first), got[1].at[first], base + 3, down),
    ]

    def middle():
        copies[0].wait_recv()
        relay[0][...] = (widen(block(after, first)[...]) + widen(far[0][...])).astype(BF)
        copies.append(send(relay[0], got[0].at[first], base + 4, up))
        copies[1].wait_recv()
        relay[1][...] = (widen(block(before, second)[...]) + widen(far[1][...])).astype(BF)
        copies.append(send(relay[1], got[1].at[second], base + 5, down))

    def last():
        for copy in copies[2:]:
            copy.wait_recv()
        for part in (first, second):
            value = (
                widen(block(me, part)[...])
                + widen(got[0].at[part][...])
                + widen(got[1].at[part][...])
            )
            result.at[part][...] = value.astype(BF)
        for copy in copies:
            copy.wait_send()

    return middle, last


TOP = ROWS // 2
CUT = TOP // 32 * 16


def rings_scratch():
    dma = pltpu.SemaphoreType.DMA
    return [
        pltpu.VMEM((2, 4, TOP, 128), BF),
        pltpu.VMEM((2, 2, 2, TOP, 128), BF),
        pltpu.VMEM((2, 2, 2, TOP, 128), BF),
        pltpu.VMEM((2, 2, 4, TOP, 128), BF),
        pltpu.VMEM((2, 2, TOP - CUT, 128), BF),
        pltpu.VMEM((2, 2, TOP - CUT, 128), BF),
        pltpu.VMEM((2, 2, TOP, 128), BF),
        dma((24,)),
        dma((24,)),
    ]


def grid_place():
    c, z, x = place()
    r = lax.axis_index("replica")
    y, zh = r // 2, r % 2
    zf = zh * 2 + z

    def device(ty, tz):
        return {"section": c, "shard": (tz % 2) * 4 + x, "replica": ty * 2 + tz // 2}

    return (
        y,
        zf,
        (
            device((y + 1) % 4, zf),
            device((y + 3) % 4, zf),
            device(y, (zf + 1) % 4),
            device(y, (zf + 3) % 4),
        ),
    )


def layer_rings(pieces, out, wide_sum, far, relay, got, far_s, relay_s, got_s, sends, recvs):
    y, zf, (y_up, y_down, z_up, z_down) = grid_place()

    def send(src, dst, index, target):
        copy = pltpu.make_async_remote_copy(
            src_ref=src,
            dst_ref=dst,
            send_sem=sends.at[index],
            recv_sem=recvs.at[index],
            device_id=target,
            device_id_type=MESH,
        )
        copy.start()
        return copy

    low, high = pl.ds(0, 2), pl.ds(2, 2)
    top, bottom = pl.ds(0, TOP), pl.ds(TOP, TOP)
    first, second = pl.ds(0, CUT), pl.ds(CUT, TOP - CUT)

    def wide(k):
        return (
            [far.at[k, 0], far.at[k, 1]],
            [relay.at[k, 0], relay.at[k, 1]],
            [got.at[k, 0], got.at[k, 1]],
            wide_sum.at[k],
        )

    def small(k, result):
        parts = pl.ds(0, CUT), pl.ds(0, TOP - CUT)
        return (
            [far_s.at[k, 0, parts[0]], far_s.at[k, 1, parts[1]]],
            [relay_s.at[k, 0, parts[0]], relay_s.at[k, 1, parts[1]]],
            [got_s.at[k, 0], got_s.at[k, 1]],
            result,
        )

    y_mid, y_last = ring_reduce(
        send,
        0,
        lambda i, part: pieces.at[i, part, top],
        y,
        y_up,
        y_down,
        low,
        high,
        *wide(0),
    )
    z_mid, z_last = ring_reduce(
        send,
        6,
        lambda i, part: pieces.at[part, i, bottom],
        zf,
        z_up,
        z_down,
        low,
        high,
        *wide(1),
    )
    later = []

    def turn():
        y_last()
        later.append(
            ring_reduce(
                send,
                12,
                lambda i, part: wide_sum.at[0, i, part],
                zf,
                z_up,
                z_down,
                first,
                second,
                *small(0, out.at[top]),
            )
        )
        z_last()
        later.append(
            ring_reduce(
                send,
                18,
                lambda i, part: wide_sum.at[1, i, part],
                y,
                y_up,
                y_down,
                first,
                second,
                *small(1, out.at[bottom]),
            )
        )

    def middle():
        y_mid()
        z_mid()

    def finish():
        for mid, _ in later:
            mid()
        for _, last in later:
            last()

    return middle, turn, finish


def spread_scratch():
    dma = pltpu.SemaphoreType.DMA
    return [pltpu.VMEM((GOT_ROWS, 128), BF), dma((9,)), dma((10,)), dma((3,)), dma((13,)), dma((13,))]


def spread_stages(layer, summed, out, own, home_send, home_recv, local_sems, sends, recvs):
    c, z, x = place()
    r = lax.axis_index("replica")
    y, zh = r // 2, r % 2
    zf, (y_up, y_down, _, _) = grid_place()[1:]
    across = {"section": c, "shard": z * 4 + x, "replica": y * 2 + 1 - zh}
    me = c * 4 + x
    mine = pl.ds(pl.multiple_of(me * 144, 16), 144)
    holds = c == layer
    other = c != layer
    stays = jnp.logical_and(holds, z == layer)
    leaves = jnp.logical_or(other, z != layer)

    def copy(src, dst, send_sem, recv_sem, target):
        return pltpu.make_async_remote_copy(
            src_ref=src,
            dst_ref=dst,
            send_sem=send_sem,
            recv_sem=recv_sem,
            device_id=target,
            device_id_type=MESH,
        )

    def split_part(tx):
        return summed.at[pl.ds(pl.multiple_of(tx * 144, 16), 144)]

    def to_row(dx, base):
        tx = (x + dx) % 4
        return copy(
            split_part(tx),
            own.at[mine],
            home_send.at[base + dx],
            home_recv.at[base + dx],
            at(layer, z, tx),
        )

    def split_here():
        return pltpu.make_async_copy(split_part(x), own.at[mine], local_sems.at[0])

    own_part = pl.ds(SPLIT_ROWS, OWN_ROWS)
    slot = pl.ds(pl.multiple_of(8 * 144 + z * OWN_ROWS, 16), OWN_ROWS)

    def to_owner(t):
        return copy(
            summed.at[own_part],
            own.at[slot],
            home_send.at[8],
            home_recv.at[8 + t],
            at(layer, c, x),
        )

    def from_row(dx):
        return copy(
            split_part(x),
            own.at[mine],
            home_send.at[4 + dx],
            home_recv.at[4 + dx],
            at(1 - c, z, x),
        )

    def from_owner(t):
        return copy(
            summed.at[own_part],
            own.at[slot],
            home_send.at[8],
            home_recv.at[8 + t],
            at(1 - c, z, x),
        )

    def own_here():
        return pltpu.make_async_copy(summed.at[own_part], own.at[slot], local_sems.at[1])

    def home():
        @pl.when(holds)
        def _():
            split_here().start()
            for dx in (1, 2, 3):
                to_row(dx, 0).start()

        @pl.when(other)
        def _():
            for dx in range(4):
                to_row(dx, 4).start()

        @pl.when(stays)
        def _():
            own_here().start()

        @pl.when(leaves)
        def _():
            to_owner(z).start()

    here, there = y * 2 + zh, y * 2 + 1 - zh
    front, back = pl.ds(0, GOT_ROWS // 2), pl.ds(GOT_ROWS // 2, GOT_ROWS // 2)

    def step(index, source, place_at, target):
        return copy(source, place_at, sends.at[index], recvs.at[index], target)

    def over():
        return step(0, own, out.at[here], across)

    def kept():
        return pltpu.make_async_copy(own, out.at[here], local_sems.at[2])

    def ring(base, source, block):
        def item(i):
            part = (front, back, back, front)[i]
            target = (y_up, y_down, y_up, y_down)[i]
            return step(base + i, source.at[part], out.at[block, part], target)

        return item

    def relays(base, which):
        below, above = ((y + 3) % 4) * 2 + which, ((y + 1) % 4) * 2 + which

        def item(i):
            place_at = (out.at[below, front], out.at[above, back])[i]
            return step(base + 4 + i, place_at, place_at, (y_up, y_down)[i])

        return item

    def first_ring():
        return ring(1, own, here)

    def second_ring():
        return ring(7, out.at[there], there)

    def arrived():
        @pl.when(holds)
        def _():
            split_here().wait()
            for dx in (1, 2, 3):
                to_row(dx, 0).wait_recv()
            for dx in range(4):
                from_row(dx).wait_recv()

            @pl.when(z == layer)
            def _():
                own_here().wait()
                from_owner(1 - layer).wait_recv()

            @pl.when(z != layer)
            def _():
                from_owner(0).wait_recv()
                from_owner(1).wait_recv()

            kept().start()
            over().start()
            for i in range(4):
                first_ring()(i).start()

    def pass_first():
        @pl.when(holds)
        def _():
            for i in range(2):
                first_ring()(i).wait_recv()
                relays(1, zh)(i).start()
            over().wait_recv()
            for i in range(4):
                second_ring()(i).start()

    def pass_second():
        @pl.when(holds)
        def _():
            for i in range(2):
                second_ring()(i).wait_recv()
                relays(7, 1 - zh)(i).start()

    def end():
        @pl.when(holds)
        def _():
            rounds = ((first_ring(), relays(1, zh)), (second_ring(), relays(7, 1 - zh)))
            for direct, relayed in rounds:
                for i in (2, 3):
                    direct(i).wait_recv()
                for i in range(2):
                    relayed(i).wait_recv()
            over().wait_send()
            for direct, relayed in rounds:
                for i in range(4):
                    direct(i).wait_send()
                for i in range(2):
                    relayed(i).wait_send()
            kept().wait()
            for dx in (1, 2, 3):
                to_row(dx, 0).wait_send()

        @pl.when(other)
        def _():
            for dx in range(4):
                to_row(dx, 4).wait_send()

        @pl.when(leaves)
        def _():
            to_owner(z).wait_send()

    return home, arrived, pass_first, pass_second, end


def spread_beside(layer, summed, out, refs):
    c, z, x = place()
    r = lax.axis_index("replica")
    y_up, y_down, _, _ = grid_place()[2]
    across = {"section": c, "shard": z * 4 + x, "replica": (r // 2) * 2 + 1 - r % 2}
    friends = [at(c, z, (x + 2) % 4)] + [at(1 - c, z, (x + dx) % 4) for dx in (1, 2, 3)]
    friends += [at(c, 1 - z, x), at(1 - c, 1 - z, x), y_up, y_down, across]
    home, arrived, pass_first, pass_second, end = spread_stages(layer, summed, out, *refs)

    def finish():
        pass_second()
        end()

    return friends, home, arrived, pass_first, finish


def reduce_kernel(pieces, out, summed, *refs):
    c, z, x = place()
    r = lax.axis_index("replica")
    across = {"section": c, "shard": z * 4 + x, "replica": (r // 2) * 2 + 1 - r % 2}
    greet(list(grid_place()[2]) + [across, at(1 - c, 1 - z, x)] + team_mates())
    spread_refs, ring_refs = refs[:6], refs[6:]
    middle, turn, finish = layer_rings(pieces, summed, *ring_refs)
    middle()
    turn()
    finish()
    for stage in spread_stages(0, summed, out, *spread_refs):
        stage()


def reduce_grads(pieces):
    return pl.pallas_call(
        reduce_kernel,
        out_shape=jax.ShapeDtypeStruct((8, GOT_ROWS, 128), BF),
        in_specs=[VMEM],
        out_specs=VMEM,
        scratch_shapes=[pltpu.VMEM((ROWS, 128), BF)] + spread_scratch() + rings_scratch(),
        compiler_params=pltpu.CompilerParams(
            collective_id=4, has_side_effects=True, vmem_limit_bytes=LIMIT
        ),
    )(pieces)


def shared_kernel(*refs):
    attended, middle_low, normed_all, qkv_grad, normed, last_grad, vectors, rows = refs[:8]
    refs = refs[8:]
    out, out_rows, products, last_keys, last_queries, parts, *refs = refs
    home_send, home_recv, home_local, *scatter_refs = refs
    c, z, x = place()
    products[...] = dot_tn(attended[...], middle_low[...])
    last_keys[...] = dot_tn(normed_all[...], qkv_grad[:, 384:512])
    last_queries[...] = dot_tn(normed[...], last_grad[...])
    for j in range(8):
        block = pl.ds(136 * j, 136)

        def stack(value, lanes):
            tail = vectors[j, :, lanes]
            return jnp.concatenate([value, tail], axis=0).astype(BF)

        if j < 7:
            product = products[block, :]
        else:
            product = jnp.concatenate(
                [products[952:1024, :], products[1088:1152, :]], axis=0
            )
        parts[j, :, 0:128] = stack(last_keys[block, :], pl.ds(0, 128))
        parts[j, :, 128:1152] = stack(product[:, 0:1024], pl.ds(128, 1024))
        parts[j, :, 1152:1280] = stack(
            product[:, 1024:1152] + last_queries[block, :], pl.ds(1152, 128)
        )

    def same_layer():
        return pltpu.make_async_remote_copy(
            src_ref=rows.at[c],
            dst_ref=out_rows.at[z],
            send_sem=home_send.at[0],
            recv_sem=home_recv.at[0],
            device_id=at(c, 1 - z, x),
            device_id_type=MESH,
        )

    def same_here():
        return pltpu.make_async_copy(rows.at[c], out_rows.at[z], home_local)

    def other_layer(t):
        return pltpu.make_async_remote_copy(
            src_ref=rows.at[1 - c],
            dst_ref=out_rows.at[z],
            send_sem=home_send.at[1],
            recv_sem=home_recv.at[1 + t],
            device_id=at(1 - c, c, x),
            device_id_type=MESH,
        )

    def begin():
        @pl.when(z == c)
        def _():
            same_here().start()

        @pl.when(z != c)
        def _():
            same_layer().start()

        other_layer(z).start()

    def end():
        @pl.when(z == c)
        def _():
            same_here().wait()
            same_layer().wait_recv()

        @pl.when(z != c)
        def _():
            other_layer(0).wait_recv()
            other_layer(1).wait_recv()
            same_layer().wait_send()

        other_layer(z).wait_send()

    friends = [at(c, 1 - z, x), at(1 - c, 1 - z, x)]
    def mine_part(where, part):
        return parts[c * 4 + where, part, :].astype(F32)

    scatter_core(
        64,
        lambda where: parts.at[(1 - c) * 4 + where],
        mine_part,
        lambda where: None,
        (friends, begin, nothing, nothing, end),
        out,
        *scatter_refs,
    )


def shared_scatter(*operands):
    dma = pltpu.SemaphoreType.DMA
    return pl.pallas_call(
        shared_kernel,
        out_shape=(
            jax.ShapeDtypeStruct((144, 1280), F32),
            jax.ShapeDtypeStruct((2, 128, D), BF),
        ),
        in_specs=[VMEM] * 8,
        out_specs=(VMEM, VMEM),
        scratch_shapes=[
            pltpu.VMEM((1152, 1152), F32),
            pltpu.VMEM((D, 128), F32),
            pltpu.VMEM((D, 128), F32),
            pltpu.VMEM((8, 144, 1280), BF),
            dma((2,)),
            dma((3,)),
            dma,
        ]
        + scatter_scratch(144, 1280, 64),
        compiler_params=pltpu.CompilerParams(
            collective_id=6, has_side_effects=True, vmem_limit_bytes=LIMIT
        ),
    )(*operands)


def segments(start, size, piece_rows):
    done = 0
    while done < size:
        piece, row = divmod(start + done, piece_rows)
        count = min(piece_rows - row, size - done)
        yield piece, row, done, count
        done += count


def pieces_kernel(
    normed_all, qkv_grad, second_all, up_grad, activated, low_all, shared, out, wide, tall
):
    wide[:, 896:1024] = jnp.zeros((D, 128), F32)
    wide[:, 0:384] = dot_tn(normed_all[...], qkv_grad[:, 0:384])
    wide[:, 384:928] = dot_tn(second_all[...], up_grad[...])
    blank = jnp.zeros((8, 128), F32)
    for chunk in range(8):
        for j in range(8):
            block = wide[136 * j : 136 * j + 136, 128 * chunk : 128 * chunk + 128]
            place_at = pl.ds((j % 4) * 144, 144)
            out[chunk // 2, (chunk % 2) * 2 + j // 4, place_at, :] = jnp.concatenate(
                [block, blank], axis=0
            ).astype(BF)
    tall[:, 1024:1152] = jnp.zeros((544, 128), F32)
    tall[:, 0:D] = dot_tn(activated[...], low_all[...])

    def put(base, piece_rows, start, value):
        for piece, row, at_row, count in segments(start, value.shape[0], piece_rows):
            out[piece // 4, piece % 4, base + row : base + row + count, :] = value[
                at_row : at_row + count
            ].astype(BF)

    for k in range(9):
        put(SPLIT_ROWS, DOWN_ROWS, 544 * k, tall[:, 128 * k : 128 * k + 128])
    put(SPLIT_ROWS, DOWN_ROWS, 9 * 544, jnp.zeros((16 * DOWN_ROWS - 9 * 544, 128), F32))
    base = SPLIT_ROWS + DOWN_ROWS
    for k in range(10):
        put(base, SHARED_ROWS, 144 * k, shared[:, 128 * k : 128 * k + 128])
    put(base, SHARED_ROWS, 1440, jnp.zeros((16 * SHARED_ROWS - 1440, 128), F32))


def grad_pieces(*operands):
    return pl.pallas_call(
        pieces_kernel,
        out_shape=jax.ShapeDtypeStruct((4, 4, ROWS, 128), BF),
        in_specs=[VMEM] * 7,
        out_specs=VMEM,
        scratch_shapes=[pltpu.VMEM((D, 1024), F32), pltpu.VMEM((544, 1152), F32)],
        compiler_params=pltpu.CompilerParams(vmem_limit_bytes=LIMIT),
    )(*operands)


def assemble_kernel(
    first_got, second_got, qkv, out_w, up, down, vectors, shared, got, got_sem
):
    c = lax.axis_index("section")

    @pl.when(c == 0)
    def _():
        pltpu.make_async_copy(first_got, got, got_sem).start()

    @pl.when(c == 1)
    def _():
        pltpu.make_async_copy(second_got, got, got_sem).start()

    @pl.when(c == 0)
    def _():
        pltpu.make_async_copy(first_got, got, got_sem).wait()

    @pl.when(c == 1)
    def _():
        pltpu.make_async_copy(second_got, got, got_sem).wait()

    for q in range(8):
        for chunk in range(8):
            block = got[chunk, 144 * q : 144 * q + 144, :].astype(F32)[:136]
            if chunk < 3:
                start = chunk * D + 128 * q
                qkv[:, start : start + 128] = block
            elif chunk < 7:
                start = 544 * q + 128 * (chunk - 3)
                up[:, start : start + 128] = block
            else:
                up[:, 544 * q + 512 : 544 * q + 544] = block[:, :32]
    for k in range(9):
        width = 128 if k < 8 else 64
        for piece, row, at_row, count in segments(544 * k, 544, DOWN_ROWS):
            start = 8 * 144 + (piece % 2) * OWN_ROWS + row
            block = got[piece // 2, start : start + count, :].astype(F32)
            down[at_row : at_row + count, 128 * k : 128 * k + width] = block[:, :width]
    for k in range(10):
        for piece, row, at_row, count in segments(144 * k, 144, SHARED_ROWS):
            start = 8 * 144 + (piece % 2) * OWN_ROWS + DOWN_ROWS + row
            block = got[piece // 2, start : start + count, :].astype(F32)
            shared[k, at_row : at_row + count, :] = block
        vectors[:, 128 * k : 128 * k + 128] = shared[k, 136:144, :]
        if 1 <= k < 9:
            out_w[:, 128 * (k - 1) : 128 * k] = shared[k, 0:136, :]
    out_w[:, 1024:D] = shared[9, 0:136, 0:64]
    qkv[:, 1024:D] = shared[9, 0:136, 64:128]
    qkv[:, D + 1024 : 2 * D] = shared[0, 0:136, 0:64]
    qkv[:, 2 * D + 1024 : 3 * D] = shared[0, 0:136, 64:128]


def assemble(first_got, second_got):
    shapes = ((136, 3 * D), (136, D), (136, FF), (544, D), (8, 1280))
    return pl.pallas_call(
        assemble_kernel,
        out_shape=tuple(jax.ShapeDtypeStruct(shape, F32) for shape in shapes),
        in_specs=[pl.BlockSpec(memory_space=pl.ANY)] * 2,
        out_specs=(VMEM,) * 5,
        scratch_shapes=[
            pltpu.VMEM((10, 144, 128), F32),
            pltpu.VMEM((8, GOT_ROWS, 128), BF),
            pltpu.SemaphoreType.DMA,
        ],
        compiler_params=pltpu.CompilerParams(vmem_limit_bytes=LIMIT),
    )(first_got, second_got)


def dot_nt(left, right):
    return lax.dot_general(left, right, (((1,), (1,)), ((), ())), preferred_element_type=F32)


def dot_tn(left, right):
    return lax.dot_general(left, right, (((0,), (0,)), ((), ())), preferred_element_type=F32)


def dot(left, right):
    return jnp.dot(left, right, preferred_element_type=F32)


def lane_half(block, which):
    lane = lax.broadcasted_iota(jnp.int32, block.shape, 1)
    keep = lane < 64 if which == 0 else lane >= 64
    return jnp.where(keep, block, jnp.zeros_like(block))


def softmax_rows(scores, start):
    row = lax.broadcasted_iota(jnp.int32, scores.shape, 0) + start
    key = lax.broadcasted_iota(jnp.int32, scores.shape, 1)
    masked = jnp.where(key <= row, scores, NEG_FILL)
    shifted = jnp.exp(masked - jnp.max(masked, axis=1, keepdims=True))
    return shifted * (1.0 / jnp.sum(shifted, axis=1, keepdims=True))


STEP = 256


def team_mates():
    c, z, x = place()
    return [at((c + dc) % 2, z, (x + dx) % 4) for dc, dx in TEAM_STEPS]


def lanes_of(q):
    return pl.ds(pl.multiple_of(q * 128, 128), 128)


def attend_kernel(projected, last_query, out, attended, send_sems, recv_sems, local_sem):
    c, z, x = place()
    me = c * 4 + x
    mates = team_mates()
    arrive(mates)

    def copy_to(q):
        return pltpu.make_async_remote_copy(
            src_ref=attended.at[q],
            dst_ref=out.at[:, lanes_of(me)],
            send_sem=send_sems.at[q],
            recv_sem=recv_sems.at[me],
            device_id=at(q // 4, z, q % 4),
            device_id_type=MESH,
        )

    def copy_from(q):
        return pltpu.make_async_remote_copy(
            src_ref=attended.at[q],
            dst_ref=out.at[:, lanes_of(q)],
            send_sem=send_sems.at[q],
            recv_sem=recv_sems.at[q],
            device_id=at(q // 4, z, q % 4),
            device_id_type=MESH,
        )

    def keep(q):
        return pltpu.make_async_copy(attended.at[q], out.at[:, lanes_of(q)], local_sem)

    both = projected[:, 384:512]
    soft = softmax_rows(dot_nt(last_query[...] * 0.125, both), me * 128).astype(BF)
    out[:, 1024:1152] = dot(soft, lane_half(both, 1)).astype(BF)
    for start in range(0, 1024, STEP):
        size = start + STEP
        query = projected[start:size, 0:128] * 0.125
        total = jnp.zeros((STEP, 128), F32)
        for head in range(2):
            keys = lane_half(projected[0:size, 128:256], head)
            values = lane_half(projected[0:size, 256:384], head)
            soft = softmax_rows(dot_nt(query, keys), start).astype(BF)
            total = total + dot(soft, values)
        if start == 0:
            meet(mates)
        for q in range(start // 128, size // 128):
            begin = q * 128 - start
            attended[q] = total[begin : begin + 128].astype(BF)

            @pl.when(me == q)
            def _():
                keep(q).start()

            @pl.when(me != q)
            def _():
                copy_to(q).start()

    for q in range(8):

        @pl.when(me == q)
        def _():
            keep(q).wait()

        @pl.when(me != q)
        def _():
            copy_from(q).wait_recv()
            copy_to(q).wait_send()


def attend(projected, last_query):
    return pl.pallas_call(
        attend_kernel,
        out_shape=jax.ShapeDtypeStruct((128, 1152), BF),
        in_specs=[VMEM, VMEM],
        out_specs=VMEM,
        scratch_shapes=[
            pltpu.VMEM((8, 128, 128), BF),
            pltpu.SemaphoreType.DMA((8,)),
            pltpu.SemaphoreType.DMA((8,)),
            pltpu.SemaphoreType.DMA,
        ],
        compiler_params=pltpu.CompilerParams(
            collective_id=1, has_side_effects=True, vmem_limit_bytes=LIMIT
        ),
    )(projected, last_query)


def attend_back_kernel(
    projected,
    last_query,
    rows,
    out,
    out_last,
    grad,
    key_total,
    value_total,
    send_sems,
    recv_sems,
    local_sem,
):
    c, z, x = place()
    me = c * 4 + x
    mates = team_mates()
    arrive(mates)
    local = pltpu.make_async_copy(rows.at[:, lanes_of(me)], grad.at[row_block(me)], local_sem)
    local.start()
    meet(mates)
    send = sender(send_sems, recv_sems)
    copies = []
    for index, (dc, dx) in enumerate(TEAM_STEPS):
        tc, tx = (c + dc) % 2, (x + dx) % 4
        copies.append(
            send(rows.at[:, lanes_of(tc * 4 + tx)], grad.at[row_block(me)], index, at(tc, z, tx))
        )
    key_total[...] = jnp.zeros_like(key_total)
    value_total[...] = jnp.zeros_like(value_total)
    both = projected[:, 384:512]
    query = last_query[...] * 0.125
    last_grad = rows[:, 1024:1152]
    soft = softmax_rows(dot_nt(query, both), me * 128)
    grad_soft = dot_nt(last_grad, both)
    inner = jnp.sum(soft * grad_soft, axis=1, keepdims=True)
    grad_scores = (soft * (grad_soft - inner)).astype(BF)
    out_last[...] = (dot(grad_scores, lane_half(both, 0)) * 0.125).astype(BF)
    out[:, 384:512] = (dot_tn(grad_scores, query) + dot_tn(soft.astype(BF), last_grad)).astype(BF)
    local.wait()
    for copy in copies:
        copy.wait_recv()
    for start in range(0, 1024, STEP):
        size = start + STEP
        query = projected[start:size, 0:128] * 0.125
        grad_rows = grad[start:size, :]
        total = jnp.zeros((STEP, 128), F32)
        for head in range(2):
            keys = lane_half(projected[0:size, 128:256], head)
            values = lane_half(projected[0:size, 256:384], head)
            soft = softmax_rows(dot_nt(query, keys), start)
            grad_soft = dot_nt(grad_rows, values)
            inner = jnp.sum(soft * grad_soft, axis=1, keepdims=True)
            grad_scores = (soft * (grad_soft - inner)).astype(BF)
            total = total + dot(grad_scores, keys)
            key_total[0:size, :] += dot_tn(grad_scores, lane_half(query, head))
            value_total[0:size, :] += dot_tn(soft.astype(BF), lane_half(grad_rows, head))
        out[start:size, 0:128] = (total * 0.125).astype(BF)
    out[:, 128:256] = key_total[...].astype(BF)
    out[:, 256:384] = value_total[...].astype(BF)
    for copy in copies:
        copy.wait_send()


def attend_back(projected, last_query, rows):
    return pl.pallas_call(
        attend_back_kernel,
        out_shape=(
            jax.ShapeDtypeStruct((1024, 512), BF),
            jax.ShapeDtypeStruct((128, 128), BF),
        ),
        in_specs=[VMEM] * 3,
        out_specs=(VMEM, VMEM),
        scratch_shapes=[
            pltpu.VMEM((1024, 128), BF),
            pltpu.VMEM((1024, 128), F32),
            pltpu.VMEM((1024, 128), F32),
            pltpu.SemaphoreType.DMA((7,)),
            pltpu.SemaphoreType.DMA((7,)),
            pltpu.SemaphoreType.DMA,
        ],
        compiler_params=pltpu.CompilerParams(
            collective_id=2, has_side_effects=True, vmem_limit_bytes=LIMIT
        ),
    )(projected, last_query, rows)


def norm_forward(hidden, gain, offset):
    center = hidden - jnp.mean(hidden, axis=-1, keepdims=True)
    inverse = lax.rsqrt(jnp.mean(center * center, axis=-1, keepdims=True) + EPSILON)
    unit = center * inverse
    return unit * gain + offset, unit, inverse


def norm_backward(grad_rows, unit, inverse, gain):
    grad_unit = grad_rows * gain
    grad_in = inverse * (
        grad_unit
        - jnp.mean(grad_unit, axis=-1, keepdims=True)
        - unit * jnp.mean(grad_unit * unit, axis=-1, keepdims=True)
    )
    return grad_in, jnp.sum(grad_rows * unit, axis=0), jnp.sum(grad_rows, axis=0)


def gelu_pair(values):
    tangent = jnp.tanh(GELU_C * (values + 0.044715 * values * values * values))
    output = 0.5 * values * (1.0 + tangent)
    slope = 0.5 * (1.0 + tangent) + 0.5 * values * (1.0 - tangent * tangent) * GELU_C * (
        1.0 + 3.0 * 0.044715 * values * values
    )
    return output, slope


def layer_forward(hidden, w):
    normed, unit_one, inverse_one = norm_forward(hidden, w["gain_one"], w["bias_one"])
    normed = normed.astype(BF)
    normed_all, projected = team_gather(
        gather_qkv_kernel,
        0,
        normed,
        w["qkv"],
        (w["qkv_bias"].reshape(1, 512),),
        (jax.ShapeDtypeStruct((1024, 512), BF),),
    )
    normed_all = normed_all.reshape(1024, D)
    last_query = (dot(normed, w["last_query"]) + w["last_bias"]).astype(BF)
    attended = attend(projected, last_query)
    packed = jnp.concatenate([attended[:, :1024], attended[:, 1088:]], axis=1)
    middle = hidden + dot(packed, w["out"]) + w["out_bias"]
    second, unit_two, inverse_two = norm_forward(middle, w["gain_two"], w["bias_two"])
    second_all, upper, activated = team_gather(
        gather_up_kernel,
        7,
        second.astype(BF),
        w["up"],
        (w["up_bias"].reshape(1, 544),),
        (jax.ShapeDtypeStruct((1024, 544), F32), jax.ShapeDtypeStruct((1024, 544), BF)),
    )
    second_all = second_all.reshape(1024, D)
    output = middle + product_scatter(dot, 5, activated, w["down"]) + w["down_bias"]
    saved = dict(
        normed=normed,
        normed_all=normed_all,
        unit_one=unit_one,
        inverse_one=inverse_one,
        projected=projected,
        last_query=last_query,
        attended=attended,
        unit_two=unit_two,
        inverse_two=inverse_two,
        second_all=second_all,
        upper=upper,
        activated=activated,
    )
    return output, saved


def layer_backward(grad_out, grad_low_all, w, kept, q, pieces):
    grad_low = grad_out.astype(BF)
    if grad_low_all is None:
        grad_low_all, up_grad, summed = team_gather(
            gather_back_kernel,
            8,
            grad_low,
            w["down"],
            (kept["upper"], pieces),
            (jax.ShapeDtypeStruct((1024, 544), BF), jax.ShapeDtypeStruct((ROWS, 128), BF)),
            rings_scratch(),
        )
        grad_low_all = grad_low_all.reshape(1024, D)
        grad_second, got = product_scatter(dot_nt, 11, up_grad, w["up"], summed)
    else:
        slope = gelu_pair(kept["upper"])[1]
        up_grad = (dot_nt(grad_low_all, w["down"]) * slope).astype(BF)
        grad_second, got = product_scatter(dot_nt, 9, up_grad, w["up"]), None
    grad_in, gain_two, bias_two = norm_backward(
        grad_second, kept["unit_two"], kept["inverse_two"], w["gain_two"]
    )
    grad_middle = grad_out + grad_in
    middle_low = grad_middle.astype(BF)
    attended_grad = dot_nt(middle_low, w["out"]).astype(BF)
    attended_grad = jnp.concatenate(
        [attended_grad[:, :1024], jnp.zeros((128, 64), BF), attended_grad[:, 1024:]], axis=1
    )
    qkv_grad, last_grad = attend_back(kept["projected"], kept["last_query"], attended_grad)
    grad_normed = product_scatter(dot_nt, 10, qkv_grad, w["qkv"])
    grad_normed = grad_normed + dot_nt(last_grad, w["last_query"])
    grad_in, gain_one, bias_one = norm_backward(
        grad_normed, kept["unit_one"], kept["inverse_one"], w["gain_one"]
    )
    grad_input = grad_middle + grad_in

    qkv_sums = jnp.sum(qkv_grad, axis=0, dtype=F32)
    last_sums = jnp.sum(last_grad, axis=0, dtype=F32)
    zeros = jnp.zeros((1024,), F32)
    qv = jnp.concatenate(
        [
            lax.dynamic_update_slice(zeros, qkv_sums[:128], (q * 128,)),
            last_sums[:64],
            lax.dynamic_update_slice(zeros, qkv_sums[256:384], (q * 128,)),
            qkv_sums[448:512],
        ]
    )
    up_sums = lax.dynamic_update_slice(
        jnp.zeros((FF,), F32), jnp.sum(up_grad, axis=0, dtype=F32), (q * 544,)
    )
    vectors = jnp.concatenate(
        [
            qv.reshape(8, 272),
            jnp.sum(middle_low, axis=0, dtype=F32).reshape(8, 136),
            gain_one.reshape(8, 136),
            bias_one.reshape(8, 136),
            gain_two.reshape(8, 136),
            bias_two.reshape(8, 136),
            up_sums.reshape(8, 544),
            jnp.sum(grad_low, axis=0, dtype=F32).reshape(8, 136),
        ],
        axis=1,
    )
    vectors = jnp.pad(vectors, ((0, 0), (0, 8 * 1280 - 1632))).reshape(8, 8, 1280)
    swapped_grad = jnp.concatenate([jnp.zeros((128, 64), BF), last_grad[:, :64]], axis=1)
    operands = (
        kept["attended"],
        jnp.pad(middle_low, ((0, 0), (0, 64))),
        kept["normed_all"],
        qkv_grad,
        kept["normed"],
        swapped_grad,
        vectors,
    )
    split = (
        kept["normed_all"],
        qkv_grad,
        kept["second_all"],
        up_grad,
        kept["activated"],
        grad_low_all,
    )
    return grad_input, operands, split, got


BOTH = ("section", "shard")


def pairs(route):
    out = []
    for c in range(2):
        for z in range(2):
            for x in range(4):
                tc, tz = route(c, z)
                out.append((c * 8 + z * 4 + x, tc * 8 + tz * 4 + x))
    return out


def local(
    inputs,
    cotangent,
    w_qkv,
    qv_bias,
    w_out,
    out_bias,
    gain_one,
    bias_one,
    gain_two,
    bias_two,
    w_up,
    up_bias,
    w_down,
    down_bias,
):
    c, z, x = place()
    q = c * 4 + x
    swap = [pair for pair in pairs(lambda a, b: (b, a)) if pair[0] != pair[1]]
    cross_back = pairs(lambda a, b: (b, 1 - a))

    def swapped(array):
        return jnp.where(c == z, array, lax.ppermute(array, BOTH, swap))

    def by_z(own, other):
        return jnp.where(z == 0, own, other), jnp.where(z == 0, other, own)

    small = jnp.concatenate(
        [
            qv_bias[0],
            up_bias[0],
            out_bias[0],
            gain_one[0],
            bias_one[0],
            gain_two[0],
            bias_two[0],
            down_bias[0],
        ]
    )
    own_qkv = w_qkv[0]
    last_cols = [own_qkv[:, part * D + 1024 : (part + 1) * D] for part in range(3)]
    common = jnp.concatenate(
        [
            jnp.concatenate(
                [last_cols[1], last_cols[2], last_cols[0], jnp.zeros((136, 64), BF)], axis=1
            ),
            jnp.pad(small, (0, 2048 - 1632)).reshape(8, 256),
        ]
    )
    blocks = jnp.concatenate(
        [own_qkv[:, part * D : part * D + 1024].reshape(136, 8, 128) for part in range(3)]
        + [w_up[0].reshape(136, 8, 544)],
        axis=2,
    ).transpose(1, 0, 2)
    blocks = jnp.pad(blocks, ((0, 0), (0, 8), (0, 0)))
    replica = lax.axis_index("replica")
    late = lax.dynamic_slice(
        jnp.pad(blocks, ((0, 0), (0, 0), (0, 96))), (0, 0, replica * 128), (8, 144, 128)
    )
    first_blocks, late, all_common, hidden, top_grad = spread_weights(
        late, common, inputs[:, 0], cotangent[:, 0]
    )
    teams = [[a * 8 + b * 4 + d for a in range(2) for d in range(4)] for b in range(2)]
    top_grad_all = lax.all_gather(top_grad, BOTH, axis_index_groups=teams, axis=0, tiled=True)
    second_blocks = lax.all_gather(late, "replica", axis=0)
    own_out = lax.all_gather(w_out[0], "shard", axis=0, tiled=True)
    partner_out = lax.ppermute(own_out, "section", [(0, 1), (1, 0)])
    all_out = (
        jnp.where(c == 0, own_out, partner_out),
        jnp.where(c == 0, partner_out, own_out),
    )
    cuts = (
        first_blocks.reshape(4, 2, 2, 4, 144, 128)
        .transpose(2, 3, 4, 0, 1, 5)[:, :, :136]
        .reshape(D, 1024)[:, :928],
        second_blocks.transpose(1, 2, 0, 3)[:, :136].reshape(D, 1024)[:, :928],
    )
    down_own = swapped(w_down[0])
    down_other = lax.ppermute(w_down[0], BOTH, cross_back)
    all_down = by_z(down_own, down_other)

    def layer_weights(layer):
        cut = cuts[layer]
        shared = all_common[layer, :, :136].reshape(D, 256)
        vec = all_common[layer, :, 136:].reshape(8, 2048)[:, :1632].astype(F32)

        def piece(start, size):
            return vec[:, start : start + size].reshape(-1)

        qv = piece(0, 272)
        six = vec[:, 816:].reshape(8, 6, 136).transpose(1, 0, 2).reshape(6, D)
        six = lax.optimization_barrier(six)
        none = jnp.zeros((128,), F32)
        qkv_bias = jnp.concatenate(
            [
                lax.dynamic_slice(qv, (q * 128,), (128,)),
                none,
                lax.dynamic_slice(qv, (D + q * 128,), (128,)),
                none[:64],
                qv[2 * D - 64 :],
            ]
        )
        return dict(
            qkv=jnp.concatenate([cut[:, :384], shared[:, :128]], axis=1),
            last_query=shared[:, 128:],
            qkv_bias=qkv_bias,
            last_bias=jnp.concatenate([qv[1024:D], none[:64]]),
            out=all_out[layer],
            out_bias=six[0:1],
            gain_one=six[1:2],
            bias_one=six[2:3],
            gain_two=six[3:4],
            bias_two=six[4:5],
            up=cut[:, 384:],
            up_bias=lax.dynamic_slice(piece(272, 544), (q * 544,), (544,)),
            down=all_down[layer],
            down_bias=six[5:6],
        )

    weights = [layer_weights(0), layer_weights(1)]
    hidden = hidden.astype(F32)
    top_grad = top_grad.astype(F32)
    out_first, kept_first = layer_forward(hidden, weights[0])
    out_second, kept_second = layer_forward(out_first.astype(BF).astype(F32), weights[1])
    grad_second, operands, split, _ = layer_backward(
        top_grad, top_grad_all, weights[1], kept_second, q, None
    )
    rows = jnp.stack([out_first.astype(BF), out_second.astype(BF)])
    shared, section_out = shared_scatter(*operands, rows)
    pieces = grad_pieces(*split, shared)
    grad_first, operands, split, second_got = layer_backward(
        grad_second.astype(BF).astype(F32), None, weights[0], kept_first, q, pieces
    )
    rows = jnp.stack([grad_first.astype(BF), grad_second.astype(BF)])
    shared, input_grad = shared_scatter(*operands, rows)
    first_got = reduce_grads(grad_pieces(*split, shared))
    grad_qkv, grad_out_w, grad_up, grad_down, vectors = assemble(first_got, second_got)
    section_out = section_out.astype(F32)[None, :, None]
    input_grad = input_grad.astype(F32)[None, :, None]
    vec = vectors.reshape(-1)
    grads = (
        grad_qkv,
        vec[:272],
        grad_out_w,
        vec[272:408],
        vec[408:544],
        vec[544:680],
        vec[680:816],
        vec[816:952],
        grad_up,
        vec[952:1496],
        grad_down,
        vec[1496:1632],
    )
    return (section_out, input_grad) + tuple(grad[None] for grad in grads)


def solution(mesh):
    return jax.shard_map(
        local,
        mesh=mesh,
        in_specs=(
            P(None, "replica", "shard", None),
            P(None, "replica", "shard", None),
            P("section", "shard", None),
            P("section", "shard"),
            P("section", "shard", None),
            P("section", "shard"),
            P("section", "shard"),
            P("section", "shard"),
            P("section", "shard"),
            P("section", "shard"),
            P("section", "shard", None),
            P("section", "shard"),
            P("section", "shard", None),
            P("section", "shard"),
        ),
        out_specs=(
            P("section", None, "replica", "shard", None),
            P("section", None, "replica", "shard", None),
            P("section", "shard", None),
            P("section", "shard"),
            P("section", "shard", None),
            P("section", "shard"),
            P("section", "shard"),
            P("section", "shard"),
            P("section", "shard"),
            P("section", "shard"),
            P("section", "shard", None),
            P("section", "shard"),
            P("section", "shard", None),
            P("section", "shard"),
        ),
        check_vma=False,
    )
```

```python
import functools

import jax
import jax.numpy as jnp
from jax import lax
from jax.experimental import pallas as pl
from jax.experimental.pallas import tpu as pltpu
from jax.sharding import PartitionSpec as P

D = 1088
FF = 4352
HEAD_DIM = 64
EPSILON = 1e-05
GELU_C = 0.7978845608028654
NEG_FILL = -1e30
BF = jnp.bfloat16
F32 = jnp.float32
MESH = pl.DeviceIdType.MESH
VMEM = pl.BlockSpec(memory_space=pltpu.VMEM)
LIMIT = 56 * 1024 * 1024


def place():
    c = lax.axis_index("section")
    j = lax.axis_index("shard")
    return c, j // 4, j % 4


def at(c, z, x):
    return {"section": c, "shard": z * 4 + x}


def arrive(devices):
    barrier = pltpu.get_barrier_semaphore()
    for device in devices:
        pl.semaphore_signal(barrier, inc=1, device_id=device, device_id_type=MESH)


def meet(devices):
    pl.semaphore_wait(pltpu.get_barrier_semaphore(), len(devices))


def greet(devices):
    arrive(devices)
    meet(devices)


def nothing():
    pass


ALONE = ([], nothing, nothing, nothing, nothing)


def sender(send_sems, recv_sems):
    def make(src, dst, index, device):
        copy = pltpu.make_async_remote_copy(
            src_ref=src,
            dst_ref=dst,
            send_sem=send_sems.at[index],
            recv_sem=recv_sems.at[index],
            device_id=device,
            device_id_type=MESH,
        )
        copy.start()
        return copy

    return make


def gather_core(own, out, send_sems, recv_sems, local_sem, use, beside=ALONE):
    c, z, x = place()
    ahead, behind, far = (x + 1) % 4, (x + 3) % 4, (x + 2) % 4
    partner, up, down = at(1 - c, z, x), at(c, z, ahead), at(c, z, behind)
    rows = own.shape[0]
    first, second = pl.ds(0, rows // 2), pl.ds(rows // 2, rows // 2)
    me, other = c * 4 + x, (1 - c) * 4
    local = pltpu.make_async_copy(own, out.at[me], local_sem)
    local.start()
    friends = [partner, up, down] + beside[0]
    arrive(friends)
    local.wait()
    meet(friends)
    send = sender(send_sems, recv_sems)
    to_up = send(own.at[first], out.at[me, first], 0, up)
    to_down = send(own.at[second], out.at[me, second], 1, down)
    to_partner = send(own, out.at[me], 2, partner)
    up_rest = send(own.at[second], out.at[me, second], 3, up)
    down_rest = send(own.at[first], out.at[me, first], 4, down)
    from_down, from_up, from_far = c * 4 + behind, c * 4 + ahead, c * 4 + far
    beside[1]()
    use(me)
    to_up.wait_recv()
    pass_up = send(out.at[from_down, first], out.at[from_down, first], 5, up)
    to_down.wait_recv()
    pass_down = send(out.at[from_up, second], out.at[from_up, second], 6, down)
    to_partner.wait_recv()
    use(other + x)
    up_rest.wait_recv()
    share_down = send(out.at[from_down], out.at[from_down], 7, partner)
    down_rest.wait_recv()
    share_up = send(out.at[from_up], out.at[from_up], 8, partner)
    use(from_down)
    use(from_up)
    beside[2]()
    pass_up.wait_recv()
    share_first = send(out.at[from_far, first], out.at[from_far, first], 9, partner)
    pass_down.wait_recv()
    share_second = send(out.at[from_far, second], out.at[from_far, second], 10, partner)
    use(from_far)
    beside[3]()
    share_down.wait_recv()
    use(other + behind)
    share_up.wait_recv()
    use(other + ahead)
    share_first.wait_recv()
    share_second.wait_recv()
    use(other + far)
    for copy in (
        to_up,
        to_down,
        to_partner,
        up_rest,
        down_rest,
        pass_up,
        pass_down,
        share_down,
        share_up,
        share_first,
        share_second,
    ):
        copy.wait_send()
    beside[4]()


def row_block(q):
    return pl.ds(pl.multiple_of(q * 128, 128), 128)


def gather_qkv_kernel(own, weight, bias, out, projected, send_sems, recv_sems, local_sem):
    def use(q):
        projected[row_block(q), :] = (dot(out[q], weight[...]) + bias[...]).astype(BF)

    gather_core(own, out, send_sems, recv_sems, local_sem, use)


def gather_up_kernel(own, weight, bias, out, upper, activated, send_sems, recv_sems, local_sem):
    def use(q):
        values = dot(out[q], weight[...]) + bias[...]
        upper[row_block(q), :] = values
        activated[row_block(q), :] = gelu_pair(values)[0].astype(BF)

    gather_core(own, out, send_sems, recv_sems, local_sem, use)


def gather_back_kernel(
    own, weight, upper, pieces, out, up_grad, wide_sum, send_sems, recv_sems, local_sem, *rings
):
    def use(q):
        slope = gelu_pair(upper[row_block(q), :])[1]
        up_grad[row_block(q), :] = (dot_nt(out[q], weight[...]) * slope).astype(BF)

    stages = []

    def begin():
        stages.extend(rings_first(pieces, wide_sum, *rings))

    def end():
        stages[1]()
        stages[2]()

    gather_core(
        own,
        out,
        send_sems,
        recv_sems,
        local_sem,
        use,
        (
            list(grid_place()[2]),
            begin,
            nothing,
            lambda: stages[0](),
            end,
        ),
    )


def team_gather(kernel, collective_id, own, weight, rest, results, scratch=()):
    rows, columns = own.shape
    return pl.pallas_call(
        kernel,
        out_shape=(jax.ShapeDtypeStruct((8, rows, columns), BF),) + results,
        in_specs=[VMEM] * (2 + len(rest)),
        out_specs=(VMEM,) * (1 + len(results)),
        scratch_shapes=[
            pltpu.SemaphoreType.DMA((11,)),
            pltpu.SemaphoreType.DMA((11,)),
            pltpu.SemaphoreType.DMA,
        ]
        + list(scratch),
        compiler_params=pltpu.CompilerParams(
            collective_id=collective_id, has_side_effects=True, vmem_limit_bytes=LIMIT
        ),
    )(own, weight, *rest)


def scatter_core(
    half,
    other_part,
    mine_part,
    prepare,
    beside,
    out,
    from_partner,
    far_sum,
    up_sum,
    down_sum,
    far_first,
    far_second,
    got_down,
    got_up,
    send_sems,
    recv_sems,
):
    c, z, x = place()
    ahead, behind, far = (x + 1) % 4, (x + 3) % 4, (x + 2) % 4
    partner, up, down = at(1 - c, z, x), at(c, z, ahead), at(c, z, behind)
    rows = out.shape[0]
    first, second = pl.ds(0, half), pl.ds(half, rows - half)
    send = sender(send_sems, recv_sems)
    friends = [partner, up, down] + beside[0]
    arrive(friends)
    order = (far, ahead, behind, x)
    parts = [other_part(where) for where in order]
    meet(friends)
    swaps = [
        send(part, from_partner.at[where], index, partner)
        for index, (where, part) in enumerate(zip(order, parts))
    ]
    beside[1]()
    for where in (far, ahead, behind, x):
        prepare(where)
    swap_far, swap_up, swap_down, swap_own = swaps

    def both(where, part):
        return mine_part(where, part) + from_partner[where, part, :].astype(F32)

    swap_far.wait_recv()
    far_sum[first, :] = both(far, first).astype(BF)
    far_up = send(far_sum.at[first], far_first, 4, up)
    far_sum[second, :] = both(far, second).astype(BF)
    far_down = send(far_sum.at[second], far_second, 5, down)
    swap_up.wait_recv()
    up_sum[second, :] = both(ahead, second).astype(BF)
    up_second = send(up_sum.at[second], got_down.at[second], 6, up)
    swap_down.wait_recv()
    down_sum[first, :] = both(behind, first).astype(BF)
    down_first = send(down_sum.at[first], got_up.at[first], 7, down)
    beside[2]()
    far_up.wait_recv()
    up_sum[first, :] = (both(ahead, first) + far_first[...].astype(F32)).astype(BF)
    up_first = send(up_sum.at[first], got_down.at[first], 8, up)
    far_down.wait_recv()
    down_sum[second, :] = (both(behind, second) + far_second[...].astype(F32)).astype(BF)
    down_second = send(down_sum.at[second], got_up.at[second], 9, down)
    swap_own.wait_recv()
    out[first, :] = both(x, first)
    out[second, :] = both(x, second)
    beside[3]()
    up_second.wait_recv()
    up_first.wait_recv()
    down_first.wait_recv()
    down_second.wait_recv()
    out[...] = out[...] + got_down[...].astype(F32) + got_up[...].astype(F32)
    for copy in (
        swap_far,
        swap_up,
        swap_down,
        swap_own,
        far_up,
        far_down,
        up_second,
        down_first,
        up_first,
        down_second,
    ):
        copy.wait_send()
    beside[4]()


def product_scatter_kernel(product, task, left, right, *refs):
    c, z, x = place()
    beside = ALONE
    if task == "home":
        wide_sum, out, own, other, mine, *refs = refs
        refs, summed, more = refs[:10], refs[10], refs[11:]
        beside = home_beside(1, wide_sum, summed, own, more[:5], more[5:])
    elif task == "spread":
        own, out, got, other, mine, *refs = refs
        refs, more = refs[:10], refs[10:]
        beside = spread_beside(1, own, got, more)
    else:
        out, other, mine, *refs = refs

    def other_part(where):
        rows = left[row_block((1 - c) * 4 + where), :]
        other[where] = product(rows, right[...]).astype(BF)
        return other.at[where]

    def prepare(where):
        mine[where] = product(left[row_block(c * 4 + where), :], right[...])

    scatter_core(
        64, other_part, lambda where, part: mine[where, part, :], prepare, beside, out, *refs
    )


def scatter_scratch(rows, columns, half):
    block = pltpu.VMEM((rows, columns), BF)
    return [
        pltpu.VMEM((4, rows, columns), BF),
        block,
        block,
        block,
        pltpu.VMEM((half, columns), BF),
        pltpu.VMEM((rows - half, columns), BF),
        block,
        block,
        pltpu.SemaphoreType.DMA((10,)),
        pltpu.SemaphoreType.DMA((10,)),
    ]


def product_scatter(product, collective_id, left, right, extra=None):
    out_shape = (jax.ShapeDtypeStruct((128, D), F32),)
    operands = (left, right)
    task, scratch = "", []
    if extra is not None:
        operands += (extra,)
        if extra.shape == WIDE:
            task = "home"
            out_shape += (jax.ShapeDtypeStruct((GOT_ROWS, 128), BF),)
            scratch = [pltpu.VMEM((ROWS, 128), BF)] + second_scratch() + home_scratch()
        else:
            task = "spread"
            out_shape += (jax.ShapeDtypeStruct((8, GOT_ROWS, 128), BF),)
            scratch = spread_scratch()
    out = pl.pallas_call(
        functools.partial(product_scatter_kernel, product, task),
        out_shape=out_shape,
        in_specs=[VMEM] * len(operands),
        out_specs=(VMEM,) * len(out_shape),
        scratch_shapes=[pltpu.VMEM((4, 128, D), BF), pltpu.VMEM((4, 128, D), F32)]
        + scatter_scratch(128, D, 64)
        + scratch,
        compiler_params=pltpu.CompilerParams(
            collective_id=collective_id, has_side_effects=True, vmem_limit_bytes=LIMIT
        ),
    )(*operands)
    return out[0] if extra is None else out


TEAM_STEPS = tuple((dc, dx) for dc in range(2) for dx in range(4) if dc or dx)


def ring_spread(send, base, source, block, me, up, down, first, second):
    before, after = (me + 3) % 4, (me + 1) % 4
    copies = [
        send(source(first), block(me, first), base, up),
        send(source(second), block(me, second), base + 1, down),
        send(source(second), block(me, second), base + 2, up),
        send(source(first), block(me, first), base + 3, down),
    ]

    def middle():
        copies[0].wait_recv()
        copies.append(send(block(before, first), block(before, first), base + 4, up))
        copies[1].wait_recv()
        copies.append(send(block(after, second), block(after, second), base + 5, down))

    def last():
        for copy in copies[2:]:
            copy.wait_recv()

    return copies, middle, last


def weights_kernel(
    late,
    common,
    rows,
    other_rows,
    first,
    second,
    out_common,
    out_rows,
    out_other,
    send_sems,
    recv_sems,
    common_send,
    common_recv,
    share_send,
    share_recv,
    ring_send,
    ring_recv,
    swap_send,
    swap_recv,
    local_sems,
):
    c, z, x = place()
    r = lax.axis_index("replica")
    y, zh = r // 2, r % 2
    zf = zh * 2 + z
    slot = z * 4 + x

    def device(ty, tz):
        return {"section": c, "shard": (tz % 2) * 4 + x, "replica": ty * 2 + tz // 2}

    y_up, y_down = device((y + 1) % 4, zf), device((y + 3) % 4, zf)
    z_up, z_down = device(y, (zf + 1) % 4), device(y, (zf + 3) % 4)
    z_other = device(y, (zf + 3 + 2 * z) % 4)
    partner, diagonal, z_pair = at(1 - c, z, x), at(1 - c, 1 - z, x), at(c, 1 - z, x)
    team = [((c + dc) % 2, (x + dx) % 4) for dc, dx in TEAM_STEPS]
    core_steps = [(dz, dx) for dx in (1, 3, 2, 0) for dz in range(2) if dz or dx]
    core = [((z + dz) % 2, (x + dx) % 4) for dz, dx in core_steps]
    source_of = [core_steps.index((dz, (4 - dx) % 4)) for dz, dx in core_steps]
    greet(
        [at(tc, z, tx) for tc, tx in team]
        + [at(c, 1 - z, (x + dx) % 4) for dx in range(4)]
        + [diagonal, y_up, y_down, z_other]
    )

    def remote(src, dst, sends, recvs, index, target):
        return pltpu.make_async_remote_copy(
            src_ref=src,
            dst_ref=dst,
            send_sem=sends.at[index],
            recv_sem=recvs.at[index],
            device_id=target,
            device_id_type=MESH,
        )

    def to_team(index, layer):
        tc, tx = team[index]
        place_at = first.at[y, zf, x] if layer == 0 else second.at[slot]
        return remote(late.at[tc * 4 + tx], place_at, send_sems, recv_sems, index, at(tc, z, tx))

    def swapped(index):
        src, dst = ((rows, out_rows), (other_rows, out_other))[index]
        return remote(src.at[c], dst, swap_send, swap_recv, index, diagonal)

    def kept(index):
        src, dst = ((rows, out_rows), (other_rows, out_other))[index]
        return pltpu.make_async_copy(src.at[c], dst, local_sems.at[2 + index])

    def common_to(index):
        tz, tx = core[index]
        return remote(
            common, out_common.at[c, slot], common_send, common_recv, index, at(c, tz, tx)
        )

    def shared(index):
        if index == 7:
            source = out_common.at[c, slot]
        else:
            tz, tx = core[index]
            source = out_common.at[c, tz * 4 + tx]
        return remote(source, source, share_send, share_recv, index, partner)

    keep = pltpu.make_async_copy(common, out_common.at[c, slot], local_sems.at[0])
    keep.start()

    @pl.when(c == 0)
    def _():
        for index in range(7):
            to_team(index, 0).start()
        pltpu.make_async_copy(late.at[c * 4 + x], first.at[y, zf, x], local_sems.at[1]).start()

    @pl.when(c == 1)
    def _():
        for index in range(7):
            to_team(index, 1).start()
        pltpu.make_async_copy(late.at[c * 4 + x], second.at[slot], local_sems.at[1]).start()

    for index in range(7):
        common_to(index).start()

    @pl.when(c == z)
    def _():
        kept(0).start()
        kept(1).start()

    @pl.when(c != z)
    def _():
        swapped(0).start()
        swapped(1).start()

    for index, (dc, dx) in enumerate(TEAM_STEPS):

        @pl.when((c + dc) % 2 == 0)
        def _():
            to_team(index, 0).wait_recv()

        @pl.when((c + dc) % 2 == 1)
        def _():
            to_team(index, 1).wait_recv()

    @pl.when(c == 0)
    def _():
        pltpu.make_async_copy(late.at[c * 4 + x], first.at[y, zf, x], local_sems.at[1]).wait()

    @pl.when(c == 1)
    def _():
        pltpu.make_async_copy(late.at[c * 4 + x], second.at[slot], local_sems.at[1]).wait()

    def send(src, dst, index, target):
        copy = remote(src, dst, ring_send, ring_recv, index, target)
        copy.start()
        return copy

    one, two = pl.ds(0, 1), pl.ds(1, 1)
    three, four = pl.ds(2, 1), pl.ds(3, 1)
    left, right = pl.ds(0, 2), pl.ds(2, 2)
    y_copies, y_middle, y_last = ring_spread(
        send,
        0,
        lambda part: first.at[y, zf, part],
        lambda i, part: first.at[i, zf, part],
        y,
        y_up,
        y_down,
        one,
        two,
    )
    z_copies, z_middle, z_last = ring_spread(
        send,
        6,
        lambda part: first.at[y, zf, part],
        lambda i, part: first.at[y, i, part],
        zf,
        z_up,
        z_down,
        three,
        four,
    )
    pair_copy = send(second.at[pl.ds(z * 4, 4)], second.at[pl.ds(z * 4, 4)], 24, z_pair)
    keep.wait()
    shared(7).start()
    for index in range(7):
        common_to(source_of[index]).wait_recv()
        shared(index).start()
    y_middle()
    z_middle()
    y_last()
    more_z, z_middle_too, z_last_too = ring_spread(
        send,
        12,
        lambda part: first.at[part, zf, pl.ds(0, 2)],
        lambda i, part: first.at[part, i, pl.ds(0, 2)],
        zf,
        z_up,
        z_down,
        left,
        right,
    )
    z_last()
    more_y, y_middle_too, y_last_too = ring_spread(
        send,
        18,
        lambda part: first.at[y, part, pl.ds(2, 2)],
        lambda i, part: first.at[i, part, pl.ds(2, 2)],
        y,
        y_up,
        y_down,
        left,
        right,
    )
    z_middle_too()
    y_middle_too()
    pair_copy.wait_recv()
    for index in range(8):
        shared(index).wait_recv()
    z_last_too()
    y_last_too()

    @pl.when(c == z)
    def _():
        kept(0).wait()
        kept(1).wait()

    @pl.when(c != z)
    def _():
        for index in range(2):
            swapped(index).wait_recv()
            swapped(index).wait_send()

    @pl.when(c == 0)
    def _():
        for index in range(7):
            to_team(index, 0).wait_send()

    @pl.when(c == 1)
    def _():
        for index in range(7):
            to_team(index, 1).wait_send()

    for index in range(7):
        common_to(index).wait_send()
    for index in range(8):
        shared(index).wait_send()
    for copy in y_copies + z_copies + more_z + more_y + [pair_copy]:
        copy.wait_send()


def spread_weights(late, common, rows, other_rows):
    dma = pltpu.SemaphoreType.DMA
    return pl.pallas_call(
        weights_kernel,
        out_shape=(
            jax.ShapeDtypeStruct((4, 4, 4, 144, 128), BF),
            jax.ShapeDtypeStruct(late.shape, BF),
            jax.ShapeDtypeStruct((2, 8) + common.shape, BF),
            jax.ShapeDtypeStruct(rows.shape[1:], BF),
            jax.ShapeDtypeStruct(rows.shape[1:], BF),
        ),
        in_specs=[VMEM] * 4,
        out_specs=(VMEM,) * 5,
        scratch_shapes=[
            dma((7,)),
            dma((7,)),
            dma((7,)),
            dma((7,)),
            dma((8,)),
            dma((8,)),
            dma((25,)),
            dma((25,)),
            dma((2,)),
            dma((2,)),
            dma((4,)),
        ],
        compiler_params=pltpu.CompilerParams(
            collective_id=3, has_side_effects=True, vmem_limit_bytes=LIMIT
        ),
    )(late, common, rows, other_rows)


SPLIT_ROWS = 4 * 144
DOWN_ROWS = 320
SHARED_ROWS = 96
ROWS = SPLIT_ROWS + DOWN_ROWS + SHARED_ROWS
OWN_ROWS = DOWN_ROWS + SHARED_ROWS
GOT_ROWS = 8 * 144 + 2 * OWN_ROWS


def widen(block):
    return block.astype(F32)


def ring_reduce(send, base, block, me, up, down, first, second, far, relay, got, result):
    after, before, opposite = (me + 1) % 4, (me + 3) % 4, (me + 2) % 4
    copies = [
        send(block(opposite, first), far[0], base, up),
        send(block(opposite, second), far[1], base + 1, down),
        send(block(after, second), got[0].at[second], base + 2, up),
        send(block(before, first), got[1].at[first], base + 3, down),
    ]

    def middle():
        copies[0].wait_recv()
        relay[0][...] = (widen(block(after, first)[...]) + widen(far[0][...])).astype(BF)
        copies.append(send(relay[0], got[0].at[first], base + 4, up))
        copies[1].wait_recv()
        relay[1][...] = (widen(block(before, second)[...]) + widen(far[1][...])).astype(BF)
        copies.append(send(relay[1], got[1].at[second], base + 5, down))

    def last():
        for copy in copies[2:]:
            copy.wait_recv()
        for part in (first, second):
            value = (
                widen(block(me, part)[...])
                + widen(got[0].at[part][...])
                + widen(got[1].at[part][...])
            )
            result.at[part][...] = value.astype(BF)
        for copy in copies:
            copy.wait_send()

    return middle, last


TOP = ROWS // 2
CUT = TOP // 32 * 16


WIDE = (2, 4, TOP, 128)


def first_scratch():
    dma = pltpu.SemaphoreType.DMA
    return [
        pltpu.VMEM((2, 2, 2, TOP, 128), BF),
        pltpu.VMEM((2, 2, 2, TOP, 128), BF),
        pltpu.VMEM((2, 2, 4, TOP, 128), BF),
        dma((12,)),
        dma((12,)),
    ]


def second_scratch():
    dma = pltpu.SemaphoreType.DMA
    return [
        pltpu.VMEM((2, 2, TOP - CUT, 128), BF),
        pltpu.VMEM((2, 2, TOP - CUT, 128), BF),
        pltpu.VMEM((2, 2, TOP, 128), BF),
        dma((12,)),
        dma((12,)),
    ]


def grid_place():
    c, z, x = place()
    r = lax.axis_index("replica")
    y, zh = r // 2, r % 2
    zf = zh * 2 + z

    def device(ty, tz):
        return {"section": c, "shard": (tz % 2) * 4 + x, "replica": ty * 2 + tz // 2}

    return (
        y,
        zf,
        (
            device((y + 1) % 4, zf),
            device((y + 3) % 4, zf),
            device(y, (zf + 1) % 4),
            device(y, (zf + 3) % 4),
        ),
    )


def starter(sends, recvs):
    def send(src, dst, index, target):
        copy = pltpu.make_async_remote_copy(
            src_ref=src,
            dst_ref=dst,
            send_sem=sends.at[index],
            recv_sem=recvs.at[index],
            device_id=target,
            device_id_type=MESH,
        )
        copy.start()
        return copy

    return send


def rings_first(pieces, wide_sum, far, relay, got, sends, recvs):
    y, zf, (y_up, y_down, z_up, z_down) = grid_place()
    send = starter(sends, recvs)
    low, high = pl.ds(0, 2), pl.ds(2, 2)
    top, bottom = pl.ds(0, TOP), pl.ds(TOP, TOP)

    def buffers(k):
        return (
            [far.at[k, 0], far.at[k, 1]],
            [relay.at[k, 0], relay.at[k, 1]],
            [got.at[k, 0], got.at[k, 1]],
            wide_sum.at[k],
        )

    y_mid, y_last = ring_reduce(
        send,
        0,
        lambda i, part: pieces.at[i, part, top],
        y,
        y_up,
        y_down,
        low,
        high,
        *buffers(0),
    )
    z_mid, z_last = ring_reduce(
        send,
        6,
        lambda i, part: pieces.at[part, i, bottom],
        zf,
        z_up,
        z_down,
        low,
        high,
        *buffers(1),
    )

    def middle():
        y_mid()
        z_mid()

    return middle, y_last, z_last


def rings_second(k, wide_sum, out, far, relay, got, sends, recvs):
    y, zf, (y_up, y_down, z_up, z_down) = grid_place()
    parts = pl.ds(0, CUT), pl.ds(0, TOP - CUT)
    me, up, down = ((zf, z_up, z_down), (y, y_up, y_down))[k]
    return ring_reduce(
        starter(sends, recvs),
        6 * k,
        lambda i, part: wide_sum.at[k, i, part],
        me,
        up,
        down,
        pl.ds(0, CUT),
        pl.ds(CUT, TOP - CUT),
        [far.at[k, 0, parts[0]], far.at[k, 1, parts[1]]],
        [relay.at[k, 0, parts[0]], relay.at[k, 1, parts[1]]],
        [got.at[k, 0], got.at[k, 1]],
        out.at[pl.ds(TOP * k, TOP)],
    )


def home_scratch():
    dma = pltpu.SemaphoreType.DMA
    return [dma((9,)), dma((10,)), dma((2,))]


def spread_scratch():
    dma = pltpu.SemaphoreType.DMA
    return [dma, dma((13,)), dma((13,))]


def remote_copy(src, dst, send_sem, recv_sem, target):
    return pltpu.make_async_remote_copy(
        src_ref=src,
        dst_ref=dst,
        send_sem=send_sem,
        recv_sem=recv_sem,
        device_id=target,
        device_id_type=MESH,
    )


def home_stages(layer, summed, own, home_send, home_recv, local_sems):
    c, z, x = place()
    me = c * 4 + x
    mine = pl.ds(pl.multiple_of(me * 144, 16), 144)
    holds = c == layer
    other = c != layer
    stays = jnp.logical_and(holds, z == layer)
    leaves = jnp.logical_or(other, z != layer)
    copy = remote_copy

    def split_part(tx):
        return summed.at[pl.ds(pl.multiple_of(tx * 144, 16), 144)]

    def to_row(dx, base):
        tx = (x + dx) % 4
        return copy(
            split_part(tx),
            own.at[mine],
            home_send.at[base + dx],
            home_recv.at[base + dx],
            at(layer, z, tx),
        )

    def split_here():
        return pltpu.make_async_copy(split_part(x), own.at[mine], local_sems.at[0])

    own_part = pl.ds(SPLIT_ROWS, OWN_ROWS)
    slot = pl.ds(pl.multiple_of(8 * 144 + z * OWN_ROWS, 16), OWN_ROWS)

    def to_owner(t):
        return copy(
            summed.at[own_part],
            own.at[slot],
            home_send.at[8],
            home_recv.at[8 + t],
            at(layer, c, x),
        )

    def from_row(dx):
        return copy(
            split_part(x),
            own.at[mine],
            home_send.at[4 + dx],
            home_recv.at[4 + dx],
            at(1 - c, z, x),
        )

    def from_owner(t):
        return copy(
            summed.at[own_part],
            own.at[slot],
            home_send.at[8],
            home_recv.at[8 + t],
            at(1 - c, z, x),
        )

    def own_here():
        return pltpu.make_async_copy(summed.at[own_part], own.at[slot], local_sems.at[1])

    def home():
        @pl.when(holds)
        def _():
            split_here().start()
            for dx in (1, 2, 3):
                to_row(dx, 0).start()

        @pl.when(other)
        def _():
            for dx in range(4):
                to_row(dx, 4).start()

        @pl.when(stays)
        def _():
            own_here().start()

        @pl.when(leaves)
        def _():
            to_owner(z).start()

    def arrived():
        @pl.when(holds)
        def _():
            split_here().wait()
            for dx in (1, 2, 3):
                to_row(dx, 0).wait_recv()
            for dx in range(4):
                from_row(dx).wait_recv()

            @pl.when(z == layer)
            def _():
                own_here().wait()
                from_owner(1 - layer).wait_recv()

            @pl.when(z != layer)
            def _():
                from_owner(0).wait_recv()
                from_owner(1).wait_recv()

    def end():
        @pl.when(holds)
        def _():
            for dx in (1, 2, 3):
                to_row(dx, 0).wait_send()

        @pl.when(other)
        def _():
            for dx in range(4):
                to_row(dx, 4).wait_send()

        @pl.when(leaves)
        def _():
            to_owner(z).wait_send()

    return home, arrived, end


def spread_stages(layer, own, out, local_sem, sends, recvs):
    c, z, x = place()
    r = lax.axis_index("replica")
    y, zh = r // 2, r % 2
    y_up, y_down, _, _ = grid_place()[2]
    across = {"section": c, "shard": z * 4 + x, "replica": y * 2 + 1 - zh}
    holds = c == layer
    copy = remote_copy
    here, there = y * 2 + zh, y * 2 + 1 - zh
    front, back = pl.ds(0, GOT_ROWS // 2), pl.ds(GOT_ROWS // 2, GOT_ROWS // 2)

    def step(index, source, place_at, target):
        return copy(source, place_at, sends.at[index], recvs.at[index], target)

    def over():
        return step(0, own, out.at[here], across)

    def kept():
        return pltpu.make_async_copy(own, out.at[here], local_sem)

    def ring(base, source, block):
        def item(i):
            part = (front, back, back, front)[i]
            target = (y_up, y_down, y_up, y_down)[i]
            return step(base + i, source.at[part], out.at[block, part], target)

        return item

    def relays(base, which):
        below, above = ((y + 3) % 4) * 2 + which, ((y + 1) % 4) * 2 + which

        def item(i):
            place_at = (out.at[below, front], out.at[above, back])[i]
            return step(base + 4 + i, place_at, place_at, (y_up, y_down)[i])

        return item

    def first_ring():
        return ring(1, own, here)

    def second_ring():
        return ring(7, out.at[there], there)

    def start():
        @pl.when(holds)
        def _():
            kept().start()
            over().start()
            for i in range(4):
                first_ring()(i).start()

    def pass_first():
        @pl.when(holds)
        def _():
            for i in range(2):
                first_ring()(i).wait_recv()
                relays(1, zh)(i).start()
            over().wait_recv()
            for i in range(4):
                second_ring()(i).start()

    def pass_second():
        @pl.when(holds)
        def _():
            for i in range(2):
                second_ring()(i).wait_recv()
                relays(7, 1 - zh)(i).start()

    def end():
        @pl.when(holds)
        def _():
            rounds = ((first_ring(), relays(1, zh)), (second_ring(), relays(7, 1 - zh)))
            for direct, relayed in rounds:
                for i in (2, 3):
                    direct(i).wait_recv()
                for i in range(2):
                    relayed(i).wait_recv()
            over().wait_send()
            for direct, relayed in rounds:
                for i in range(4):
                    direct(i).wait_send()
                for i in range(2):
                    relayed(i).wait_send()
            kept().wait()

    return start, pass_first, pass_second, end


def across_device():
    c, z, x = place()
    r = lax.axis_index("replica")
    return {"section": c, "shard": z * 4 + x, "replica": (r // 2) * 2 + 1 - r % 2}


def home_beside(layer, wide_sum, summed, own, second_refs, home_refs):
    c, z, x = place()
    friends = [at(c, z, (x + 2) % 4)] + [at(1 - c, z, (x + dx) % 4) for dx in (1, 2, 3)]
    friends += [at(1 - c, 1 - z, x)] + list(grid_place()[2])
    home, arrived, end = home_stages(layer, summed, own, *home_refs)
    rings = []

    def begin():
        for k in range(2):
            rings.append(rings_second(k, wide_sum, summed, *second_refs))

    def first():
        for ring in rings:
            ring[0]()

    def second():
        for ring in rings:
            ring[1]()
        home()

    def finish():
        arrived()
        end()

    return friends, begin, first, second, finish


def spread_beside(layer, own, out, refs):
    start, pass_first, pass_second, end = spread_stages(layer, own, out, *refs)
    friends = list(grid_place()[2][:2]) + [across_device()]
    return friends, start, pass_first, pass_second, end


def reduce_kernel(pieces, out, wide_sum, summed, own, *refs):
    c, z, x = place()
    greet(list(grid_place()[2]) + [across_device(), at(1 - c, 1 - z, x)] + team_mates())
    first_refs, second_refs, home_refs, spread_refs = refs[:5], refs[5:10], refs[10:13], refs[13:]
    middle, y_last, z_last = rings_first(pieces, wide_sum, *first_refs)
    middle()
    y_last()
    rings = [rings_second(0, wide_sum, summed, *second_refs)]
    z_last()
    rings.append(rings_second(1, wide_sum, summed, *second_refs))
    for ring in rings:
        ring[0]()
    for ring in rings:
        ring[1]()
    for stage in home_stages(0, summed, own, *home_refs):
        stage()
    for stage in spread_stages(0, own, out, *spread_refs):
        stage()


def reduce_grads(pieces):
    return pl.pallas_call(
        reduce_kernel,
        out_shape=jax.ShapeDtypeStruct((8, GOT_ROWS, 128), BF),
        in_specs=[VMEM],
        out_specs=VMEM,
        scratch_shapes=[
            pltpu.VMEM(WIDE, BF),
            pltpu.VMEM((ROWS, 128), BF),
            pltpu.VMEM((GOT_ROWS, 128), BF),
        ]
        + first_scratch()
        + second_scratch()
        + home_scratch()
        + spread_scratch(),
        compiler_params=pltpu.CompilerParams(
            collective_id=4, has_side_effects=True, vmem_limit_bytes=LIMIT
        ),
    )(pieces)


def shared_kernel(*refs):
    attended, middle_low, normed_all, qkv_grad, normed, last_grad, vectors, rows = refs[:8]
    refs = refs[8:]
    out, out_rows, products, last_keys, last_queries, parts, *refs = refs
    home_send, home_recv, home_local, *scatter_refs = refs
    c, z, x = place()
    products[...] = dot_tn(attended[...], middle_low[...])
    last_keys[...] = dot_tn(normed_all[...], qkv_grad[:, 384:512])
    last_queries[...] = dot_tn(normed[...], last_grad[...])
    for j in range(8):
        block = pl.ds(136 * j, 136)

        def stack(value, lanes):
            tail = vectors[j, :, lanes]
            return jnp.concatenate([value, tail], axis=0).astype(BF)

        if j < 7:
            product = products[block, :]
        else:
            product = jnp.concatenate(
                [products[952:1024, :], products[1088:1152, :]], axis=0
            )
        parts[j, :, 0:128] = stack(last_keys[block, :], pl.ds(0, 128))
        parts[j, :, 128:1152] = stack(product[:, 0:1024], pl.ds(128, 1024))
        parts[j, :, 1152:1280] = stack(
            product[:, 1024:1152] + last_queries[block, :], pl.ds(1152, 128)
        )

    def same_layer():
        return pltpu.make_async_remote_copy(
            src_ref=rows.at[c],
            dst_ref=out_rows.at[z],
            send_sem=home_send.at[0],
            recv_sem=home_recv.at[0],
            device_id=at(c, 1 - z, x),
            device_id_type=MESH,
        )

    def same_here():
        return pltpu.make_async_copy(rows.at[c], out_rows.at[z], home_local)

    def other_layer(t):
        return pltpu.make_async_remote_copy(
            src_ref=rows.at[1 - c],
            dst_ref=out_rows.at[z],
            send_sem=home_send.at[1],
            recv_sem=home_recv.at[1 + t],
            device_id=at(1 - c, c, x),
            device_id_type=MESH,
        )

    def begin():
        @pl.when(z == c)
        def _():
            same_here().start()

        @pl.when(z != c)
        def _():
            same_layer().start()

        other_layer(z).start()

    def end():
        @pl.when(z == c)
        def _():
            same_here().wait()
            same_layer().wait_recv()

        @pl.when(z != c)
        def _():
            other_layer(0).wait_recv()
            other_layer(1).wait_recv()
            same_layer().wait_send()

        other_layer(z).wait_send()

    friends = [at(c, 1 - z, x), at(1 - c, 1 - z, x)]
    def mine_part(where, part):
        return parts[c * 4 + where, part, :].astype(F32)

    scatter_core(
        64,
        lambda where: parts.at[(1 - c) * 4 + where],
        mine_part,
        lambda where: None,
        (friends, begin, nothing, nothing, end),
        out,
        *scatter_refs,
    )


def shared_scatter(*operands):
    dma = pltpu.SemaphoreType.DMA
    return pl.pallas_call(
        shared_kernel,
        out_shape=(
            jax.ShapeDtypeStruct((144, 1280), F32),
            jax.ShapeDtypeStruct((2, 128, D), BF),
        ),
        in_specs=[VMEM] * 8,
        out_specs=(VMEM, VMEM),
        scratch_shapes=[
            pltpu.VMEM((1152, 1152), F32),
            pltpu.VMEM((D, 128), F32),
            pltpu.VMEM((D, 128), F32),
            pltpu.VMEM((8, 144, 1280), BF),
            dma((2,)),
            dma((3,)),
            dma,
        ]
        + scatter_scratch(144, 1280, 64),
        compiler_params=pltpu.CompilerParams(
            collective_id=6, has_side_effects=True, vmem_limit_bytes=LIMIT
        ),
    )(*operands)


def segments(start, size, piece_rows):
    done = 0
    while done < size:
        piece, row = divmod(start + done, piece_rows)
        count = min(piece_rows - row, size - done)
        yield piece, row, done, count
        done += count


def pieces_kernel(
    normed_all, qkv_grad, second_all, up_grad, activated, low_all, shared, out, wide, tall
):
    wide[:, 896:1024] = jnp.zeros((D, 128), F32)
    wide[:, 0:384] = dot_tn(normed_all[...], qkv_grad[:, 0:384])
    wide[:, 384:928] = dot_tn(second_all[...], up_grad[...])
    blank = jnp.zeros((8, 128), F32)
    for chunk in range(8):
        for j in range(8):
            block = wide[136 * j : 136 * j + 136, 128 * chunk : 128 * chunk + 128]
            place_at = pl.ds((j % 4) * 144, 144)
            out[chunk // 2, (chunk % 2) * 2 + j // 4, place_at, :] = jnp.concatenate(
                [block, blank], axis=0
            ).astype(BF)
    tall[:, 1024:1152] = jnp.zeros((544, 128), F32)
    tall[:, 0:D] = dot_tn(activated[...], low_all[...])

    def put(base, piece_rows, start, value):
        for piece, row, at_row, count in segments(start, value.shape[0], piece_rows):
            out[piece // 4, piece % 4, base + row : base + row + count, :] = value[
                at_row : at_row + count
            ].astype(BF)

    for k in range(9):
        put(SPLIT_ROWS, DOWN_ROWS, 544 * k, tall[:, 128 * k : 128 * k + 128])
    put(SPLIT_ROWS, DOWN_ROWS, 9 * 544, jnp.zeros((16 * DOWN_ROWS - 9 * 544, 128), F32))
    base = SPLIT_ROWS + DOWN_ROWS
    for k in range(10):
        put(base, SHARED_ROWS, 144 * k, shared[:, 128 * k : 128 * k + 128])
    put(base, SHARED_ROWS, 1440, jnp.zeros((16 * SHARED_ROWS - 1440, 128), F32))


def grad_pieces(*operands):
    return pl.pallas_call(
        pieces_kernel,
        out_shape=jax.ShapeDtypeStruct((4, 4, ROWS, 128), BF),
        in_specs=[VMEM] * 7,
        out_specs=VMEM,
        scratch_shapes=[pltpu.VMEM((D, 1024), F32), pltpu.VMEM((544, 1152), F32)],
        compiler_params=pltpu.CompilerParams(vmem_limit_bytes=LIMIT),
    )(*operands)


def assemble_kernel(
    first_got, second_got, qkv, out_w, up, down, vectors, shared, got, got_sem
):
    c = lax.axis_index("section")

    @pl.when(c == 0)
    def _():
        pltpu.make_async_copy(first_got, got, got_sem).start()

    @pl.when(c == 1)
    def _():
        pltpu.make_async_copy(second_got, got, got_sem).start()

    @pl.when(c == 0)
    def _():
        pltpu.make_async_copy(first_got, got, got_sem).wait()

    @pl.when(c == 1)
    def _():
        pltpu.make_async_copy(second_got, got, got_sem).wait()

    for q in range(8):
        for chunk in range(8):
            block = got[chunk, 144 * q : 144 * q + 144, :].astype(F32)[:136]
            if chunk < 3:
                start = chunk * D + 128 * q
                qkv[:, start : start + 128] = block
            elif chunk < 7:
                start = 544 * q + 128 * (chunk - 3)
                up[:, start : start + 128] = block
            else:
                up[:, 544 * q + 512 : 544 * q + 544] = block[:, :32]
    for k in range(9):
        width = 128 if k < 8 else 64
        for piece, row, at_row, count in segments(544 * k, 544, DOWN_ROWS):
            start = 8 * 144 + (piece % 2) * OWN_ROWS + row
            block = got[piece // 2, start : start + count, :].astype(F32)
            down[at_row : at_row + count, 128 * k : 128 * k + width] = block[:, :width]
    for k in range(10):
        for piece, row, at_row, count in segments(144 * k, 144, SHARED_ROWS):
            start = 8 * 144 + (piece % 2) * OWN_ROWS + DOWN_ROWS + row
            block = got[piece // 2, start : start + count, :].astype(F32)
            shared[k, at_row : at_row + count, :] = block
        vectors[:, 128 * k : 128 * k + 128] = shared[k, 136:144, :]
        if 1 <= k < 9:
            out_w[:, 128 * (k - 1) : 128 * k] = shared[k, 0:136, :]
    out_w[:, 1024:D] = shared[9, 0:136, 0:64]
    qkv[:, 1024:D] = shared[9, 0:136, 64:128]
    qkv[:, D + 1024 : 2 * D] = shared[0, 0:136, 0:64]
    qkv[:, 2 * D + 1024 : 3 * D] = shared[0, 0:136, 64:128]


def assemble(first_got, second_got):
    shapes = ((136, 3 * D), (136, D), (136, FF), (544, D), (8, 1280))
    return pl.pallas_call(
        assemble_kernel,
        out_shape=tuple(jax.ShapeDtypeStruct(shape, F32) for shape in shapes),
        in_specs=[pl.BlockSpec(memory_space=pl.ANY)] * 2,
        out_specs=(VMEM,) * 5,
        scratch_shapes=[
            pltpu.VMEM((10, 144, 128), F32),
            pltpu.VMEM((8, GOT_ROWS, 128), BF),
            pltpu.SemaphoreType.DMA,
        ],
        compiler_params=pltpu.CompilerParams(vmem_limit_bytes=LIMIT),
    )(first_got, second_got)


def dot_nt(left, right):
    return lax.dot_general(left, right, (((1,), (1,)), ((), ())), preferred_element_type=F32)


def dot_tn(left, right):
    return lax.dot_general(left, right, (((0,), (0,)), ((), ())), preferred_element_type=F32)


def dot(left, right):
    return jnp.dot(left, right, preferred_element_type=F32)


def lane_half(block, which):
    lane = lax.broadcasted_iota(jnp.int32, block.shape, 1)
    keep = lane < 64 if which == 0 else lane >= 64
    return jnp.where(keep, block, jnp.zeros_like(block))


def softmax_rows(scores, start):
    row = lax.broadcasted_iota(jnp.int32, scores.shape, 0) + start
    key = lax.broadcasted_iota(jnp.int32, scores.shape, 1)
    masked = jnp.where(key <= row, scores, NEG_FILL)
    shifted = jnp.exp(masked - jnp.max(masked, axis=1, keepdims=True))
    return shifted * (1.0 / jnp.sum(shifted, axis=1, keepdims=True))


STEP = 256


def team_mates():
    c, z, x = place()
    return [at((c + dc) % 2, z, (x + dx) % 4) for dc, dx in TEAM_STEPS]


def lanes_of(q):
    return pl.ds(pl.multiple_of(q * 128, 128), 128)


def attend_kernel(projected, last_query, out, attended, send_sems, recv_sems, local_sem):
    c, z, x = place()
    me = c * 4 + x
    mates = team_mates()
    arrive(mates)

    def copy_to(q):
        return pltpu.make_async_remote_copy(
            src_ref=attended.at[q],
            dst_ref=out.at[:, lanes_of(me)],
            send_sem=send_sems.at[q],
            recv_sem=recv_sems.at[me],
            device_id=at(q // 4, z, q % 4),
            device_id_type=MESH,
        )

    def copy_from(q):
        return pltpu.make_async_remote_copy(
            src_ref=attended.at[q],
            dst_ref=out.at[:, lanes_of(q)],
            send_sem=send_sems.at[q],
            recv_sem=recv_sems.at[q],
            device_id=at(q // 4, z, q % 4),
            device_id_type=MESH,
        )

    def keep(q):
        return pltpu.make_async_copy(attended.at[q], out.at[:, lanes_of(q)], local_sem)

    both = projected[:, 384:512]
    soft = softmax_rows(dot_nt(last_query[...] * 0.125, both), me * 128).astype(BF)
    out[:, 1024:1152] = dot(soft, lane_half(both, 1)).astype(BF)
    for start in range(0, 1024, STEP):
        size = start + STEP
        query = projected[start:size, 0:128] * 0.125
        total = jnp.zeros((STEP, 128), F32)
        for head in range(2):
            keys = lane_half(projected[0:size, 128:256], head)
            values = lane_half(projected[0:size, 256:384], head)
            soft = softmax_rows(dot_nt(query, keys), start).astype(BF)
            total = total + dot(soft, values)
        if start == 0:
            meet(mates)
        for q in range(start // 128, size // 128):
            begin = q * 128 - start
            attended[q] = total[begin : begin + 128].astype(BF)

            @pl.when(me == q)
            def _():
                keep(q).start()

            @pl.when(me != q)
            def _():
                copy_to(q).start()

    for q in range(8):

        @pl.when(me == q)
        def _():
            keep(q).wait()

        @pl.when(me != q)
        def _():
            copy_from(q).wait_recv()
            copy_to(q).wait_send()


def attend(projected, last_query):
    return pl.pallas_call(
        attend_kernel,
        out_shape=jax.ShapeDtypeStruct((128, 1152), BF),
        in_specs=[VMEM, VMEM],
        out_specs=VMEM,
        scratch_shapes=[
            pltpu.VMEM((8, 128, 128), BF),
            pltpu.SemaphoreType.DMA((8,)),
            pltpu.SemaphoreType.DMA((8,)),
            pltpu.SemaphoreType.DMA,
        ],
        compiler_params=pltpu.CompilerParams(
            collective_id=1, has_side_effects=True, vmem_limit_bytes=LIMIT
        ),
    )(projected, last_query)


def attend_back_kernel(
    projected,
    last_query,
    rows,
    out,
    out_last,
    grad,
    key_total,
    value_total,
    send_sems,
    recv_sems,
    local_sem,
):
    c, z, x = place()
    me = c * 4 + x
    mates = team_mates()
    arrive(mates)
    local = pltpu.make_async_copy(rows.at[:, lanes_of(me)], grad.at[row_block(me)], local_sem)
    local.start()
    meet(mates)
    send = sender(send_sems, recv_sems)
    copies = []
    for index, (dc, dx) in enumerate(TEAM_STEPS):
        tc, tx = (c + dc) % 2, (x + dx) % 4
        copies.append(
            send(rows.at[:, lanes_of(tc * 4 + tx)], grad.at[row_block(me)], index, at(tc, z, tx))
        )
    key_total[...] = jnp.zeros_like(key_total)
    value_total[...] = jnp.zeros_like(value_total)
    both = projected[:, 384:512]
    query = last_query[...] * 0.125
    last_grad = rows[:, 1024:1152]
    soft = softmax_rows(dot_nt(query, both), me * 128)
    grad_soft = dot_nt(last_grad, both)
    inner = jnp.sum(soft * grad_soft, axis=1, keepdims=True)
    grad_scores = (soft * (grad_soft - inner)).astype(BF)
    out_last[...] = (dot(grad_scores, lane_half(both, 0)) * 0.125).astype(BF)
    out[:, 384:512] = (dot_tn(grad_scores, query) + dot_tn(soft.astype(BF), last_grad)).astype(BF)
    local.wait()
    for copy in copies:
        copy.wait_recv()
    for start in range(0, 1024, STEP):
        size = start + STEP
        query = projected[start:size, 0:128] * 0.125
        grad_rows = grad[start:size, :]
        total = jnp.zeros((STEP, 128), F32)
        for head in range(2):
            keys = lane_half(projected[0:size, 128:256], head)
            values = lane_half(projected[0:size, 256:384], head)
            soft = softmax_rows(dot_nt(query, keys), start)
            grad_soft = dot_nt(grad_rows, values)
            inner = jnp.sum(soft * grad_soft, axis=1, keepdims=True)
            grad_scores = (soft * (grad_soft - inner)).astype(BF)
            total = total + dot(grad_scores, keys)
            key_total[0:size, :] += dot_tn(grad_scores, lane_half(query, head))
            value_total[0:size, :] += dot_tn(soft.astype(BF), lane_half(grad_rows, head))
        out[start:size, 0:128] = (total * 0.125).astype(BF)
    out[:, 128:256] = key_total[...].astype(BF)
    out[:, 256:384] = value_total[...].astype(BF)
    for copy in copies:
        copy.wait_send()


def attend_back(projected, last_query, rows):
    return pl.pallas_call(
        attend_back_kernel,
        out_shape=(
            jax.ShapeDtypeStruct((1024, 512), BF),
            jax.ShapeDtypeStruct((128, 128), BF),
        ),
        in_specs=[VMEM] * 3,
        out_specs=(VMEM, VMEM),
        scratch_shapes=[
            pltpu.VMEM((1024, 128), BF),
            pltpu.VMEM((1024, 128), F32),
            pltpu.VMEM((1024, 128), F32),
            pltpu.SemaphoreType.DMA((7,)),
            pltpu.SemaphoreType.DMA((7,)),
            pltpu.SemaphoreType.DMA,
        ],
        compiler_params=pltpu.CompilerParams(
            collective_id=2, has_side_effects=True, vmem_limit_bytes=LIMIT
        ),
    )(projected, last_query, rows)


def norm_forward(hidden, gain, offset):
    center = hidden - jnp.mean(hidden, axis=-1, keepdims=True)
    inverse = lax.rsqrt(jnp.mean(center * center, axis=-1, keepdims=True) + EPSILON)
    unit = center * inverse
    return unit * gain + offset, unit, inverse


def norm_backward(grad_rows, unit, inverse, gain):
    grad_unit = grad_rows * gain
    grad_in = inverse * (
        grad_unit
        - jnp.mean(grad_unit, axis=-1, keepdims=True)
        - unit * jnp.mean(grad_unit * unit, axis=-1, keepdims=True)
    )
    return grad_in, jnp.sum(grad_rows * unit, axis=0), jnp.sum(grad_rows, axis=0)


def gelu_pair(values):
    tangent = jnp.tanh(GELU_C * (values + 0.044715 * values * values * values))
    output = 0.5 * values * (1.0 + tangent)
    slope = 0.5 * (1.0 + tangent) + 0.5 * values * (1.0 - tangent * tangent) * GELU_C * (
        1.0 + 3.0 * 0.044715 * values * values
    )
    return output, slope


def layer_forward(hidden, w):
    normed, unit_one, inverse_one = norm_forward(hidden, w["gain_one"], w["bias_one"])
    normed = normed.astype(BF)
    normed_all, projected = team_gather(
        gather_qkv_kernel,
        0,
        normed,
        w["qkv"],
        (w["qkv_bias"].reshape(1, 512),),
        (jax.ShapeDtypeStruct((1024, 512), BF),),
    )
    normed_all = normed_all.reshape(1024, D)
    last_query = (dot(normed, w["last_query"]) + w["last_bias"]).astype(BF)
    attended = attend(projected, last_query)
    packed = jnp.concatenate([attended[:, :1024], attended[:, 1088:]], axis=1)
    middle = hidden + dot(packed, w["out"]) + w["out_bias"]
    second, unit_two, inverse_two = norm_forward(middle, w["gain_two"], w["bias_two"])
    second_all, upper, activated = team_gather(
        gather_up_kernel,
        7,
        second.astype(BF),
        w["up"],
        (w["up_bias"].reshape(1, 544),),
        (jax.ShapeDtypeStruct((1024, 544), F32), jax.ShapeDtypeStruct((1024, 544), BF)),
    )
    second_all = second_all.reshape(1024, D)
    output = middle + product_scatter(dot, 5, activated, w["down"]) + w["down_bias"]
    saved = dict(
        normed=normed,
        normed_all=normed_all,
        unit_one=unit_one,
        inverse_one=inverse_one,
        projected=projected,
        last_query=last_query,
        attended=attended,
        unit_two=unit_two,
        inverse_two=inverse_two,
        second_all=second_all,
        upper=upper,
        activated=activated,
    )
    return output, saved


def layer_backward(grad_out, grad_low_all, w, kept, q, pieces):
    grad_low = grad_out.astype(BF)
    if grad_low_all is None:
        grad_low_all, up_grad, wide_sum = team_gather(
            gather_back_kernel,
            8,
            grad_low,
            w["down"],
            (kept["upper"], pieces),
            (jax.ShapeDtypeStruct((1024, 544), BF), jax.ShapeDtypeStruct(WIDE, BF)),
            first_scratch(),
        )
        grad_low_all = grad_low_all.reshape(1024, D)
        grad_second, own = product_scatter(dot_nt, 11, up_grad, w["up"], wide_sum)
    else:
        slope = gelu_pair(kept["upper"])[1]
        up_grad = (dot_nt(grad_low_all, w["down"]) * slope).astype(BF)
        grad_second, own = product_scatter(dot_nt, 9, up_grad, w["up"]), None
    grad_in, gain_two, bias_two = norm_backward(
        grad_second, kept["unit_two"], kept["inverse_two"], w["gain_two"]
    )
    grad_middle = grad_out + grad_in
    middle_low = grad_middle.astype(BF)
    attended_grad = dot_nt(middle_low, w["out"]).astype(BF)
    attended_grad = jnp.concatenate(
        [attended_grad[:, :1024], jnp.zeros((128, 64), BF), attended_grad[:, 1024:]], axis=1
    )
    qkv_grad, last_grad = attend_back(kept["projected"], kept["last_query"], attended_grad)
    if own is None:
        grad_normed, got = product_scatter(dot_nt, 10, qkv_grad, w["qkv"]), None
    else:
        grad_normed, got = product_scatter(dot_nt, 12, qkv_grad, w["qkv"], own)
    grad_normed = grad_normed + dot_nt(last_grad, w["last_query"])
    grad_in, gain_one, bias_one = norm_backward(
        grad_normed, kept["unit_one"], kept["inverse_one"], w["gain_one"]
    )
    grad_input = grad_middle + grad_in

    qkv_sums = jnp.sum(qkv_grad, axis=0, dtype=F32)
    last_sums = jnp.sum(last_grad, axis=0, dtype=F32)
    zeros = jnp.zeros((1024,), F32)
    qv = jnp.concatenate(
        [
            lax.dynamic_update_slice(zeros, qkv_sums[:128], (q * 128,)),
            last_sums[:64],
            lax.dynamic_update_slice(zeros, qkv_sums[256:384], (q * 128,)),
            qkv_sums[448:512],
        ]
    )
    up_sums = lax.dynamic_update_slice(
        jnp.zeros((FF,), F32), jnp.sum(up_grad, axis=0, dtype=F32), (q * 544,)
    )
    vectors = jnp.concatenate(
        [
            qv.reshape(8, 272),
            jnp.sum(middle_low, axis=0, dtype=F32).reshape(8, 136),
            gain_one.reshape(8, 136),
            bias_one.reshape(8, 136),
            gain_two.reshape(8, 136),
            bias_two.reshape(8, 136),
            up_sums.reshape(8, 544),
            jnp.sum(grad_low, axis=0, dtype=F32).reshape(8, 136),
        ],
        axis=1,
    )
    vectors = jnp.pad(vectors, ((0, 0), (0, 8 * 1280 - 1632))).reshape(8, 8, 1280)
    swapped_grad = jnp.concatenate([jnp.zeros((128, 64), BF), last_grad[:, :64]], axis=1)
    operands = (
        kept["attended"],
        jnp.pad(middle_low, ((0, 0), (0, 64))),
        kept["normed_all"],
        qkv_grad,
        kept["normed"],
        swapped_grad,
        vectors,
    )
    split = (
        kept["normed_all"],
        qkv_grad,
        kept["second_all"],
        up_grad,
        kept["activated"],
        grad_low_all,
    )
    return grad_input, operands, split, got


BOTH = ("section", "shard")


def pairs(route):
    out = []
    for c in range(2):
        for z in range(2):
            for x in range(4):
                tc, tz = route(c, z)
                out.append((c * 8 + z * 4 + x, tc * 8 + tz * 4 + x))
    return out


def local(
    inputs,
    cotangent,
    w_qkv,
    qv_bias,
    w_out,
    out_bias,
    gain_one,
    bias_one,
    gain_two,
    bias_two,
    w_up,
    up_bias,
    w_down,
    down_bias,
):
    c, z, x = place()
    q = c * 4 + x
    swap = [pair for pair in pairs(lambda a, b: (b, a)) if pair[0] != pair[1]]
    cross_back = pairs(lambda a, b: (b, 1 - a))

    def swapped(array):
        return jnp.where(c == z, array, lax.ppermute(array, BOTH, swap))

    def by_z(own, other):
        return jnp.where(z == 0, own, other), jnp.where(z == 0, other, own)

    small = jnp.concatenate(
        [
            qv_bias[0],
            up_bias[0],
            out_bias[0],
            gain_one[0],
            bias_one[0],
            gain_two[0],
            bias_two[0],
            down_bias[0],
        ]
    )
    own_qkv = w_qkv[0]
    last_cols = [own_qkv[:, part * D + 1024 : (part + 1) * D] for part in range(3)]
    common = jnp.concatenate(
        [
            jnp.concatenate(
                [last_cols[1], last_cols[2], last_cols[0], jnp.zeros((136, 64), BF)], axis=1
            ),
            jnp.pad(small, (0, 2048 - 1632)).reshape(8, 256),
        ]
    )
    blocks = jnp.concatenate(
        [own_qkv[:, part * D : part * D + 1024].reshape(136, 8, 128) for part in range(3)]
        + [w_up[0].reshape(136, 8, 544)],
        axis=2,
    ).transpose(1, 0, 2)
    blocks = jnp.pad(blocks, ((0, 0), (0, 8), (0, 0)))
    replica = lax.axis_index("replica")
    late = lax.dynamic_slice(
        jnp.pad(blocks, ((0, 0), (0, 0), (0, 96))), (0, 0, replica * 128), (8, 144, 128)
    )
    first_blocks, late, all_common, hidden, top_grad = spread_weights(
        late, common, inputs[:, 0], cotangent[:, 0]
    )
    own_out = lax.all_gather(w_out[0], "shard", axis=0, tiled=True)
    teams = [[a * 8 + b * 4 + d for a in range(2) for d in range(4)] for b in range(2)]
    top_grad_all = lax.all_gather(top_grad, BOTH, axis_index_groups=teams, axis=0, tiled=True)
    second_blocks = lax.all_gather(late, "replica", axis=0)
    partner_out = lax.ppermute(own_out, "section", [(0, 1), (1, 0)])
    all_out = (
        jnp.where(c == 0, own_out, partner_out),
        jnp.where(c == 0, partner_out, own_out),
    )
    cuts = (
        first_blocks.reshape(4, 2, 2, 4, 144, 128)
        .transpose(2, 3, 4, 0, 1, 5)[:, :, :136]
        .reshape(D, 1024)[:, :928],
        second_blocks.transpose(1, 2, 0, 3)[:, :136].reshape(D, 1024)[:, :928],
    )
    down_own = swapped(w_down[0])
    down_other = lax.ppermute(w_down[0], BOTH, cross_back)
    all_down = by_z(down_own, down_other)

    def layer_weights(layer):
        cut = cuts[layer]
        shared = all_common[layer, :, :136].reshape(D, 256)
        vec = all_common[layer, :, 136:].reshape(8, 2048)[:, :1632].astype(F32)

        def piece(start, size):
            return vec[:, start : start + size].reshape(-1)

        qv = piece(0, 272)
        six = vec[:, 816:].reshape(8, 6, 136).transpose(1, 0, 2).reshape(6, D)
        six = lax.optimization_barrier(six)
        none = jnp.zeros((128,), F32)
        qkv_bias = jnp.concatenate(
            [
                lax.dynamic_slice(qv, (q * 128,), (128,)),
                none,
                lax.dynamic_slice(qv, (D + q * 128,), (128,)),
                none[:64],
                qv[2 * D - 64 :],
            ]
        )
        return dict(
            qkv=jnp.concatenate([cut[:, :384], shared[:, :128]], axis=1),
            last_query=shared[:, 128:],
            qkv_bias=qkv_bias,
            last_bias=jnp.concatenate([qv[1024:D], none[:64]]),
            out=all_out[layer],
            out_bias=six[0:1],
            gain_one=six[1:2],
            bias_one=six[2:3],
            gain_two=six[3:4],
            bias_two=six[4:5],
            up=cut[:, 384:],
            up_bias=lax.dynamic_slice(piece(272, 544), (q * 544,), (544,)),
            down=all_down[layer],
            down_bias=six[5:6],
        )

    weights = [layer_weights(0), layer_weights(1)]
    hidden = hidden.astype(F32)
    top_grad = top_grad.astype(F32)
    out_first, kept_first = layer_forward(hidden, weights[0])
    out_second, kept_second = layer_forward(out_first.astype(BF).astype(F32), weights[1])
    grad_second, operands, split, _ = layer_backward(
        top_grad, top_grad_all, weights[1], kept_second, q, None
    )
    rows = jnp.stack([out_first.astype(BF), out_second.astype(BF)])
    shared, section_out = shared_scatter(*operands, rows)
    pieces = grad_pieces(*split, shared)
    grad_first, operands, split, second_got = layer_backward(
        grad_second.astype(BF).astype(F32), None, weights[0], kept_first, q, pieces
    )
    rows = jnp.stack([grad_first.astype(BF), grad_second.astype(BF)])
    shared, input_grad = shared_scatter(*operands, rows)
    first_got = reduce_grads(grad_pieces(*split, shared))
    grad_qkv, grad_out_w, grad_up, grad_down, vectors = assemble(first_got, second_got)
    section_out = section_out.astype(F32)[None, :, None]
    input_grad = input_grad.astype(F32)[None, :, None]
    vec = vectors.reshape(-1)
    grads = (
        grad_qkv,
        vec[:272],
        grad_out_w,
        vec[272:408],
        vec[408:544],
        vec[544:680],
        vec[680:816],
        vec[816:952],
        grad_up,
        vec[952:1496],
        grad_down,
        vec[1496:1632],
    )
    return (section_out, input_grad) + tuple(grad[None] for grad in grads)


def solution(mesh):
    return jax.shard_map(
        local,
        mesh=mesh,
        in_specs=(
            P(None, "replica", "shard", None),
            P(None, "replica", "shard", None),
            P("section", "shard", None),
            P("section", "shard"),
            P("section", "shard", None),
            P("section", "shard"),
            P("section", "shard"),
            P("section", "shard"),
            P("section", "shard"),
            P("section", "shard"),
            P("section", "shard", None),
            P("section", "shard"),
            P("section", "shard", None),
            P("section", "shard"),
        ),
        out_specs=(
            P("section", None, "replica", "shard", None),
            P("section", None, "replica", "shard", None),
            P("section", "shard", None),
            P("section", "shard"),
            P("section", "shard", None),
            P("section", "shard"),
            P("section", "shard"),
            P("section", "shard"),
            P("section", "shard"),
            P("section", "shard"),
            P("section", "shard", None),
            P("section", "shard"),
            P("section", "shard", None),
            P("section", "shard"),
        ),
        check_vma=False,
    )
```

```python
import functools

import jax
import jax.numpy as jnp
from jax import lax
from jax.experimental import pallas as pl
from jax.experimental.pallas import tpu as pltpu
from jax.sharding import PartitionSpec as P

D = 1088
FF = 4352
HEAD_DIM = 64
EPSILON = 1e-05
GELU_C = 0.7978845608028654
NEG_FILL = -1e30
BF = jnp.bfloat16
F32 = jnp.float32
MESH = pl.DeviceIdType.MESH
VMEM = pl.BlockSpec(memory_space=pltpu.VMEM)
LIMIT = 56 * 1024 * 1024


def place():
    c = lax.axis_index("section")
    j = lax.axis_index("shard")
    return c, j // 4, j % 4


def at(c, z, x):
    return {"section": c, "shard": z * 4 + x}


def arrive(devices):
    barrier = pltpu.get_barrier_semaphore()
    for device in devices:
        pl.semaphore_signal(barrier, inc=1, device_id=device, device_id_type=MESH)


def meet(devices):
    pl.semaphore_wait(pltpu.get_barrier_semaphore(), len(devices))


def greet(devices):
    arrive(devices)
    meet(devices)


def nothing():
    pass


ALONE = ([], nothing, nothing, nothing, nothing)


def sender(send_sems, recv_sems):
    def make(src, dst, index, device):
        copy = pltpu.make_async_remote_copy(
            src_ref=src,
            dst_ref=dst,
            send_sem=send_sems.at[index],
            recv_sem=recv_sems.at[index],
            device_id=device,
            device_id_type=MESH,
        )
        copy.start()
        return copy

    return make


def gather_core(own, out, send_sems, recv_sems, local_sem, use, beside=ALONE):
    c, z, x = place()
    ahead, behind, far = (x + 1) % 4, (x + 3) % 4, (x + 2) % 4
    partner, up, down = at(1 - c, z, x), at(c, z, ahead), at(c, z, behind)
    rows = own.shape[0]
    first, second = pl.ds(0, rows // 2), pl.ds(rows // 2, rows // 2)
    me, other = c * 4 + x, (1 - c) * 4
    local = pltpu.make_async_copy(own, out.at[me], local_sem)
    local.start()
    friends = [partner, up, down] + beside[0]
    arrive(friends)
    local.wait()
    meet(friends)
    send = sender(send_sems, recv_sems)
    to_up = send(own.at[first], out.at[me, first], 0, up)
    to_down = send(own.at[second], out.at[me, second], 1, down)
    to_partner = send(own, out.at[me], 2, partner)
    up_rest = send(own.at[second], out.at[me, second], 3, up)
    down_rest = send(own.at[first], out.at[me, first], 4, down)
    from_down, from_up, from_far = c * 4 + behind, c * 4 + ahead, c * 4 + far
    beside[1]()
    use(me)
    to_up.wait_recv()
    pass_up = send(out.at[from_down, first], out.at[from_down, first], 5, up)
    to_down.wait_recv()
    pass_down = send(out.at[from_up, second], out.at[from_up, second], 6, down)
    to_partner.wait_recv()
    use(other + x)
    up_rest.wait_recv()
    share_down = send(out.at[from_down], out.at[from_down], 7, partner)
    down_rest.wait_recv()
    share_up = send(out.at[from_up], out.at[from_up], 8, partner)
    use(from_down)
    use(from_up)
    beside[2]()
    pass_up.wait_recv()
    share_first = send(out.at[from_far, first], out.at[from_far, first], 9, partner)
    pass_down.wait_recv()
    share_second = send(out.at[from_far, second], out.at[from_far, second], 10, partner)
    use(from_far)
    beside[3]()
    share_down.wait_recv()
    use(other + behind)
    share_up.wait_recv()
    use(other + ahead)
    share_first.wait_recv()
    share_second.wait_recv()
    use(other + far)
    for copy in (
        to_up,
        to_down,
        to_partner,
        up_rest,
        down_rest,
        pass_up,
        pass_down,
        share_down,
        share_up,
        share_first,
        share_second,
    ):
        copy.wait_send()
    beside[4]()


def row_block(q):
    return pl.ds(pl.multiple_of(q * 128, 128), 128)


def gather_qkv_kernel(
    own, blocks, common, bias, out, projected, weight, send_sems, recv_sems, local_sem, wide
):
    def build():
        for j in range(8):
            rows = slice(136 * j, 136 * j + 136)
            for part in range(3):
                wide[rows, 128 * part : 128 * part + 128] = blocks[part, j].astype(F32)[:136]
            wide[rows, 384:512] = common[j, :, 0:128].astype(F32)[:136]
        weight[...] = wide[...].astype(BF)

    def use(q):
        projected[row_block(q), :] = (dot(out[q], weight[...]) + bias[...]).astype(BF)

    beside = ([], build, nothing, nothing, nothing)
    gather_core(own, out, send_sems, recv_sems, local_sem, use, beside)


def gather_up_kernel(
    own, blocks, bias, out, upper, activated, weight, send_sems, recv_sems, local_sem, wide
):
    def build():
        for j in range(8):
            for part in range(5):
                wide[136 * j : 136 * j + 136, 128 * part : 128 * part + 128] = blocks[
                    3 + part, j
                ].astype(F32)[:136]
        weight[...] = wide[:, 0:544].astype(BF)

    def use(q):
        values = dot(out[q], weight[...]) + bias[...]
        upper[row_block(q), :] = values
        activated[row_block(q), :] = gelu_pair(values)[0].astype(BF)

    beside = ([], build, nothing, nothing, nothing)
    gather_core(own, out, send_sems, recv_sems, local_sem, use, beside)


def gather_back_kernel(
    own, weight, upper, pieces, out, up_grad, wide_sum, send_sems, recv_sems, local_sem, *rings
):
    def use(q):
        slope = gelu_pair(upper[row_block(q), :])[1]
        up_grad[row_block(q), :] = (dot_nt(out[q], weight[...]) * slope).astype(BF)

    stages = []

    def begin():
        stages.extend(rings_first(pieces, wide_sum, *rings))

    def end():
        stages[1]()
        stages[2]()

    gather_core(
        own,
        out,
        send_sems,
        recv_sems,
        local_sem,
        use,
        (
            list(grid_place()[2]),
            begin,
            nothing,
            lambda: stages[0](),
            end,
        ),
    )


def team_gather(kernel, collective_id, own, weight, rest, results, scratch=()):
    rows, columns = own.shape
    return pl.pallas_call(
        kernel,
        out_shape=(jax.ShapeDtypeStruct((8, rows, columns), BF),) + results,
        in_specs=[VMEM] * (2 + len(rest)),
        out_specs=(VMEM,) * (1 + len(results)),
        scratch_shapes=[
            pltpu.SemaphoreType.DMA((11,)),
            pltpu.SemaphoreType.DMA((11,)),
            pltpu.SemaphoreType.DMA,
        ]
        + list(scratch),
        compiler_params=pltpu.CompilerParams(
            collective_id=collective_id, has_side_effects=True, vmem_limit_bytes=LIMIT
        ),
    )(own, weight, *rest)


def scatter_core(
    half,
    other_part,
    mine_part,
    prepare,
    beside,
    out,
    from_partner,
    far_sum,
    up_sum,
    down_sum,
    far_first,
    far_second,
    got_down,
    got_up,
    send_sems,
    recv_sems,
):
    c, z, x = place()
    ahead, behind, far = (x + 1) % 4, (x + 3) % 4, (x + 2) % 4
    partner, up, down = at(1 - c, z, x), at(c, z, ahead), at(c, z, behind)
    rows = out.shape[0]
    first, second = pl.ds(0, half), pl.ds(half, rows - half)
    send = sender(send_sems, recv_sems)
    friends = [partner, up, down] + beside[0]
    arrive(friends)
    order = (far, ahead, behind, x)
    parts = [other_part(where) for where in order]
    meet(friends)
    swaps = [
        send(part, from_partner.at[where], index, partner)
        for index, (where, part) in enumerate(zip(order, parts))
    ]
    beside[1]()
    for where in (far, ahead, behind, x):
        prepare(where)
    swap_far, swap_up, swap_down, swap_own = swaps

    def both(where, part):
        return mine_part(where, part) + from_partner[where, part, :].astype(F32)

    swap_far.wait_recv()
    far_sum[first, :] = both(far, first).astype(BF)
    far_up = send(far_sum.at[first], far_first, 4, up)
    far_sum[second, :] = both(far, second).astype(BF)
    far_down = send(far_sum.at[second], far_second, 5, down)
    swap_up.wait_recv()
    up_sum[second, :] = both(ahead, second).astype(BF)
    up_second = send(up_sum.at[second], got_down.at[second], 6, up)
    swap_down.wait_recv()
    down_sum[first, :] = both(behind, first).astype(BF)
    down_first = send(down_sum.at[first], got_up.at[first], 7, down)
    beside[2]()
    far_up.wait_recv()
    up_sum[first, :] = (both(ahead, first) + far_first[...].astype(F32)).astype(BF)
    up_first = send(up_sum.at[first], got_down.at[first], 8, up)
    far_down.wait_recv()
    down_sum[second, :] = (both(behind, second) + far_second[...].astype(F32)).astype(BF)
    down_second = send(down_sum.at[second], got_up.at[second], 9, down)
    swap_own.wait_recv()
    out[first, :] = both(x, first)
    out[second, :] = both(x, second)
    beside[3]()
    up_second.wait_recv()
    up_first.wait_recv()
    down_first.wait_recv()
    down_second.wait_recv()
    out[...] = out[...] + got_down[...].astype(F32) + got_up[...].astype(F32)
    for copy in (
        swap_far,
        swap_up,
        swap_down,
        swap_own,
        far_up,
        far_down,
        up_second,
        down_first,
        up_first,
        down_second,
    ):
        copy.wait_send()
    beside[4]()


def product_scatter_kernel(product, task, left, right, *refs):
    c, z, x = place()
    beside = ALONE
    if task == "home":
        wide_sum, out, own, other, mine, *refs = refs
        refs, summed, more = refs[:10], refs[10], refs[11:]
        beside = home_beside(1, wide_sum, summed, own, more[:5], more[5:])
    elif task == "spread":
        own, out, got, other, mine, *refs = refs
        refs, more = refs[:10], refs[10:]
        beside = spread_beside(1, own, got, more)
    else:
        out, other, mine, *refs = refs

    def other_part(where):
        rows = left[row_block((1 - c) * 4 + where), :]
        other[where] = product(rows, right[...]).astype(BF)
        return other.at[where]

    def prepare(where):
        mine[where] = product(left[row_block(c * 4 + where), :], right[...])

    scatter_core(
        64, other_part, lambda where, part: mine[where, part, :], prepare, beside, out, *refs
    )


def scatter_scratch(rows, columns, half):
    block = pltpu.VMEM((rows, columns), BF)
    return [
        pltpu.VMEM((4, rows, columns), BF),
        block,
        block,
        block,
        pltpu.VMEM((half, columns), BF),
        pltpu.VMEM((rows - half, columns), BF),
        block,
        block,
        pltpu.SemaphoreType.DMA((10,)),
        pltpu.SemaphoreType.DMA((10,)),
    ]


def product_scatter(product, collective_id, left, right, extra=None):
    out_shape = (jax.ShapeDtypeStruct((128, D), F32),)
    operands = (left, right)
    task, scratch = "", []
    if extra is not None:
        operands += (extra,)
        if extra.shape == WIDE:
            task = "home"
            out_shape += (jax.ShapeDtypeStruct((GOT_ROWS, 128), BF),)
            scratch = [pltpu.VMEM((ROWS, 128), BF)] + second_scratch() + home_scratch()
        else:
            task = "spread"
            out_shape += (jax.ShapeDtypeStruct((8, GOT_ROWS, 128), BF),)
            scratch = spread_scratch()
    out = pl.pallas_call(
        functools.partial(product_scatter_kernel, product, task),
        out_shape=out_shape,
        in_specs=[VMEM] * len(operands),
        out_specs=(VMEM,) * len(out_shape),
        scratch_shapes=[pltpu.VMEM((4, 128, D), BF), pltpu.VMEM((4, 128, D), F32)]
        + scatter_scratch(128, D, 64)
        + scratch,
        compiler_params=pltpu.CompilerParams(
            collective_id=collective_id, has_side_effects=True, vmem_limit_bytes=LIMIT
        ),
    )(*operands)
    return out[0] if extra is None else out


TEAM_STEPS = tuple((dc, dx) for dc in range(2) for dx in range(4) if dc or dx)


def ring_spread(send, base, source, block, me, up, down, first, second):
    before, after = (me + 3) % 4, (me + 1) % 4
    copies = [
        send(source(first), block(me, first), base, up),
        send(source(second), block(me, second), base + 1, down),
        send(source(second), block(me, second), base + 2, up),
        send(source(first), block(me, first), base + 3, down),
    ]

    def middle():
        copies[0].wait_recv()
        copies.append(send(block(before, first), block(before, first), base + 4, up))
        copies[1].wait_recv()
        copies.append(send(block(after, second), block(after, second), base + 5, down))

    def last():
        for copy in copies[2:]:
            copy.wait_recv()

    return copies, middle, last


def weights_kernel(
    late,
    common,
    rows,
    other_rows,
    first,
    second,
    out_common,
    out_rows,
    out_other,
    send_sems,
    recv_sems,
    common_send,
    common_recv,
    share_send,
    share_recv,
    ring_send,
    ring_recv,
    swap_send,
    swap_recv,
    local_sems,
):
    c, z, x = place()
    r = lax.axis_index("replica")
    y, zh = r // 2, r % 2
    zf = zh * 2 + z
    slot = z * 4 + x

    def device(ty, tz):
        return {"section": c, "shard": (tz % 2) * 4 + x, "replica": ty * 2 + tz // 2}

    y_up, y_down = device((y + 1) % 4, zf), device((y + 3) % 4, zf)
    z_up, z_down = device(y, (zf + 1) % 4), device(y, (zf + 3) % 4)
    z_other = device(y, (zf + 3 + 2 * z) % 4)
    partner, diagonal, z_pair = at(1 - c, z, x), at(1 - c, 1 - z, x), at(c, 1 - z, x)
    team = [((c + dc) % 2, (x + dx) % 4) for dc, dx in TEAM_STEPS]
    core_steps = [(dz, dx) for dx in (1, 3, 2, 0) for dz in range(2) if dz or dx]
    core = [((z + dz) % 2, (x + dx) % 4) for dz, dx in core_steps]
    source_of = [core_steps.index((dz, (4 - dx) % 4)) for dz, dx in core_steps]
    greet(
        [at(tc, z, tx) for tc, tx in team]
        + [at(c, 1 - z, (x + dx) % 4) for dx in range(4)]
        + [diagonal, y_up, y_down, z_other]
    )

    def remote(src, dst, sends, recvs, index, target):
        return pltpu.make_async_remote_copy(
            src_ref=src,
            dst_ref=dst,
            send_sem=sends.at[index],
            recv_sem=recvs.at[index],
            device_id=target,
            device_id_type=MESH,
        )

    def to_team(index, layer):
        tc, tx = team[index]
        place_at = first.at[y, zf, x] if layer == 0 else second.at[slot]
        return remote(late.at[tc * 4 + tx], place_at, send_sems, recv_sems, index, at(tc, z, tx))

    def swapped(index):
        src, dst = ((rows, out_rows), (other_rows, out_other))[index]
        return remote(src.at[c], dst, swap_send, swap_recv, index, diagonal)

    def kept(index):
        src, dst = ((rows, out_rows), (other_rows, out_other))[index]
        return pltpu.make_async_copy(src.at[c], dst, local_sems.at[2 + index])

    def common_to(index):
        tz, tx = core[index]
        return remote(
            common, out_common.at[c, slot], common_send, common_recv, index, at(c, tz, tx)
        )

    def shared(index):
        if index == 7:
            source = out_common.at[c, slot]
        else:
            tz, tx = core[index]
            source = out_common.at[c, tz * 4 + tx]
        return remote(source, source, share_send, share_recv, index, partner)

    keep = pltpu.make_async_copy(common, out_common.at[c, slot], local_sems.at[0])
    keep.start()

    @pl.when(c == 0)
    def _():
        for index in range(7):
            to_team(index, 0).start()
        pltpu.make_async_copy(late.at[c * 4 + x], first.at[y, zf, x], local_sems.at[1]).start()

    @pl.when(c == 1)
    def _():
        for index in range(7):
            to_team(index, 1).start()
        pltpu.make_async_copy(late.at[c * 4 + x], second.at[slot], local_sems.at[1]).start()

    for index in range(7):
        common_to(index).start()

    @pl.when(c == z)
    def _():
        kept(0).start()
        kept(1).start()

    @pl.when(c != z)
    def _():
        swapped(0).start()
        swapped(1).start()

    for index, (dc, dx) in enumerate(TEAM_STEPS):

        @pl.when((c + dc) % 2 == 0)
        def _():
            to_team(index, 0).wait_recv()

        @pl.when((c + dc) % 2 == 1)
        def _():
            to_team(index, 1).wait_recv()

    @pl.when(c == 0)
    def _():
        pltpu.make_async_copy(late.at[c * 4 + x], first.at[y, zf, x], local_sems.at[1]).wait()

    @pl.when(c == 1)
    def _():
        pltpu.make_async_copy(late.at[c * 4 + x], second.at[slot], local_sems.at[1]).wait()

    def send(src, dst, index, target):
        copy = remote(src, dst, ring_send, ring_recv, index, target)
        copy.start()
        return copy

    one, two = pl.ds(0, 1), pl.ds(1, 1)
    three, four = pl.ds(2, 1), pl.ds(3, 1)
    left, right = pl.ds(0, 2), pl.ds(2, 2)
    y_copies, y_middle, y_last = ring_spread(
        send,
        0,
        lambda part: first.at[y, zf, part],
        lambda i, part: first.at[i, zf, part],
        y,
        y_up,
        y_down,
        one,
        two,
    )
    z_copies, z_middle, z_last = ring_spread(
        send,
        6,
        lambda part: first.at[y, zf, part],
        lambda i, part: first.at[y, i, part],
        zf,
        z_up,
        z_down,
        three,
        four,
    )
    pair_copy = send(second.at[pl.ds(z * 4, 4)], second.at[pl.ds(z * 4, 4)], 24, z_pair)
    keep.wait()
    shared(7).start()
    for index in range(7):
        common_to(source_of[index]).wait_recv()
        shared(index).start()
    y_middle()
    z_middle()
    y_last()
    more_z, z_middle_too, z_last_too = ring_spread(
        send,
        12,
        lambda part: first.at[part, zf, pl.ds(0, 2)],
        lambda i, part: first.at[part, i, pl.ds(0, 2)],
        zf,
        z_up,
        z_down,
        left,
        right,
    )
    z_last()
    more_y, y_middle_too, y_last_too = ring_spread(
        send,
        18,
        lambda part: first.at[y, part, pl.ds(2, 2)],
        lambda i, part: first.at[i, part, pl.ds(2, 2)],
        y,
        y_up,
        y_down,
        left,
        right,
    )
    z_middle_too()
    y_middle_too()
    pair_copy.wait_recv()
    for index in range(8):
        shared(index).wait_recv()
    z_last_too()
    y_last_too()

    @pl.when(c == z)
    def _():
        kept(0).wait()
        kept(1).wait()

    @pl.when(c != z)
    def _():
        for index in range(2):
            swapped(index).wait_recv()
            swapped(index).wait_send()

    @pl.when(c == 0)
    def _():
        for index in range(7):
            to_team(index, 0).wait_send()

    @pl.when(c == 1)
    def _():
        for index in range(7):
            to_team(index, 1).wait_send()

    for index in range(7):
        common_to(index).wait_send()
    for index in range(8):
        shared(index).wait_send()
    for copy in y_copies + z_copies + more_z + more_y + [pair_copy]:
        copy.wait_send()


def spread_weights(late, common, rows, other_rows):
    dma = pltpu.SemaphoreType.DMA
    return pl.pallas_call(
        weights_kernel,
        out_shape=(
            jax.ShapeDtypeStruct((4, 4, 4, 144, 128), BF),
            jax.ShapeDtypeStruct(late.shape, BF),
            jax.ShapeDtypeStruct((2, 8) + common.shape, BF),
            jax.ShapeDtypeStruct(rows.shape[1:], BF),
            jax.ShapeDtypeStruct(rows.shape[1:], BF),
        ),
        in_specs=[VMEM] * 4,
        out_specs=(VMEM,) * 5,
        scratch_shapes=[
            dma((7,)),
            dma((7,)),
            dma((7,)),
            dma((7,)),
            dma((8,)),
            dma((8,)),
            dma((25,)),
            dma((25,)),
            dma((2,)),
            dma((2,)),
            dma((4,)),
        ],
        compiler_params=pltpu.CompilerParams(
            collective_id=3, has_side_effects=True, vmem_limit_bytes=LIMIT
        ),
    )(late, common, rows, other_rows)


SPLIT_ROWS = 4 * 144
DOWN_ROWS = 320
SHARED_ROWS = 96
ROWS = SPLIT_ROWS + DOWN_ROWS + SHARED_ROWS
OWN_ROWS = DOWN_ROWS + SHARED_ROWS
GOT_ROWS = 8 * 144 + 2 * OWN_ROWS


def widen(block):
    return block.astype(F32)


def ring_reduce(send, base, block, me, up, down, first, second, far, relay, got, result):
    after, before, opposite = (me + 1) % 4, (me + 3) % 4, (me + 2) % 4
    copies = [
        send(block(opposite, first), far[0], base, up),
        send(block(opposite, second), far[1], base + 1, down),
        send(block(after, second), got[0].at[second], base + 2, up),
        send(block(before, first), got[1].at[first], base + 3, down),
    ]

    def middle():
        copies[0].wait_recv()
        relay[0][...] = (widen(block(after, first)[...]) + widen(far[0][...])).astype(BF)
        copies.append(send(relay[0], got[0].at[first], base + 4, up))
        copies[1].wait_recv()
        relay[1][...] = (widen(block(before, second)[...]) + widen(far[1][...])).astype(BF)
        copies.append(send(relay[1], got[1].at[second], base + 5, down))

    def last():
        for copy in copies[2:]:
            copy.wait_recv()
        for part in (first, second):
            value = (
                widen(block(me, part)[...])
                + widen(got[0].at[part][...])
                + widen(got[1].at[part][...])
            )
            result.at[part][...] = value.astype(BF)
        for copy in copies:
            copy.wait_send()

    return middle, last


TOP = ROWS // 2
CUT = TOP // 32 * 16


WIDE = (2, 4, TOP, 128)


def first_scratch():
    dma = pltpu.SemaphoreType.DMA
    return [
        pltpu.VMEM((2, 2, 2, TOP, 128), BF),
        pltpu.VMEM((2, 2, 2, TOP, 128), BF),
        pltpu.VMEM((2, 2, 4, TOP, 128), BF),
        dma((12,)),
        dma((12,)),
    ]


def second_scratch():
    dma = pltpu.SemaphoreType.DMA
    return [
        pltpu.VMEM((2, 2, TOP - CUT, 128), BF),
        pltpu.VMEM((2, 2, TOP - CUT, 128), BF),
        pltpu.VMEM((2, 2, TOP, 128), BF),
        dma((12,)),
        dma((12,)),
    ]


def grid_place():
    c, z, x = place()
    r = lax.axis_index("replica")
    y, zh = r // 2, r % 2
    zf = zh * 2 + z

    def device(ty, tz):
        return {"section": c, "shard": (tz % 2) * 4 + x, "replica": ty * 2 + tz // 2}

    return (
        y,
        zf,
        (
            device((y + 1) % 4, zf),
            device((y + 3) % 4, zf),
            device(y, (zf + 1) % 4),
            device(y, (zf + 3) % 4),
        ),
    )


def starter(sends, recvs):
    def send(src, dst, index, target):
        copy = pltpu.make_async_remote_copy(
            src_ref=src,
            dst_ref=dst,
            send_sem=sends.at[index],
            recv_sem=recvs.at[index],
            device_id=target,
            device_id_type=MESH,
        )
        copy.start()
        return copy

    return send


def rings_first(pieces, wide_sum, far, relay, got, sends, recvs):
    y, zf, (y_up, y_down, z_up, z_down) = grid_place()
    send = starter(sends, recvs)
    low, high = pl.ds(0, 2), pl.ds(2, 2)
    top, bottom = pl.ds(0, TOP), pl.ds(TOP, TOP)

    def buffers(k):
        return (
            [far.at[k, 0], far.at[k, 1]],
            [relay.at[k, 0], relay.at[k, 1]],
            [got.at[k, 0], got.at[k, 1]],
            wide_sum.at[k],
        )

    y_mid, y_last = ring_reduce(
        send,
        0,
        lambda i, part: pieces.at[i, part, top],
        y,
        y_up,
        y_down,
        low,
        high,
        *buffers(0),
    )
    z_mid, z_last = ring_reduce(
        send,
        6,
        lambda i, part: pieces.at[part, i, bottom],
        zf,
        z_up,
        z_down,
        low,
        high,
        *buffers(1),
    )

    def middle():
        y_mid()
        z_mid()

    return middle, y_last, z_last


def rings_second(k, wide_sum, out, far, relay, got, sends, recvs):
    y, zf, (y_up, y_down, z_up, z_down) = grid_place()
    parts = pl.ds(0, CUT), pl.ds(0, TOP - CUT)
    me, up, down = ((zf, z_up, z_down), (y, y_up, y_down))[k]
    return ring_reduce(
        starter(sends, recvs),
        6 * k,
        lambda i, part: wide_sum.at[k, i, part],
        me,
        up,
        down,
        pl.ds(0, CUT),
        pl.ds(CUT, TOP - CUT),
        [far.at[k, 0, parts[0]], far.at[k, 1, parts[1]]],
        [relay.at[k, 0, parts[0]], relay.at[k, 1, parts[1]]],
        [got.at[k, 0], got.at[k, 1]],
        out.at[pl.ds(TOP * k, TOP)],
    )


def home_scratch():
    dma = pltpu.SemaphoreType.DMA
    return [dma((9,)), dma((10,)), dma((2,))]


def spread_scratch():
    dma = pltpu.SemaphoreType.DMA
    return [dma, dma((13,)), dma((13,))]


def remote_copy(src, dst, send_sem, recv_sem, target):
    return pltpu.make_async_remote_copy(
        src_ref=src,
        dst_ref=dst,
        send_sem=send_sem,
        recv_sem=recv_sem,
        device_id=target,
        device_id_type=MESH,
    )


def home_stages(layer, summed, own, home_send, home_recv, local_sems):
    c, z, x = place()
    me = c * 4 + x
    mine = pl.ds(pl.multiple_of(me * 144, 16), 144)
    holds = c == layer
    other = c != layer
    stays = jnp.logical_and(holds, z == layer)
    leaves = jnp.logical_or(other, z != layer)
    copy = remote_copy

    def split_part(tx):
        return summed.at[pl.ds(pl.multiple_of(tx * 144, 16), 144)]

    def to_row(dx, base):
        tx = (x + dx) % 4
        return copy(
            split_part(tx),
            own.at[mine],
            home_send.at[base + dx],
            home_recv.at[base + dx],
            at(layer, z, tx),
        )

    def split_here():
        return pltpu.make_async_copy(split_part(x), own.at[mine], local_sems.at[0])

    own_part = pl.ds(SPLIT_ROWS, OWN_ROWS)
    slot = pl.ds(pl.multiple_of(8 * 144 + z * OWN_ROWS, 16), OWN_ROWS)

    def to_owner(t):
        return copy(
            summed.at[own_part],
            own.at[slot],
            home_send.at[8],
            home_recv.at[8 + t],
            at(layer, c, x),
        )

    def from_row(dx):
        return copy(
            split_part(x),
            own.at[mine],
            home_send.at[4 + dx],
            home_recv.at[4 + dx],
            at(1 - c, z, x),
        )

    def from_owner(t):
        return copy(
            summed.at[own_part],
            own.at[slot],
            home_send.at[8],
            home_recv.at[8 + t],
            at(1 - c, z, x),
        )

    def own_here():
        return pltpu.make_async_copy(summed.at[own_part], own.at[slot], local_sems.at[1])

    def home():
        @pl.when(holds)
        def _():
            split_here().start()
            for dx in (1, 2, 3):
                to_row(dx, 0).start()

        @pl.when(other)
        def _():
            for dx in range(4):
                to_row(dx, 4).start()

        @pl.when(stays)
        def _():
            own_here().start()

        @pl.when(leaves)
        def _():
            to_owner(z).start()

    def arrived():
        @pl.when(holds)
        def _():
            split_here().wait()
            for dx in (1, 2, 3):
                to_row(dx, 0).wait_recv()
            for dx in range(4):
                from_row(dx).wait_recv()

            @pl.when(z == layer)
            def _():
                own_here().wait()
                from_owner(1 - layer).wait_recv()

            @pl.when(z != layer)
            def _():
                from_owner(0).wait_recv()
                from_owner(1).wait_recv()

    def end():
        @pl.when(holds)
        def _():
            for dx in (1, 2, 3):
                to_row(dx, 0).wait_send()

        @pl.when(other)
        def _():
            for dx in range(4):
                to_row(dx, 4).wait_send()

        @pl.when(leaves)
        def _():
            to_owner(z).wait_send()

    return home, arrived, end


def spread_stages(layer, own, out, local_sem, sends, recvs):
    c, z, x = place()
    r = lax.axis_index("replica")
    y, zh = r // 2, r % 2
    y_up, y_down, _, _ = grid_place()[2]
    across = {"section": c, "shard": z * 4 + x, "replica": y * 2 + 1 - zh}
    holds = c == layer
    copy = remote_copy
    here, there = y * 2 + zh, y * 2 + 1 - zh
    front, back = pl.ds(0, GOT_ROWS // 2), pl.ds(GOT_ROWS // 2, GOT_ROWS // 2)

    def step(index, source, place_at, target):
        return copy(source, place_at, sends.at[index], recvs.at[index], target)

    def over():
        return step(0, own, out.at[here], across)

    def kept():
        return pltpu.make_async_copy(own, out.at[here], local_sem)

    def ring(base, source, block):
        def item(i):
            part = (front, back, back, front)[i]
            target = (y_up, y_down, y_up, y_down)[i]
            return step(base + i, source.at[part], out.at[block, part], target)

        return item

    def relays(base, which):
        below, above = ((y + 3) % 4) * 2 + which, ((y + 1) % 4) * 2 + which

        def item(i):
            place_at = (out.at[below, front], out.at[above, back])[i]
            return step(base + 4 + i, place_at, place_at, (y_up, y_down)[i])

        return item

    def first_ring():
        return ring(1, own, here)

    def second_ring():
        return ring(7, out.at[there], there)

    def start():
        @pl.when(holds)
        def _():
            kept().start()
            over().start()
            for i in range(4):
                first_ring()(i).start()

    def pass_first():
        @pl.when(holds)
        def _():
            for i in range(2):
                first_ring()(i).wait_recv()
                relays(1, zh)(i).start()
            over().wait_recv()
            for i in range(4):
                second_ring()(i).start()

    def pass_second():
        @pl.when(holds)
        def _():
            for i in range(2):
                second_ring()(i).wait_recv()
                relays(7, 1 - zh)(i).start()

    def end():
        @pl.when(holds)
        def _():
            rounds = ((first_ring(), relays(1, zh)), (second_ring(), relays(7, 1 - zh)))
            for direct, relayed in rounds:
                for i in (2, 3):
                    direct(i).wait_recv()
                for i in range(2):
                    relayed(i).wait_recv()
            over().wait_send()
            for direct, relayed in rounds:
                for i in range(4):
                    direct(i).wait_send()
                for i in range(2):
                    relayed(i).wait_send()
            kept().wait()

    return start, pass_first, pass_second, end


def across_device():
    c, z, x = place()
    r = lax.axis_index("replica")
    return {"section": c, "shard": z * 4 + x, "replica": (r // 2) * 2 + 1 - r % 2}


def home_beside(layer, wide_sum, summed, own, second_refs, home_refs):
    c, z, x = place()
    friends = [at(c, z, (x + 2) % 4)] + [at(1 - c, z, (x + dx) % 4) for dx in (1, 2, 3)]
    friends += [at(1 - c, 1 - z, x)] + list(grid_place()[2])
    home, arrived, end = home_stages(layer, summed, own, *home_refs)
    rings = []

    def begin():
        for k in range(2):
            rings.append(rings_second(k, wide_sum, summed, *second_refs))

    def first():
        for ring in rings:
            ring[0]()

    def second():
        for ring in rings:
            ring[1]()
        home()

    def finish():
        arrived()
        end()

    return friends, begin, first, second, finish


def spread_beside(layer, own, out, refs):
    start, pass_first, pass_second, end = spread_stages(layer, own, out, *refs)
    friends = list(grid_place()[2][:2]) + [across_device()]
    return friends, start, pass_first, pass_second, end


def reduce_kernel(pieces, out, wide_sum, summed, own, *refs):
    c, z, x = place()
    greet(list(grid_place()[2]) + [across_device(), at(1 - c, 1 - z, x)] + team_mates())
    first_refs, second_refs, home_refs, spread_refs = refs[:5], refs[5:10], refs[10:13], refs[13:]
    middle, y_last, z_last = rings_first(pieces, wide_sum, *first_refs)
    middle()
    y_last()
    rings = [rings_second(0, wide_sum, summed, *second_refs)]
    z_last()
    rings.append(rings_second(1, wide_sum, summed, *second_refs))
    for ring in rings:
        ring[0]()
    for ring in rings:
        ring[1]()
    for stage in home_stages(0, summed, own, *home_refs):
        stage()
    for stage in spread_stages(0, own, out, *spread_refs):
        stage()


def reduce_grads(pieces):
    return pl.pallas_call(
        reduce_kernel,
        out_shape=jax.ShapeDtypeStruct((8, GOT_ROWS, 128), BF),
        in_specs=[VMEM],
        out_specs=VMEM,
        scratch_shapes=[
            pltpu.VMEM(WIDE, BF),
            pltpu.VMEM((ROWS, 128), BF),
            pltpu.VMEM((GOT_ROWS, 128), BF),
        ]
        + first_scratch()
        + second_scratch()
        + home_scratch()
        + spread_scratch(),
        compiler_params=pltpu.CompilerParams(
            collective_id=4, has_side_effects=True, vmem_limit_bytes=LIMIT
        ),
    )(pieces)


def shared_kernel(*refs):
    attended, middle_low, normed_all, qkv_grad, normed, last_grad, vectors, rows = refs[:8]
    second_all, up_grad, activated, low_all, pieces, *refs = refs[8:]
    out_rows, out, wide, tall, products, last_keys, last_queries, parts, *refs = refs
    home_send, home_recv, home_local, *scatter_refs = refs
    c, z, x = place()
    products[...] = dot_tn(attended[...], middle_low[...])
    last_keys[...] = dot_tn(normed_all[...], qkv_grad[:, 384:512])
    last_queries[...] = dot_tn(normed[...], last_grad[...])
    for j in range(8):
        block = pl.ds(136 * j, 136)

        def stack(value, lanes):
            tail = vectors[j, :, lanes]
            return jnp.concatenate([value, tail], axis=0).astype(BF)

        if j < 7:
            product = products[block, :]
        else:
            product = jnp.concatenate(
                [products[952:1024, :], products[1088:1152, :]], axis=0
            )
        parts[j, :, 0:128] = stack(last_keys[block, :], pl.ds(0, 128))
        parts[j, :, 128:1152] = stack(product[:, 0:1024], pl.ds(128, 1024))
        parts[j, :, 1152:1280] = stack(
            product[:, 1024:1152] + last_queries[block, :], pl.ds(1152, 128)
        )

    def same_layer():
        return pltpu.make_async_remote_copy(
            src_ref=rows.at[c],
            dst_ref=out_rows.at[z],
            send_sem=home_send.at[0],
            recv_sem=home_recv.at[0],
            device_id=at(c, 1 - z, x),
            device_id_type=MESH,
        )

    def same_here():
        return pltpu.make_async_copy(rows.at[c], out_rows.at[z], home_local)

    def other_layer(t):
        return pltpu.make_async_remote_copy(
            src_ref=rows.at[1 - c],
            dst_ref=out_rows.at[z],
            send_sem=home_send.at[1],
            recv_sem=home_recv.at[1 + t],
            device_id=at(1 - c, c, x),
            device_id_type=MESH,
        )

    def begin():
        @pl.when(z == c)
        def _():
            same_here().start()

        @pl.when(z != c)
        def _():
            same_layer().start()

        other_layer(z).start()

    def put(base, piece_rows, start, value):
        for piece, row, at_row, count in segments(start, value.shape[0], piece_rows):
            pieces[piece // 4, piece % 4, base + row : base + row + count, :] = value[
                at_row : at_row + count
            ].astype(BF)

    def columns():
        wide[:, 896:1024] = jnp.zeros((D, 128), F32)
        wide[:, 0:384] = dot_tn(normed_all[...], qkv_grad[:, 0:384])
        wide[:, 384:928] = dot_tn(second_all[...], up_grad[...])
        blank = jnp.zeros((8, 128), F32)
        for chunk in range(8):
            for j in range(8):
                block = wide[136 * j : 136 * j + 136, 128 * chunk : 128 * chunk + 128]
                place_at = pl.ds((j % 4) * 144, 144)
                pieces[chunk // 2, (chunk % 2) * 2 + j // 4, place_at, :] = jnp.concatenate(
                    [block, blank], axis=0
                ).astype(BF)

    def downs():
        tall[:, 1024:1152] = jnp.zeros((544, 128), F32)
        tall[:, 0:D] = dot_tn(activated[...], low_all[...])
        for k in range(9):
            put(SPLIT_ROWS, DOWN_ROWS, 544 * k, tall[:, 128 * k : 128 * k + 128])
        put(SPLIT_ROWS, DOWN_ROWS, 9 * 544, jnp.zeros((16 * DOWN_ROWS - 9 * 544, 128), F32))

    def end():
        base = SPLIT_ROWS + DOWN_ROWS
        for k in range(10):
            put(base, SHARED_ROWS, 144 * k, out[:, 128 * k : 128 * k + 128])
        put(base, SHARED_ROWS, 1440, jnp.zeros((16 * SHARED_ROWS - 1440, 128), F32))

        @pl.when(z == c)
        def _():
            same_here().wait()
            same_layer().wait_recv()

        @pl.when(z != c)
        def _():
            other_layer(0).wait_recv()
            other_layer(1).wait_recv()
            same_layer().wait_send()

        other_layer(z).wait_send()

    friends = [at(c, 1 - z, x), at(1 - c, 1 - z, x)]
    def mine_part(where, part):
        return parts[c * 4 + where, part, :].astype(F32)

    scatter_core(
        64,
        lambda where: parts.at[(1 - c) * 4 + where],
        mine_part,
        lambda where: None,
        (friends, begin, downs, columns, end),
        out,
        *scatter_refs,
    )


def shared_scatter(*operands):
    dma = pltpu.SemaphoreType.DMA
    return pl.pallas_call(
        shared_kernel,
        out_shape=(
            jax.ShapeDtypeStruct((4, 4, ROWS, 128), BF),
            jax.ShapeDtypeStruct((2, 128, D), BF),
        ),
        in_specs=[VMEM] * 12,
        out_specs=(VMEM, VMEM),
        scratch_shapes=[
            pltpu.VMEM((144, 1280), F32),
            pltpu.VMEM((D, 1024), F32),
            pltpu.VMEM((544, 1152), F32),
            pltpu.VMEM((1152, 1152), F32),
            pltpu.VMEM((D, 128), F32),
            pltpu.VMEM((D, 128), F32),
            pltpu.VMEM((8, 144, 1280), BF),
            dma((2,)),
            dma((3,)),
            dma,
        ]
        + scatter_scratch(144, 1280, 64),
        compiler_params=pltpu.CompilerParams(
            collective_id=6, has_side_effects=True, vmem_limit_bytes=LIMIT
        ),
    )(*operands)


def segments(start, size, piece_rows):
    done = 0
    while done < size:
        piece, row = divmod(start + done, piece_rows)
        count = min(piece_rows - row, size - done)
        yield piece, row, done, count
        done += count


def assemble_kernel(
    first_got, second_got, qkv, out_w, up, down, vectors, shared, got, got_sem
):
    c = lax.axis_index("section")

    @pl.when(c == 0)
    def _():
        pltpu.make_async_copy(first_got, got, got_sem).start()

    @pl.when(c == 1)
    def _():
        pltpu.make_async_copy(second_got, got, got_sem).start()

    @pl.when(c == 0)
    def _():
        pltpu.make_async_copy(first_got, got, got_sem).wait()

    @pl.when(c == 1)
    def _():
        pltpu.make_async_copy(second_got, got, got_sem).wait()

    for q in range(8):
        for chunk in range(8):
            block = got[chunk, 144 * q : 144 * q + 144, :].astype(F32)[:136]
            if chunk < 3:
                start = chunk * D + 128 * q
                qkv[:, start : start + 128] = block
            elif chunk < 7:
                start = 544 * q + 128 * (chunk - 3)
                up[:, start : start + 128] = block
            else:
                up[:, 544 * q + 512 : 544 * q + 544] = block[:, :32]
    for k in range(9):
        width = 128 if k < 8 else 64
        for piece, row, at_row, count in segments(544 * k, 544, DOWN_ROWS):
            start = 8 * 144 + (piece % 2) * OWN_ROWS + row
            block = got[piece // 2, start : start + count, :].astype(F32)
            down[at_row : at_row + count, 128 * k : 128 * k + width] = block[:, :width]
    for k in range(10):
        for piece, row, at_row, count in segments(144 * k, 144, SHARED_ROWS):
            start = 8 * 144 + (piece % 2) * OWN_ROWS + DOWN_ROWS + row
            block = got[piece // 2, start : start + count, :].astype(F32)
            shared[k, at_row : at_row + count, :] = block
        vectors[:, 128 * k : 128 * k + 128] = shared[k, 136:144, :]
        if 1 <= k < 9:
            out_w[:, 128 * (k - 1) : 128 * k] = shared[k, 0:136, :]
    out_w[:, 1024:D] = shared[9, 0:136, 0:64]
    qkv[:, 1024:D] = shared[9, 0:136, 64:128]
    qkv[:, D + 1024 : 2 * D] = shared[0, 0:136, 0:64]
    qkv[:, 2 * D + 1024 : 3 * D] = shared[0, 0:136, 64:128]


def assemble(first_got, second_got):
    shapes = ((136, 3 * D), (136, D), (136, FF), (544, D), (8, 1280))
    return pl.pallas_call(
        assemble_kernel,
        out_shape=tuple(jax.ShapeDtypeStruct(shape, F32) for shape in shapes),
        in_specs=[pl.BlockSpec(memory_space=pl.ANY)] * 2,
        out_specs=(VMEM,) * 5,
        scratch_shapes=[
            pltpu.VMEM((10, 144, 128), F32),
            pltpu.VMEM((8, GOT_ROWS, 128), BF),
            pltpu.SemaphoreType.DMA,
        ],
        compiler_params=pltpu.CompilerParams(vmem_limit_bytes=LIMIT),
    )(first_got, second_got)


def dot_nt(left, right):
    return lax.dot_general(left, right, (((1,), (1,)), ((), ())), preferred_element_type=F32)


def dot_tn(left, right):
    return lax.dot_general(left, right, (((0,), (0,)), ((), ())), preferred_element_type=F32)


def dot(left, right):
    return jnp.dot(left, right, preferred_element_type=F32)


def lane_half(block, which):
    lane = lax.broadcasted_iota(jnp.int32, block.shape, 1)
    keep = lane < 64 if which == 0 else lane >= 64
    return jnp.where(keep, block, jnp.zeros_like(block))


def softmax_rows(scores, start):
    row = lax.broadcasted_iota(jnp.int32, scores.shape, 0) + start
    key = lax.broadcasted_iota(jnp.int32, scores.shape, 1)
    masked = jnp.where(key <= row, scores, NEG_FILL)
    shifted = jnp.exp(masked - jnp.max(masked, axis=1, keepdims=True))
    return shifted * (1.0 / jnp.sum(shifted, axis=1, keepdims=True))


STEP = 256


def team_mates():
    c, z, x = place()
    return [at((c + dc) % 2, z, (x + dx) % 4) for dc, dx in TEAM_STEPS]


def lanes_of(q):
    return pl.ds(pl.multiple_of(q * 128, 128), 128)


def attend_kernel(projected, last_query, out, attended, send_sems, recv_sems, local_sem):
    c, z, x = place()
    me = c * 4 + x
    mates = team_mates()
    arrive(mates)

    def copy_to(q):
        return pltpu.make_async_remote_copy(
            src_ref=attended.at[q],
            dst_ref=out.at[:, lanes_of(me)],
            send_sem=send_sems.at[q],
            recv_sem=recv_sems.at[me],
            device_id=at(q // 4, z, q % 4),
            device_id_type=MESH,
        )

    def copy_from(q):
        return pltpu.make_async_remote_copy(
            src_ref=attended.at[q],
            dst_ref=out.at[:, lanes_of(q)],
            send_sem=send_sems.at[q],
            recv_sem=recv_sems.at[q],
            device_id=at(q // 4, z, q % 4),
            device_id_type=MESH,
        )

    def keep(q):
        return pltpu.make_async_copy(attended.at[q], out.at[:, lanes_of(q)], local_sem)

    both = projected[:, 384:512]
    soft = softmax_rows(dot_nt(last_query[...] * 0.125, both), me * 128).astype(BF)
    out[:, 1024:1152] = dot(soft, lane_half(both, 1)).astype(BF)
    for start in range(0, 1024, STEP):
        size = start + STEP
        query = projected[start:size, 0:128] * 0.125
        total = jnp.zeros((STEP, 128), F32)
        for head in range(2):
            keys = lane_half(projected[0:size, 128:256], head)
            values = lane_half(projected[0:size, 256:384], head)
            soft = softmax_rows(dot_nt(query, keys), start).astype(BF)
            total = total + dot(soft, values)
        if start == 0:
            meet(mates)
        for q in range(start // 128, size // 128):
            begin = q * 128 - start
            attended[q] = total[begin : begin + 128].astype(BF)

            @pl.when(me == q)
            def _():
                keep(q).start()

            @pl.when(me != q)
            def _():
                copy_to(q).start()

    for q in range(8):

        @pl.when(me == q)
        def _():
            keep(q).wait()

        @pl.when(me != q)
        def _():
            copy_from(q).wait_recv()
            copy_to(q).wait_send()


def attend(projected, last_query):
    return pl.pallas_call(
        attend_kernel,
        out_shape=jax.ShapeDtypeStruct((128, 1152), BF),
        in_specs=[VMEM, VMEM],
        out_specs=VMEM,
        scratch_shapes=[
            pltpu.VMEM((8, 128, 128), BF),
            pltpu.SemaphoreType.DMA((8,)),
            pltpu.SemaphoreType.DMA((8,)),
            pltpu.SemaphoreType.DMA,
        ],
        compiler_params=pltpu.CompilerParams(
            collective_id=1, has_side_effects=True, vmem_limit_bytes=LIMIT
        ),
    )(projected, last_query)


def attend_back_kernel(
    projected,
    last_query,
    rows,
    out,
    out_last,
    grad,
    key_total,
    value_total,
    send_sems,
    recv_sems,
    local_sem,
):
    c, z, x = place()
    me = c * 4 + x
    mates = team_mates()
    arrive(mates)
    local = pltpu.make_async_copy(rows.at[:, lanes_of(me)], grad.at[row_block(me)], local_sem)
    local.start()
    meet(mates)
    send = sender(send_sems, recv_sems)
    copies = []
    for index, (dc, dx) in enumerate(TEAM_STEPS):
        tc, tx = (c + dc) % 2, (x + dx) % 4
        copies.append(
            send(rows.at[:, lanes_of(tc * 4 + tx)], grad.at[row_block(me)], index, at(tc, z, tx))
        )
    key_total[...] = jnp.zeros_like(key_total)
    value_total[...] = jnp.zeros_like(value_total)
    both = projected[:, 384:512]
    query = last_query[...] * 0.125
    last_grad = rows[:, 1024:1152]
    soft = softmax_rows(dot_nt(query, both), me * 128)
    grad_soft = dot_nt(last_grad, both)
    inner = jnp.sum(soft * grad_soft, axis=1, keepdims=True)
    grad_scores = (soft * (grad_soft - inner)).astype(BF)
    out_last[...] = (dot(grad_scores, lane_half(both, 0)) * 0.125).astype(BF)
    out[:, 384:512] = (dot_tn(grad_scores, query) + dot_tn(soft.astype(BF), last_grad)).astype(BF)
    local.wait()
    for copy in copies:
        copy.wait_recv()
    for start in range(0, 1024, STEP):
        size = start + STEP
        query = projected[start:size, 0:128] * 0.125
        grad_rows = grad[start:size, :]
        total = jnp.zeros((STEP, 128), F32)
        for head in range(2):
            keys = lane_half(projected[0:size, 128:256], head)
            values = lane_half(projected[0:size, 256:384], head)
            soft = softmax_rows(dot_nt(query, keys), start)
            grad_soft = dot_nt(grad_rows, values)
            inner = jnp.sum(soft * grad_soft, axis=1, keepdims=True)
            grad_scores = (soft * (grad_soft - inner)).astype(BF)
            total = total + dot(grad_scores, keys)
            key_total[0:size, :] += dot_tn(grad_scores, lane_half(query, head))
            value_total[0:size, :] += dot_tn(soft.astype(BF), lane_half(grad_rows, head))
        out[start:size, 0:128] = (total * 0.125).astype(BF)
    out[:, 128:256] = key_total[...].astype(BF)
    out[:, 256:384] = value_total[...].astype(BF)
    for copy in copies:
        copy.wait_send()


def attend_back(projected, last_query, rows):
    return pl.pallas_call(
        attend_back_kernel,
        out_shape=(
            jax.ShapeDtypeStruct((1024, 512), BF),
            jax.ShapeDtypeStruct((128, 128), BF),
        ),
        in_specs=[VMEM] * 3,
        out_specs=(VMEM, VMEM),
        scratch_shapes=[
            pltpu.VMEM((1024, 128), BF),
            pltpu.VMEM((1024, 128), F32),
            pltpu.VMEM((1024, 128), F32),
            pltpu.SemaphoreType.DMA((7,)),
            pltpu.SemaphoreType.DMA((7,)),
            pltpu.SemaphoreType.DMA,
        ],
        compiler_params=pltpu.CompilerParams(
            collective_id=2, has_side_effects=True, vmem_limit_bytes=LIMIT
        ),
    )(projected, last_query, rows)


def norm_forward(hidden, gain, offset):
    center = hidden - jnp.mean(hidden, axis=-1, keepdims=True)
    inverse = lax.rsqrt(jnp.mean(center * center, axis=-1, keepdims=True) + EPSILON)
    unit = center * inverse
    return unit * gain + offset, unit, inverse


def norm_backward(grad_rows, unit, inverse, gain):
    grad_unit = grad_rows * gain
    grad_in = inverse * (
        grad_unit
        - jnp.mean(grad_unit, axis=-1, keepdims=True)
        - unit * jnp.mean(grad_unit * unit, axis=-1, keepdims=True)
    )
    return grad_in, jnp.sum(grad_rows * unit, axis=0), jnp.sum(grad_rows, axis=0)


def gelu_pair(values):
    tangent = jnp.tanh(GELU_C * (values + 0.044715 * values * values * values))
    output = 0.5 * values * (1.0 + tangent)
    slope = 0.5 * (1.0 + tangent) + 0.5 * values * (1.0 - tangent * tangent) * GELU_C * (
        1.0 + 3.0 * 0.044715 * values * values
    )
    return output, slope


def layer_forward(hidden, w):
    normed, unit_one, inverse_one = norm_forward(hidden, w["gain_one"], w["bias_one"])
    normed = normed.astype(BF)
    normed_all, projected, qkv_weight = team_gather(
        gather_qkv_kernel,
        0,
        normed,
        w["blocks"],
        (w["common"], w["qkv_bias"].reshape(1, 512)),
        (jax.ShapeDtypeStruct((1024, 512), BF), jax.ShapeDtypeStruct((D, 512), BF)),
        (pltpu.VMEM((D, 512), F32),),
    )
    normed_all = normed_all.reshape(1024, D)
    last_query = (dot(normed, w["last_query"]) + w["last_bias"]).astype(BF)
    attended = attend(projected, last_query)
    packed = jnp.concatenate([attended[:, :1024], attended[:, 1088:]], axis=1)
    middle = hidden + dot(packed, w["out"]) + w["out_bias"]
    second, unit_two, inverse_two = norm_forward(middle, w["gain_two"], w["bias_two"])
    second_all, upper, activated, up_weight = team_gather(
        gather_up_kernel,
        7,
        second.astype(BF),
        w["blocks"],
        (w["up_bias"].reshape(1, 544),),
        (
            jax.ShapeDtypeStruct((1024, 544), F32),
            jax.ShapeDtypeStruct((1024, 544), BF),
            jax.ShapeDtypeStruct((D, 544), BF),
        ),
        (pltpu.VMEM((D, 640), F32),),
    )
    second_all = second_all.reshape(1024, D)
    output = middle + product_scatter(dot, 5, activated, w["down"]) + w["down_bias"]
    saved = dict(
        normed=normed,
        normed_all=normed_all,
        unit_one=unit_one,
        inverse_one=inverse_one,
        projected=projected,
        last_query=last_query,
        attended=attended,
        unit_two=unit_two,
        inverse_two=inverse_two,
        second_all=second_all,
        upper=upper,
        activated=activated,
        qkv_weight=qkv_weight,
        up_weight=up_weight,
    )
    return output, saved


def layer_backward(grad_out, grad_low_all, w, kept, q, pieces):
    grad_low = grad_out.astype(BF)
    if grad_low_all is None:
        grad_low_all, up_grad, wide_sum = team_gather(
            gather_back_kernel,
            8,
            grad_low,
            w["down"],
            (kept["upper"], pieces),
            (jax.ShapeDtypeStruct((1024, 544), BF), jax.ShapeDtypeStruct(WIDE, BF)),
            first_scratch(),
        )
        grad_low_all = grad_low_all.reshape(1024, D)
        grad_second, own = product_scatter(dot_nt, 11, up_grad, kept["up_weight"], wide_sum)
    else:
        slope = gelu_pair(kept["upper"])[1]
        up_grad = (dot_nt(grad_low_all, w["down"]) * slope).astype(BF)
        grad_second, own = product_scatter(dot_nt, 9, up_grad, kept["up_weight"]), None
    grad_in, gain_two, bias_two = norm_backward(
        grad_second, kept["unit_two"], kept["inverse_two"], w["gain_two"]
    )
    grad_middle = grad_out + grad_in
    middle_low = grad_middle.astype(BF)
    attended_grad = dot_nt(middle_low, w["out"]).astype(BF)
    attended_grad = jnp.concatenate(
        [attended_grad[:, :1024], jnp.zeros((128, 64), BF), attended_grad[:, 1024:]], axis=1
    )
    qkv_grad, last_grad = attend_back(kept["projected"], kept["last_query"], attended_grad)
    if own is None:
        grad_normed, got = product_scatter(dot_nt, 10, qkv_grad, kept["qkv_weight"]), None
    else:
        grad_normed, got = product_scatter(dot_nt, 12, qkv_grad, kept["qkv_weight"], own)
    grad_normed = grad_normed + dot_nt(last_grad, w["last_query"])
    grad_in, gain_one, bias_one = norm_backward(
        grad_normed, kept["unit_one"], kept["inverse_one"], w["gain_one"]
    )
    grad_input = grad_middle + grad_in

    qkv_sums = jnp.sum(qkv_grad, axis=0, dtype=F32)
    last_sums = jnp.sum(last_grad, axis=0, dtype=F32)
    zeros = jnp.zeros((1024,), F32)
    qv = jnp.concatenate(
        [
            lax.dynamic_update_slice(zeros, qkv_sums[:128], (q * 128,)),
            last_sums[:64],
            lax.dynamic_update_slice(zeros, qkv_sums[256:384], (q * 128,)),
            qkv_sums[448:512],
        ]
    )
    up_sums = lax.dynamic_update_slice(
        jnp.zeros((FF,), F32), jnp.sum(up_grad, axis=0, dtype=F32), (q * 544,)
    )
    vectors = jnp.concatenate(
        [
            qv.reshape(8, 272),
            jnp.sum(middle_low, axis=0, dtype=F32).reshape(8, 136),
            gain_one.reshape(8, 136),
            bias_one.reshape(8, 136),
            gain_two.reshape(8, 136),
            bias_two.reshape(8, 136),
            up_sums.reshape(8, 544),
            jnp.sum(grad_low, axis=0, dtype=F32).reshape(8, 136),
        ],
        axis=1,
    )
    vectors = jnp.pad(vectors, ((0, 0), (0, 8 * 1280 - 1632))).reshape(8, 8, 1280)
    swapped_grad = jnp.concatenate([jnp.zeros((128, 64), BF), last_grad[:, :64]], axis=1)
    operands = (
        kept["attended"],
        jnp.pad(middle_low, ((0, 0), (0, 64))),
        kept["normed_all"],
        qkv_grad,
        kept["normed"],
        swapped_grad,
        vectors,
    )
    split = (
        kept["second_all"],
        up_grad,
        kept["activated"],
        grad_low_all,
    )
    return grad_input, operands, split, got


BOTH = ("section", "shard")


def pairs(route):
    out = []
    for c in range(2):
        for z in range(2):
            for x in range(4):
                tc, tz = route(c, z)
                out.append((c * 8 + z * 4 + x, tc * 8 + tz * 4 + x))
    return out


def local(
    inputs,
    cotangent,
    w_qkv,
    qv_bias,
    w_out,
    out_bias,
    gain_one,
    bias_one,
    gain_two,
    bias_two,
    w_up,
    up_bias,
    w_down,
    down_bias,
):
    c, z, x = place()
    q = c * 4 + x
    swap = [pair for pair in pairs(lambda a, b: (b, a)) if pair[0] != pair[1]]
    cross_back = pairs(lambda a, b: (b, 1 - a))

    def swapped(array):
        return jnp.where(c == z, array, lax.ppermute(array, BOTH, swap))

    def by_z(own, other):
        return jnp.where(z == 0, own, other), jnp.where(z == 0, other, own)

    small = jnp.concatenate(
        [
            qv_bias[0],
            up_bias[0],
            out_bias[0],
            gain_one[0],
            bias_one[0],
            gain_two[0],
            bias_two[0],
            down_bias[0],
        ]
    )
    own_qkv = w_qkv[0]
    last_cols = [own_qkv[:, part * D + 1024 : (part + 1) * D] for part in range(3)]
    common = jnp.concatenate(
        [
            jnp.concatenate(
                [last_cols[1], last_cols[2], last_cols[0], jnp.zeros((136, 64), BF)], axis=1
            ),
            jnp.pad(small, (0, 2048 - 1632)).reshape(8, 256),
        ]
    )
    blocks = jnp.concatenate(
        [own_qkv[:, part * D : part * D + 1024].reshape(136, 8, 128) for part in range(3)]
        + [w_up[0].reshape(136, 8, 544)],
        axis=2,
    ).transpose(1, 0, 2)
    blocks = jnp.pad(blocks, ((0, 0), (0, 8), (0, 0)))
    replica = lax.axis_index("replica")
    late = lax.dynamic_slice(
        jnp.pad(blocks, ((0, 0), (0, 0), (0, 96))), (0, 0, replica * 128), (8, 144, 128)
    )
    first_blocks, late, all_common, hidden, top_grad = spread_weights(
        late, common, inputs[:, 0], cotangent[:, 0]
    )
    own_out = lax.all_gather(w_out[0], "shard", axis=0, tiled=True)
    teams = [[a * 8 + b * 4 + d for a in range(2) for d in range(4)] for b in range(2)]
    top_grad_all = lax.all_gather(top_grad, BOTH, axis_index_groups=teams, axis=0, tiled=True)
    second_blocks = lax.all_gather(late, "replica", axis=0)
    partner_out = lax.ppermute(own_out, "section", [(0, 1), (1, 0)])
    all_out = (
        jnp.where(c == 0, own_out, partner_out),
        jnp.where(c == 0, partner_out, own_out),
    )
    all_blocks = (first_blocks.reshape(8, 8, 144, 128), second_blocks)
    down_own = swapped(w_down[0])
    down_other = lax.ppermute(w_down[0], BOTH, cross_back)
    all_down = by_z(down_own, down_other)

    def layer_weights(layer):
        vec = all_common[layer, :, 136:].reshape(8, 2048)[:, :1632].astype(F32)

        def piece(start, size):
            return vec[:, start : start + size].reshape(-1)

        qv = piece(0, 272)
        six = vec[:, 816:].reshape(8, 6, 136).transpose(1, 0, 2).reshape(6, D)
        six = lax.optimization_barrier(six)
        none = jnp.zeros((128,), F32)
        qkv_bias = jnp.concatenate(
            [
                lax.dynamic_slice(qv, (q * 128,), (128,)),
                none,
                lax.dynamic_slice(qv, (D + q * 128,), (128,)),
                none[:64],
                qv[2 * D - 64 :],
            ]
        )
        return dict(
            blocks=all_blocks[layer],
            common=all_common[layer],
            last_query=all_common[layer, :, :136, 128:].reshape(D, 128),
            qkv_bias=qkv_bias,
            last_bias=jnp.concatenate([qv[1024:D], none[:64]]),
            out=all_out[layer],
            out_bias=six[0:1],
            gain_one=six[1:2],
            bias_one=six[2:3],
            gain_two=six[3:4],
            bias_two=six[4:5],
            up_bias=lax.dynamic_slice(piece(272, 544), (q * 544,), (544,)),
            down=all_down[layer],
            down_bias=six[5:6],
        )

    weights = [layer_weights(0), layer_weights(1)]
    hidden = hidden.astype(F32)
    top_grad = top_grad.astype(F32)
    out_first, kept_first = layer_forward(hidden, weights[0])
    out_second, kept_second = layer_forward(out_first.astype(BF).astype(F32), weights[1])
    grad_second, operands, split, _ = layer_backward(
        top_grad, top_grad_all, weights[1], kept_second, q, None
    )
    rows = jnp.stack([out_first.astype(BF), out_second.astype(BF)])
    pieces, section_out = shared_scatter(*operands, rows, *split)
    grad_first, operands, split, second_got = layer_backward(
        grad_second.astype(BF).astype(F32), None, weights[0], kept_first, q, pieces
    )
    rows = jnp.stack([grad_first.astype(BF), grad_second.astype(BF)])
    pieces, input_grad = shared_scatter(*operands, rows, *split)
    first_got = reduce_grads(pieces)
    grad_qkv, grad_out_w, grad_up, grad_down, vectors = assemble(first_got, second_got)
    section_out = section_out.astype(F32)[None, :, None]
    input_grad = input_grad.astype(F32)[None, :, None]
    vec = vectors.reshape(-1)
    grads = (
        grad_qkv,
        vec[:272],
        grad_out_w,
        vec[272:408],
        vec[408:544],
        vec[544:680],
        vec[680:816],
        vec[816:952],
        grad_up,
        vec[952:1496],
        grad_down,
        vec[1496:1632],
    )
    return (section_out, input_grad) + tuple(grad[None] for grad in grads)


def solution(mesh):
    return jax.shard_map(
        local,
        mesh=mesh,
        in_specs=(
            P(None, "replica", "shard", None),
            P(None, "replica", "shard", None),
            P("section", "shard", None),
            P("section", "shard"),
            P("section", "shard", None),
            P("section", "shard"),
            P("section", "shard"),
            P("section", "shard"),
            P("section", "shard"),
            P("section", "shard"),
            P("section", "shard", None),
            P("section", "shard"),
            P("section", "shard", None),
            P("section", "shard"),
        ),
        out_specs=(
            P("section", None, "replica", "shard", None),
            P("section", None, "replica", "shard", None),
            P("section", "shard", None),
            P("section", "shard"),
            P("section", "shard", None),
            P("section", "shard"),
            P("section", "shard"),
            P("section", "shard"),
            P("section", "shard"),
            P("section", "shard"),
            P("section", "shard", None),
            P("section", "shard"),
            P("section", "shard", None),
            P("section", "shard"),
        ),
        check_vma=False,
    )
```
